256 devices in a mesh: lat: 8 (over y, x_hi), lon: 32 (over x_lo, z, core).
Axes of the slice: x: 4 (x_hi: 2, x_lo: 2; x = x_hi * 2 + x_lo), y: 4, z: 8, core: 2. Of those that a mesh axis runs over, the one named last changes fastest.
Arguments:
- fields: bfloat16 [4, 48, 768, 512], P(None, 'lat', 'lon'), may hold values from -6 to 6
- cotangent: bfloat16 [4, 48, 768, 512], P(None, 'lat', 'lon'), may hold values from -6 to 6
- layer_norm_gain: float32 [512], replicated, may hold values from 0.25 to 1.75
- qkv_weight: bfloat16 [512, 1536], replicated, as said below
- out_weight: bfloat16 [512, 512], replicated, may hold values from -0.25 to 0.25
Outputs:
- output: bfloat16 [4, 48, 768, 512], P(None, 'lat', 'lon')
- fields_gradient: bfloat16 [4, 48, 768, 512], P(None, 'lat', 'lon')
- grad_qkv: float32 [512, 1536], replicated
- grad_out: float32 [512, 512], replicated
- norm_gain_gradient: float32 [512], replicated
The draws below stay inside these ranges and needn't reach their ends.
Inputs may be any that keep to these rules, and one draw needn't show every extreme that they name: `qkv_weight`: entries have mean zero and deviation about 512 ** -0.5 or larger.
All inputs are finite; a program needn't handle non-finite values.
Results may differ from the reference program's by a relative error of at most 0.014.
The reference program's roundings to bfloat16 on the way count: a program that leaves them out, or rounds other values in their place, can miss the bound.
Values may be sent and summed in bfloat16 or wider, within the bound.
No kernel may reach another device: no remote copies, remote signals or barrier semaphores. Data moves between devices by JAX's collectives and lax.ppermute only.
A program may use at most 128 MiB of HBM per device.

```python
import math
import jax
import jax.numpy as jnp
from jax import lax

D = 512
HEADS = 8
LEV = 4
WIN_LEV = 2
WIN_LAT = 6
WIN_LON = 12
NLAT = 48
NLON = 768


def draw_qkv_weight(key, part):
    key = jax.random.fold_in(key, 11)
    values = jax.random.normal(key, (D, 3 * D), jnp.float32) / math.sqrt(D)
    return values.astype(jnp.bfloat16)


def block_scale(own_key, shape, cuts, least, largest):
    def one(dim, parts):
        draws = jax.random.uniform(jax.random.fold_in(jax.random.fold_in(own_key, 6), dim), (parts,), jnp.float32, least / len(cuts), largest / len(cuts))
        return jnp.repeat(jnp.exp(draws), shape[dim] // parts).reshape((-1,) + (1,) * (len(shape) - dim - 1))

    gain = one(*cuts[0])
    for cut in cuts[1:]:
        gain = gain * one(*cut)
    return gain


def centred(own_key, extent, spread, most, cuts=(), held_as=jnp.bfloat16):
    drawn = jax.random.normal(own_key, extent, jnp.float32) * spread
    if len(cuts) > 0:
        drawn = block_scale(own_key, extent, cuts, -0.22, 0.18) * drawn
    return jnp.clip(drawn, min=-most, max=most).astype(held_as)


def setup_inputs(seed: int = 0) -> dict:
    key_list = jax.random.split(jax.random.key(seed), 6)
    return {
        "fields": centred(key_list[0], (LEV, NLAT, NLON, D), 1.0, 6.0, ((1, 8), (2, 32))),
        "cotangent": centred(key_list[1], (LEV, NLAT, NLON, D), 1.0, 6.0, ((1, 8), (2, 32))),
        "layer_norm_gain": jnp.clip(1.0 + 0.15 * jax.random.normal(key_list[2], (D,), jnp.float32), 0.25, 1.75),
        "qkv_weight": draw_qkv_weight(jax.random.fold_in(key_list[5], 71), 0),
        "out_weight": centred(key_list[4], (D, D), D ** -0.5, 0.25),
    }


def to_windows(field):
    levels, lat_rows, lon_cols, channels = field.shape
    blocked = field.reshape(levels // WIN_LEV, WIN_LEV, lat_rows // WIN_LAT, WIN_LAT, lon_cols // WIN_LON, WIN_LON, channels)
    blocked = blocked.transpose(0, 2, 4, 1, 3, 5, 6)
    return blocked.reshape(-1, WIN_LEV * WIN_LAT * WIN_LON, channels)

def from_windows(blocks, levels, lat_rows, lon_cols):
    channels = blocks.shape[-1]
    blocked = blocks.reshape(levels // WIN_LEV, lat_rows // WIN_LAT, lon_cols // WIN_LON, WIN_LEV, WIN_LAT, WIN_LON, channels)
    blocked = blocked.transpose(0, 3, 1, 4, 2, 5, 6)
    return blocked.reshape(levels, lat_rows, lon_cols, channels)

def head_split(block):
    count, span, channels = block.shape
    return block.astype(jnp.float32).reshape(count, span, HEADS, channels // HEADS)

def softmax_probs(q_heads, k_heads, region):
    factor = 1.0 / math.sqrt(q_heads.shape[-1])
    raw = jnp.einsum('wqhd,wkhd->whqk', q_heads, k_heads) * factor
    same = region[:, :, None] == region[:, None, :]
    raw = jnp.where(same[:, None], raw, -1000000000.0)
    return jax.nn.softmax(raw, axis=-1)

def attend(queries, key_rows, val_rows, region):
    count, span, channels = queries.shape
    probs = softmax_probs(head_split(queries), head_split(key_rows), region)
    rounded = probs.astype(jnp.bfloat16).astype(jnp.float32)
    mixed = jnp.einsum('whqk,wkhd->wqhd', rounded, head_split(val_rows))
    return mixed.astype(jnp.bfloat16).reshape(count, span, channels)

def attend_back(queries, key_rows, val_rows, region, grad_mixed):
    count, span, channels = queries.shape
    q_heads = head_split(queries)
    k_heads = head_split(key_rows)
    v_heads = head_split(val_rows)
    g_heads = head_split(grad_mixed)
    factor = 1.0 / math.sqrt(q_heads.shape[-1])
    probs = softmax_probs(q_heads, k_heads, region)
    rounded = probs.astype(jnp.bfloat16).astype(jnp.float32)
    grad_vals = jnp.einsum('whqk,wqhd->wkhd', rounded, g_heads).astype(jnp.bfloat16)
    grad_probs = jnp.einsum('wqhd,wkhd->whqk', g_heads, v_heads)
    inner = lax.optimization_barrier(jnp.sum(grad_probs * probs, axis=-1, keepdims=True))
    grad_raw = (probs * (grad_probs - inner) * factor).astype(jnp.bfloat16).astype(jnp.float32)
    grad_query = jnp.einsum('whqk,wkhd->wqhd', grad_raw, k_heads).astype(jnp.bfloat16)
    grad_key = jnp.einsum('whqk,wqhd->wkhd', grad_raw, q_heads).astype(jnp.bfloat16)
    joined = jnp.concatenate([grad_query.reshape(count, span, channels), grad_key.reshape(count, span, channels), grad_vals.reshape(count, span, channels)], axis=-1)
    return joined

def reference(fields, cotangent, layer_norm_gain, qkv_weight, out_weight):
    levels, lat_rows, lon_cols, channels = fields.shape
    span = WIN_LEV * WIN_LAT * WIN_LON
    shifts = (WIN_LEV // 2, WIN_LAT // 2, WIN_LON // 2)
    fields_f = fields.astype(jnp.float32)
    centre = lax.optimization_barrier(jnp.mean(fields_f, axis=-1, keepdims=True))
    mean_removed = fields_f - centre
    inverse_deviation = lax.rsqrt(lax.optimization_barrier(jnp.mean(mean_removed * mean_removed, axis=-1, keepdims=True)) + 1e-05)
    standardized_input = mean_removed * inverse_deviation
    normalized_fields = (standardized_input * layer_norm_gain).astype(jnp.bfloat16)
    rolled = jnp.roll(normalized_fields, (-shifts[0], -shifts[1], -shifts[2]), axis=(0, 1, 2))
    rolled_grad = jnp.roll(cotangent, (-shifts[0], -shifts[1], -shifts[2]), axis=(0, 1, 2))
    level_reg = (jnp.arange(levels) == levels - 1).astype(jnp.int32)
    lat_reg = (jnp.arange(lat_rows) >= lat_rows - shifts[1]).astype(jnp.int32)
    region_grid = 2 * level_reg[:, None, None] + lat_reg[None, :, None] + jnp.zeros((levels, lat_rows, lon_cols), jnp.int32)
    per_group = lon_cols // WIN_LON
    groups = levels // WIN_LEV * (lat_rows // WIN_LAT)
    win_norm = to_windows(rolled).reshape(groups, per_group, span, channels)
    win_grad = to_windows(rolled_grad).reshape(groups, per_group, span, channels)
    win_region = to_windows(region_grid[..., None]).reshape(groups, per_group, span)

    def one_group(carry, pieces):
        acc_qkv, acc_out = carry
        block, grad_block, region = pieces
        flat = block.reshape(-1, channels)
        qkv = jnp.dot(flat, qkv_weight, preferred_element_type=jnp.float32).astype(jnp.bfloat16)
        qkv = qkv.reshape(per_group, span, 3 * channels)
        queries = qkv[..., :channels]
        key_rows = qkv[..., channels:2 * channels]
        val_rows = qkv[..., 2 * channels:]
        mixed = attend(queries, key_rows, val_rows, region)
        mixed_flat = mixed.reshape(-1, channels)
        proj = jnp.dot(mixed_flat, out_weight, preferred_element_type=jnp.float32).astype(jnp.bfloat16)
        grad_flat = grad_block.reshape(-1, channels)
        acc_out = acc_out + jnp.dot(mixed_flat.T, grad_flat, preferred_element_type=jnp.float32)
        grad_mixed = jnp.dot(grad_flat, out_weight.T, preferred_element_type=jnp.float32).astype(jnp.bfloat16)
        grad_act = attend_back(queries, key_rows, val_rows, region, grad_mixed.reshape(per_group, span, channels))
        grad_act = grad_act.reshape(-1, 3 * channels)
        acc_qkv = acc_qkv + jnp.dot(flat.T, grad_act, preferred_element_type=jnp.float32)
        grad_norm = jnp.dot(grad_act, qkv_weight.T, preferred_element_type=jnp.float32).astype(jnp.bfloat16)
        return ((acc_qkv, acc_out), (proj.reshape(per_group, span, channels), grad_norm.reshape(per_group, span, channels)))
    start = (jnp.zeros((channels, 3 * channels), jnp.float32), jnp.zeros((channels, channels), jnp.float32))
    (grad_qkv, grad_out), (proj_all, gnorm_all) = lax.scan(one_group, start, (win_norm, win_grad, win_region))
    proj_grid = from_windows(proj_all.reshape(-1, span, channels), levels, lat_rows, lon_cols)
    gnorm_grid = from_windows(gnorm_all.reshape(-1, span, channels), levels, lat_rows, lon_cols)
    proj_back = jnp.roll(proj_grid, shifts, axis=(0, 1, 2))
    normalized_gradient = jnp.roll(gnorm_grid, shifts, axis=(0, 1, 2)).astype(jnp.float32)
    output = (fields_f + proj_back.astype(jnp.float32)).astype(jnp.bfloat16)
    norm_gain_gradient = lax.optimization_barrier(jnp.sum(normalized_gradient * standardized_input, axis=(0, 1, 2)))
    gain_scaled = normalized_gradient * layer_norm_gain
    first_term = lax.optimization_barrier(jnp.mean(gain_scaled, axis=-1, keepdims=True))
    second_term = lax.optimization_barrier(jnp.mean(gain_scaled * standardized_input, axis=-1, keepdims=True))
    fields_gradient = (cotangent.astype(jnp.float32) + inverse_deviation * (gain_scaled - first_term - standardized_input * second_term)).astype(jnp.bfloat16)
    return (output, fields_gradient, grad_qkv, grad_out, norm_gain_gradient)
```

```python
import functools
import math

import jax
import jax.numpy as jnp
import numpy as np
from jax import lax
from jax.experimental import pallas as pl
from jax.experimental.pallas import tpu as pltpu
from jax.sharding import PartitionSpec as P

HEADS = 8
LEV, ROWS, COLS = 4, 6, 24
WL, WR, WC = 2, 6, 12
D = 512
SPAN = WL * WR * WC
TOK = LEV * ROWS * COLS
BOTH = ("lat", "lon")
f32 = jnp.float32
bf16 = jnp.bfloat16
VMEM = 56 * 1024 * 1024


def index_of(y, x, z, c):
    return (y * 2 + x // 2) * 32 + (x % 2) * 16 + z * 2 + c


def place_of(i):
    return i // 64, ((i // 32) % 2) * 2 + (i // 16) % 2, (i // 2) % 8, i % 2


def route(step):
    return [(i, index_of(*step(*place_of(i)))) for i in range(256)]


def to_sibling(y, x, z, c):
    return y, x, z, 1 - c


def first_axis(k):
    return lambda y, x, z, c: ((y + k) % 4, x, z, c) if c == 0 else (y, (x + k) % 4, z, c)


def second_axis(k):
    return lambda y, x, z, c: (y, (x + k) % 4, z, c) if c == 0 else ((y + k) % 4, x, z, c)


def flip_z(k):
    return lambda y, x, z, c: (y, x, z ^ k, c)


def send(x, step):
    return lax.ppermute(x, BOTH, route(step))


def shifted(dlat, dlon):
    def pairs():
        out = []
        for i in range(256):
            a, b = i // 32, i % 32
            out.append((i, ((a + dlat) % 8) * 32 + (b + dlon) % 32))
        return out

    return pairs()


def gather_tables():
    local = np.zeros((TOK, TOK), np.float32)
    lat = np.zeros((TOK, LEV * 3 * 18), np.float32)
    lon = np.zeros((TOK, LEV * 3 * 6), np.float32)
    diag = np.zeros((TOK, LEV * 3 * 6), np.float32)
    for lr in range(LEV):
        for rr in range(ROWS):
            for cr in range(COLS):
                w = (lr // WL) * (COLS // WC) + cr // WC
                t = w * SPAN + (lr % WL) * WR * WC + rr * WC + cr % WC
                lo, r, c = (lr + 1) % LEV, rr + 3, cr + 6
                if r < ROWS and c < COLS:
                    local[t, lo * ROWS * COLS + r * COLS + c] = 1
                elif c < COLS:
                    lat[t, lo * 54 + (r - ROWS) * 18 + c - 6] = 1
                elif r < ROWS:
                    lon[t, lo * 18 + (r - 3) * 6 + c - COLS] = 1
                else:
                    diag[t, lo * 18 + (r - ROWS) * 6 + c - COLS] = 1
    return local, lat, lon, diag


def scatter_tables():
    lat = np.zeros((TOK, LEV * 3 * 18), np.float32)
    lon = np.zeros((TOK, LEV * 3 * 6), np.float32)
    diag = np.zeros((TOK, LEV * 3 * 6), np.float32)
    for lv in range(LEV):
        for r in range(ROWS):
            for c in range(COLS):
                t = lv * ROWS * COLS + r * COLS + c
                if r < 3 and c >= 6:
                    lat[t, lv * 54 + r * 18 + c - 6] = 1
                elif r >= 3 and c < 6:
                    lon[t, lv * 18 + (r - 3) * 6 + c] = 1
                elif r < 3:
                    diag[t, lv * 18 + r * 6 + c] = 1
    return lat, lon, diag


def dot(a, b, dims=((1,), (0,))):
    return lax.dot_general(a, b, (dims, ((), ())), preferred_element_type=f32)


NT = ((1,), (1,))
TN = ((0,), (0,))


def normalise(x):
    centred = x - jnp.mean(x, axis=-1, keepdims=True)
    rstd = lax.rsqrt(jnp.mean(centred * centred, axis=-1, keepdims=True) + 1e-5)
    return centred * rstd, rstd


def main_kernel(
    place,
    f_loc, f_lat, f_lon, f_diag,
    c_loc, c_lat, c_lon, c_diag,
    p_loc, p_lat, p_lon, p_diag,
    gain, w_ref, o_ref,
    mixed, gact, own, other,
    normed, qkv, ctw, gm, acc,
):
    def windows(a, b, c, d):
        return (
            dot(p_loc[...], a[...])
            + dot(p_lat[...], b[...])
            + dot(p_lon[...], c[...])
            + dot(p_diag[...], d[...])
        )

    xhat, _ = normalise(windows(f_loc, f_lat, f_lon, f_diag))
    normed[...] = (xhat * gain[...]).astype(bf16)
    qkv[...] = dot(normed[...], w_ref[...]).astype(bf16)
    ctw[...] = windows(c_loc, c_lat, c_lon, c_diag).astype(bf16)
    gm[...] = dot(ctw[...], o_ref[...], NT).astype(bf16)

    last_lat = place[0]
    two = 2 * SPAN
    row2 = lax.broadcasted_iota(jnp.int32, (two, 128), 0)
    lane2 = lax.broadcasted_iota(jnp.int32, (two, 128), 1)
    pick = ((row2 < SPAN) == (lane2 < 64)).astype(f32).astype(bf16)
    low = lax.broadcasted_iota(jnp.int32, (SPAN, 128), 1) < 64

    def lev_of(t):
        return (t >= SPAN // 2).astype(jnp.int32)

    def half_of(t):
        u = t - SPAN // 2 * lev_of(t)
        return (u >= SPAN // 4).astype(jnp.int32)

    tq = lax.broadcasted_iota(jnp.int32, (two, SPAN), 0)
    tq = tq - SPAN * (tq >= SPAN).astype(jnp.int32)
    tk = lax.broadcasted_iota(jnp.int32, (two, SPAN), 1)
    lev_diff = jnp.abs(lev_of(tq) - lev_of(tk))
    half_diff = jnp.abs(half_of(tq) - half_of(tk)) * last_lat
    factor = 1.0 / math.sqrt(D // HEADS)

    def join(r):
        return jnp.where(low, r[:SPAN], r[SPAN:]).astype(bf16)

    def window(w, carry):
        at = pl.ds(pl.multiple_of(w * SPAN, SPAN), SPAN)
        top = (w >= 2).astype(jnp.int32)
        same = (lev_diff * top + half_diff) == 0
        for p in range(HEADS // 2):
            cols = pl.ds(128 * p, 128)
            q = qkv[at, pl.ds(128 * p, 128)]
            k = qkv[at, pl.ds(D + 128 * p, 128)]
            v = qkv[at, pl.ds(2 * D + 128 * p, 128)]
            g = gm[at, cols]
            q2 = jnp.concatenate([q, q], axis=0) * pick
            g2 = jnp.concatenate([g, g], axis=0) * pick
            s = jnp.where(same, dot(q2, k, NT) * factor, -1000000000.0)
            e = jnp.exp(s - jnp.max(s, axis=-1, keepdims=True))
            probs = e * (1.0 / jnp.sum(e, axis=-1, keepdims=True))
            rounded = probs.astype(bf16)
            mixed[at, cols] = join(dot(rounded, v))
            gact[at, pl.ds(2 * D + 128 * p, 128)] = dot(rounded, g2, TN).astype(bf16)
            dp = dot(g2, v, NT)
            inner = jnp.sum(dp * probs, axis=-1, keepdims=True)
            ds = (probs * (dp - inner) * factor).astype(bf16)
            gact[at, cols] = join(dot(ds, k))
            gact[at, pl.ds(D + 128 * p, 128)] = dot(ds, q2, TN).astype(bf16)
        return carry

    lax.fori_loop(0, 4, window, 0)

    acc[:, : 3 * D] = dot(normed[...], gact[...], TN)
    acc[:, 3 * D :] = dot(mixed[...], ctw[...], TN)

    y, x, c = place[1], place[2], place[3]

    def fill(out, core):
        d1 = jnp.where(core == 0, y, x)
        d2 = jnp.where(core == 0, x, y)
        for s1 in range(4):
            for s2 in range(4):
                r = core * 256 + lax.rem(d1 + s1, 4) * 64 + lax.rem(d2 + s2, 4) * 16
                rows = acc[pl.ds(pl.multiple_of(r, 16), 16), :]
                out[pl.ds((s1 * 4 + s2) * 16, 16), :] = rows.astype(bf16)

    fill(own, c)
    fill(other, 1 - c)


def back_kernel(mixed, gact, w_ref, o_ref, p_lat, p_lon, p_diag, both, to_lat, to_lon, to_diag):
    both[:, :D] = dot(mixed[...], o_ref[...]).astype(bf16)
    both[:, D:] = dot(gact[...], w_ref[...], NT).astype(bf16)
    to_lat[...] = dot(p_lat[...], both[...], TN).astype(bf16)
    to_lon[...] = dot(p_lon[...], both[...], TN).astype(bf16)
    to_diag[...] = dot(p_diag[...], both[...], TN).astype(bf16)


def finish_kernel(
    f_loc, c_loc, both, r_lat, r_lon, r_diag, p_loc, s_lat, s_lon, s_diag, gain, out, grad
):
    grid = (
        dot(p_loc[...], both[...], TN)
        + dot(s_lat[...], r_lat[...])
        + dot(s_lon[...], r_lon[...])
        + dot(s_diag[...], r_diag[...])
    )
    x = f_loc[...].astype(f32)
    out[...] = (x + grid[:, :D]).astype(bf16)
    xhat, rstd = normalise(x)
    g = grid[:, D:] * gain[...]
    first = jnp.mean(g, axis=-1, keepdims=True)
    second = jnp.mean(g * xhat, axis=-1, keepdims=True)
    grad[...] = (c_loc[...].astype(f32) + rstd * (g - first - xhat * second)).astype(bf16)


def weights_kernel(place, *refs):
    pieces, (w_ref, gain, g_qkv, g_out, g_gain) = refs[:8], refs[8:]
    y, x, c = place[1], place[2], place[3]
    for side in range(2):
        core = c if side == 0 else 1 - c
        d1 = jnp.where(core == 0, y, x)
        d2 = jnp.where(core == 0, x, y)
        for s1 in range(4):
            for s2 in range(4):
                r = core * 256 + lax.rem(d1 + s1, 4) * 64 + lax.rem(d2 + s2, 4) * 16
                at = pl.ds(pl.multiple_of(r, 16), 16)
                block = pieces[side * 4 + s1][pl.ds(s2 * 16, 16), :].astype(f32)
                g_qkv[at, :] = block[:, : 3 * D]
                g_out[at, :] = block[:, 3 * D :]
    total = jnp.sum(g_qkv[...] * w_ref[...].astype(f32), axis=1, keepdims=True)
    g_gain[...] = total / gain[...]


def params():
    return pltpu.CompilerParams(vmem_limit_bytes=VMEM)


def spec(count, scalar=False):
    whole = [pl.BlockSpec(memory_space=pltpu.VMEM)] * count
    return ([pl.BlockSpec(memory_space=pltpu.SMEM)] if scalar else []) + whole


def shape(*dims, dtype=bf16):
    return jax.ShapeDtypeStruct(dims, dtype)


def cost(flops, moved):
    return pl.CostEstimate(flops=flops, bytes_accessed=moved, transcendentals=0)


def add(*xs):
    total = xs[0].astype(f32)
    for x in xs[1:]:
        total = total + x.astype(f32)
    return total.astype(bf16)


def halo(field):
    lat = field[:, :3, 6:].reshape(-1, D)
    lon = field[:, 3:, :6].reshape(-1, D)
    diag = field[:, :3, :6].reshape(-1, D)
    return (
        lax.ppermute(lat, BOTH, shifted(-1, 0)),
        lax.ppermute(lon, BOTH, shifted(0, -1)),
        lax.ppermute(diag, BOTH, shifted(-1, -1)),
    )


def on_device(fields, cotangent, layer_norm_gain, qkv_weight, out_weight):
    a, b = lax.axis_index("lat"), lax.axis_index("lon")
    place = jnp.stack(
        [
            (a == 7).astype(jnp.int32),
            (a // 2).astype(jnp.int32),
            ((a % 2) * 2 + b // 16).astype(jnp.int32),
            (b % 2).astype(jnp.int32),
        ]
    )
    gain_row = layer_norm_gain.reshape(1, D)
    p_loc, p_lat, p_lon, p_diag = [jnp.asarray(t, bf16) for t in gather_tables()]
    s_lat, s_lon, s_diag = [jnp.asarray(t, bf16) for t in scatter_tables()]
    f_loc, c_loc = fields.reshape(TOK, D), cotangent.reshape(TOK, D)
    f_halo = halo(fields)
    c_halo = halo(cotangent)

    mixed, gact, own, other = pl.pallas_call(
        main_kernel,
        out_shape=[shape(TOK, D), shape(TOK, 3 * D), shape(256, 4 * D), shape(256, 4 * D)],
        in_specs=spec(15, True),
        out_specs=spec(4),
        scratch_shapes=[
            pltpu.VMEM((TOK, D), bf16),
            pltpu.VMEM((TOK, 3 * D), bf16),
            pltpu.VMEM((TOK, D), bf16),
            pltpu.VMEM((TOK, D), bf16),
            pltpu.VMEM((D, 4 * D), f32),
        ],
        compiler_params=params(),
        cost_estimate=cost(8 * 10**9, 10**7),
        name="main",
    )(
        place, f_loc, *f_halo, c_loc, *c_halo, p_loc, p_lat, p_lon, p_diag,
        gain_row, qkv_weight, out_weight,
    )

    there = send(other, to_sibling)
    part = [add(own[64 * k : 64 * k + 64], there[64 * k : 64 * k + 64]) for k in range(4)]
    part = add(part[0], *[send(part[k], first_axis(k)) for k in (1, 2, 3)])
    part = add(part[:16], *[send(part[16 * k : 16 * k + 16], second_axis(k)) for k in (1, 2, 3)])
    for k in (1, 2, 4):
        part = add(part, send(part, flip_z(k)))

    both, to_lat, to_lon, to_diag = pl.pallas_call(
        back_kernel,
        out_shape=[shape(TOK, 2 * D), shape(216, 2 * D), shape(72, 2 * D), shape(72, 2 * D)],
        in_specs=spec(7),
        out_specs=spec(4),
        compiler_params=params(),
        cost_estimate=cost(2 * 10**9, 5 * 10**6),
        name="back",
    )(mixed, gact, qkv_weight, out_weight, p_lat, p_lon, p_diag)
    r_lat = lax.ppermute(to_lat, BOTH, shifted(1, 0))
    r_lon = lax.ppermute(to_lon, BOTH, shifted(0, 1))
    r_diag = lax.ppermute(to_diag, BOTH, shifted(1, 1))
    out, grad = pl.pallas_call(
        finish_kernel,
        out_shape=[shape(TOK, D), shape(TOK, D)],
        in_specs=spec(11),
        out_specs=spec(2),
        compiler_params=params(),
        cost_estimate=cost(2 * 10**9, 8 * 10**6),
        name="finish",
    )(f_loc, c_loc, both, r_lat, r_lon, r_diag, p_loc, s_lat, s_lon, s_diag, gain_row)

    block = jnp.concatenate([part] + [send(part, second_axis(4 - s)) for s in (1, 2, 3)], axis=0)
    mine = [block] + [send(block, first_axis(4 - s)) for s in (1, 2, 3)]
    sibling = [send(m, to_sibling) for m in mine]
    g_qkv, g_out, g_gain = pl.pallas_call(
        weights_kernel,
        out_shape=[shape(D, 3 * D, dtype=f32), shape(D, D, dtype=f32), shape(D, 1, dtype=f32)],
        in_specs=spec(10, True),
        out_specs=spec(3),
        compiler_params=params(),
        cost_estimate=cost(10**7, 8 * 10**6),
        name="weights",
    )(place, *mine, *sibling, qkv_weight, layer_norm_gain.reshape(D, 1))

    grid = (LEV, ROWS, COLS, D)
    return out.reshape(grid), grad.reshape(grid), g_qkv, g_out, g_gain.reshape(D)


def solution(mesh):
    return jax.shard_map(
        on_device,
        mesh=mesh,
        in_specs=(P(None, "lat", "lon", None), P(None, "lat", "lon", None), P(), P(), P()),
        out_specs=(P(None, "lat", "lon", None), P(None, "lat", "lon", None), P(), P(), P()),
        check_vma=False,
    )
```

```python
import functools
import math

import jax
import jax.numpy as jnp
import numpy as np
from jax import lax
from jax.experimental import pallas as pl
from jax.experimental.pallas import tpu as pltpu
from jax.sharding import PartitionSpec as P

HEADS = 8
LEV, ROWS, COLS = 4, 6, 24
WL, WR, WC = 2, 6, 12
D = 512
SPAN = WL * WR * WC
TOK = LEV * ROWS * COLS
BOTH = ("lat", "lon")
f32 = jnp.float32
bf16 = jnp.bfloat16
VMEM = 24 * 1024 * 1024


def index_of(y, x, z, c):
    return (y * 2 + x // 2) * 32 + (x % 2) * 16 + z * 2 + c


def place_of(i):
    return i // 64, ((i // 32) % 2) * 2 + (i // 16) % 2, (i // 2) % 8, i % 2


def route(step):
    return [(i, index_of(*step(*place_of(i)))) for i in range(256)]


def to_sibling(y, x, z, c):
    return y, x, z, 1 - c


def first_axis(k):
    return lambda y, x, z, c: ((y + k) % 4, x, z, c) if c == 0 else (y, (x + k) % 4, z, c)


def second_axis(k):
    return lambda y, x, z, c: (y, (x + k) % 4, z, c) if c == 0 else ((y + k) % 4, x, z, c)


def flip_z(k):
    return lambda y, x, z, c: (y, x, z ^ k, c)


def send(x, step):
    return lax.ppermute(x, BOTH, route(step))


def shifted(dlat, dlon):
    def pairs():
        out = []
        for i in range(256):
            a, b = i // 32, i % 32
            out.append((i, ((a + dlat) % 8) * 32 + (b + dlon) % 32))
        return out

    return pairs()


def gather_tables():
    local = np.zeros((TOK, TOK), np.float32)
    lat = np.zeros((TOK, LEV * 3 * 18), np.float32)
    lon = np.zeros((TOK, LEV * 3 * 6), np.float32)
    diag = np.zeros((TOK, LEV * 3 * 6), np.float32)
    for lr in range(LEV):
        for rr in range(ROWS):
            for cr in range(COLS):
                w = (lr // WL) * (COLS // WC) + cr // WC
                t = w * SPAN + (lr % WL) * WR * WC + rr * WC + cr % WC
                lo, r, c = (lr + 1) % LEV, rr + 3, cr + 6
                if r < ROWS and c < COLS:
                    local[t, lo * ROWS * COLS + r * COLS + c] = 1
                elif c < COLS:
                    lat[t, lo * 54 + (r - ROWS) * 18 + c - 6] = 1
                elif r < ROWS:
                    lon[t, lo * 18 + (r - 3) * 6 + c - COLS] = 1
                else:
                    diag[t, lo * 18 + (r - ROWS) * 6 + c - COLS] = 1
    return local, lat, lon, diag


def scatter_tables():
    lat = np.zeros((TOK, LEV * 3 * 18), np.float32)
    lon = np.zeros((TOK, LEV * 3 * 6), np.float32)
    diag = np.zeros((TOK, LEV * 3 * 6), np.float32)
    for lv in range(LEV):
        for r in range(ROWS):
            for c in range(COLS):
                t = lv * ROWS * COLS + r * COLS + c
                if r < 3 and c >= 6:
                    lat[t, lv * 54 + r * 18 + c - 6] = 1
                elif r >= 3 and c < 6:
                    lon[t, lv * 18 + (r - 3) * 6 + c] = 1
                elif r < 3:
                    diag[t, lv * 18 + r * 6 + c] = 1
    return lat, lon, diag


def dot(a, b, dims=((1,), (0,))):
    return lax.dot_general(a, b, (dims, ((), ())), preferred_element_type=f32)


NT = ((1,), (1,))
TN = ((0,), (0,))


def normalise(x):
    centred = x - jnp.mean(x, axis=-1, keepdims=True)
    rstd = lax.rsqrt(jnp.mean(centred * centred, axis=-1, keepdims=True) + 1e-5)
    return centred * rstd, rstd


def pairs_mask():
    row = lax.broadcasted_iota(jnp.int32, (2 * SPAN, 128), 0)
    lane = lax.broadcasted_iota(jnp.int32, (2 * SPAN, 128), 1)
    return ((row < SPAN) == (lane < 64)).astype(f32).astype(bf16)


def joined(r):
    low = lax.broadcasted_iota(jnp.int32, (SPAN, 128), 1) < 64
    return jnp.where(low, r[:SPAN], r[SPAN:]).astype(bf16)


def doubled(x, pick):
    return jnp.concatenate([x, x], axis=0) * pick


def gathered(pieces, tables):
    total = dot(tables[0][...], pieces[0][...])
    for p, t in zip(pieces[1:], tables[1:]):
        total = total + dot(t[...], p[...])
    return total


def forward_kernel(place, *refs):
    pieces, tables, (gain, w_ref, normed, qkv, probs, mixed) = refs[:4], refs[4:8], refs[8:]
    xhat, _ = normalise(gathered(pieces, tables))
    normed[...] = (xhat * gain[...]).astype(bf16)
    qkv[...] = dot(normed[...], w_ref[...]).astype(bf16)

    last_lat = place[0]
    two = 2 * SPAN
    pick = pairs_mask()

    def lev_of(t):
        return (t >= SPAN // 2).astype(jnp.int32)

    def half_of(t):
        return (t - SPAN // 2 * lev_of(t) >= SPAN // 4).astype(jnp.int32)

    tq = lax.broadcasted_iota(jnp.int32, (two, SPAN), 0)
    tq = tq - SPAN * (tq >= SPAN).astype(jnp.int32)
    tk = lax.broadcasted_iota(jnp.int32, (two, SPAN), 1)
    lev_diff = jnp.abs(lev_of(tq) - lev_of(tk))
    half_diff = jnp.abs(half_of(tq) - half_of(tk)) * last_lat
    factor = 1.0 / math.sqrt(D // HEADS)

    def window(w, carry):
        at = pl.ds(pl.multiple_of(w * SPAN, SPAN), SPAN)
        top = (w >= 2).astype(jnp.int32)
        same = (lev_diff * top + half_diff) == 0
        for p in range(HEADS // 2):
            q2 = doubled(qkv[at, pl.ds(128 * p, 128)], pick)
            k = qkv[at, pl.ds(D + 128 * p, 128)]
            v = qkv[at, pl.ds(2 * D + 128 * p, 128)]
            s = jnp.where(same, dot(q2, k, NT) * factor, -1000000000.0)
            e = jnp.exp(s - jnp.max(s, axis=-1, keepdims=True))
            rounded = (e * (1.0 / jnp.sum(e, axis=-1, keepdims=True))).astype(bf16)
            probs[pl.ds(pl.multiple_of((w * 4 + p) * two, two), two), :] = rounded
            mixed[at, pl.ds(128 * p, 128)] = joined(dot(rounded, v))
        return carry

    lax.fori_loop(0, 4, window, 0)


def backward_kernel(place, *refs):
    pieces, tables, (o_ref, normed, qkv, probs, mixed, gact, own, other, ctw, gm, acc) = (
        refs[:4], refs[4:8], refs[8:],
    )
    ctw[...] = gathered(pieces, tables).astype(bf16)
    gm[...] = dot(ctw[...], o_ref[...], NT).astype(bf16)
    two = 2 * SPAN
    pick = pairs_mask()
    factor = 1.0 / math.sqrt(D // HEADS)

    def window(w, carry):
        at = pl.ds(pl.multiple_of(w * SPAN, SPAN), SPAN)
        for p in range(HEADS // 2):
            cols = pl.ds(128 * p, 128)
            q2 = doubled(qkv[at, cols], pick)
            g2 = doubled(gm[at, cols], pick)
            k = qkv[at, pl.ds(D + 128 * p, 128)]
            v = qkv[at, pl.ds(2 * D + 128 * p, 128)]
            rounded = probs[pl.ds(pl.multiple_of((w * 4 + p) * two, two), two), :]
            gact[at, pl.ds(2 * D + 128 * p, 128)] = dot(rounded, g2, TN).astype(bf16)
            dp = dot(g2, v, NT)
            pr = rounded.astype(f32)
            inner = jnp.sum(dp * pr, axis=-1, keepdims=True)
            ds = (pr * (dp - inner) * factor).astype(bf16)
            gact[at, cols] = joined(dot(ds, k))
            gact[at, pl.ds(D + 128 * p, 128)] = dot(ds, q2, TN).astype(bf16)
        return carry

    lax.fori_loop(0, 4, window, 0)

    acc[:, : 3 * D] = dot(normed[...], gact[...], TN)
    acc[:, 3 * D :] = dot(mixed[...], ctw[...], TN)
    y, x, c = place[1], place[2], place[3]

    def fill(out, core):
        d1 = jnp.where(core == 0, y, x)
        d2 = jnp.where(core == 0, x, y)
        for s1 in range(4):
            for s2 in range(4):
                r = core * 256 + lax.rem(d1 + s1, 4) * 64 + lax.rem(d2 + s2, 4) * 16
                rows = acc[pl.ds(pl.multiple_of(r, 16), 16), :]
                out[pl.ds((s1 * 4 + s2) * 16, 16), :] = rows.astype(bf16)

    fill(own, c)
    fill(other, 1 - c)


def back_kernel(mixed, gact, w_ref, o_ref, p_lat, p_lon, p_diag, both, to_lat, to_lon, to_diag):
    both[:, :D] = dot(mixed[...], o_ref[...]).astype(bf16)
    both[:, D:] = dot(gact[...], w_ref[...], NT).astype(bf16)
    to_lat[...] = dot(p_lat[...], both[...], TN).astype(bf16)
    to_lon[...] = dot(p_lon[...], both[...], TN).astype(bf16)
    to_diag[...] = dot(p_diag[...], both[...], TN).astype(bf16)


def finish_kernel(
    f_loc, c_loc, both, r_lat, r_lon, r_diag, p_loc, s_lat, s_lon, s_diag, gain, out, grad
):
    grid = (
        dot(p_loc[...], both[...], TN)
        + dot(s_lat[...], r_lat[...])
        + dot(s_lon[...], r_lon[...])
        + dot(s_diag[...], r_diag[...])
    )
    x = f_loc[...].astype(f32)
    out[...] = (x + grid[:, :D]).astype(bf16)
    xhat, rstd = normalise(x)
    g = grid[:, D:] * gain[...]
    first = jnp.mean(g, axis=-1, keepdims=True)
    second = jnp.mean(g * xhat, axis=-1, keepdims=True)
    grad[...] = (c_loc[...].astype(f32) + rstd * (g - first - xhat * second)).astype(bf16)


def weights_kernel(side, place, *refs):
    pieces, refs = refs[:4], refs[4:]
    if side == 0:
        w_ref, g_qkv, g_out, g_total = refs
    else:
        w_ref, before, gain, _, _, g_qkv, g_out, g_total = refs
    y, x, c = place[1], place[2], place[3]
    step = pl.program_id(0)
    core = c if side == 0 else 1 - c
    d1 = jnp.where(core == 0, y, x)
    d2 = jnp.where(core == 0, x, y)

    @pl.when(step == 0)
    def _():
        g_total[...] = jnp.zeros_like(g_total) if side == 0 else before[...]

    for i in range(4):

        @pl.when(step == i)
        def _(i=i):
            for s2 in range(4):
                at = pl.ds(pl.multiple_of(lax.rem(d2 + s2, 4) * 16, 16), 16)
                block = pieces[i][pl.ds(s2 * 16, 16), :].astype(f32)
                g_qkv[at, :] = block[:, : 3 * D]
                g_out[at, :] = block[:, 3 * D :]

    row = core * 256 + lax.rem(d1 + step, 4) * 64
    lane = lax.broadcasted_iota(jnp.int32, (64, D), 1)
    here = lax.broadcasted_iota(jnp.int32, (64, D), 0) + row
    sums = jnp.sum(g_qkv[...] * w_ref[...].astype(f32), axis=1, keepdims=True)
    g_total[...] += jnp.sum(jnp.where(lane == here, sums, 0.0), axis=0, keepdims=True)

    if side == 1:

        @pl.when(step == 3)
        def _():
            g_total[...] = g_total[...] / gain[...]


def band(side, step, place):
    y, x, c = place[1], place[2], place[3]
    core = c if side == 0 else 1 - c
    d1 = jnp.where(core == 0, y, x)
    return core * 4 + lax.rem(d1 + step, 4), 0


def to_weights(side, place, pieces, qkv_weight, *more):
    at = functools.partial(band, side)
    whole = pl.BlockSpec((64, 4 * D), lambda i, place: (0, 0))
    row = pl.BlockSpec((1, D), lambda i, place: (0, 0))
    anywhere = pl.BlockSpec(memory_space=pl.ANY)
    extra = [] if side == 0 else [row, row, anywhere, anywhere]
    return pl.pallas_call(
        functools.partial(weights_kernel, side),
        out_shape=[shape(D, 3 * D, dtype=f32), shape(D, D, dtype=f32), shape(1, D, dtype=f32)],
        grid_spec=pltpu.PrefetchScalarGridSpec(
            num_scalar_prefetch=1,
            grid=(4,),
            in_specs=[whole] * 4 + [pl.BlockSpec((64, 3 * D), at)] + extra,
            out_specs=[pl.BlockSpec((64, 3 * D), at), pl.BlockSpec((64, D), at), row],
        ),
        input_output_aliases={} if side == 0 else {8: 0, 9: 1},
        compiler_params=params(),
        cost_estimate=cost(10**7, 4 * 10**6),
        name="weights" + str(side),
    )(place, *vms(*pieces), qkv_weight, *more)


def params():
    return pltpu.CompilerParams(vmem_limit_bytes=VMEM)


def vm(x):
    return pltpu.with_memory_space_constraint(x, pltpu.VMEM)


def vms(*xs):
    return [vm(x) for x in xs]


def vshape(*dims, dtype=bf16):
    return pltpu.VMEM(dims, dtype)


def spec(count, scalar=False):
    whole = [pl.BlockSpec(memory_space=pltpu.VMEM)] * count
    return ([pl.BlockSpec(memory_space=pltpu.SMEM)] if scalar else []) + whole


def shape(*dims, dtype=bf16):
    return jax.ShapeDtypeStruct(dims, dtype)


def cost(flops, moved):
    return pl.CostEstimate(flops=flops, bytes_accessed=moved, transcendentals=0)


def to_forward(place, pieces, tables, gain_row, qkv_weight):
    return pl.pallas_call(
        forward_kernel,
        out_shape=[
            vshape(TOK, D), vshape(TOK, 3 * D), vshape(32 * SPAN, SPAN), vshape(TOK, D),
        ],
        in_specs=spec(10, True),
        out_specs=spec(4),
        compiler_params=params(),
        cost_estimate=cost(3 * 10**9, 10**7),
        name="forward",
    )(place, *vms(*pieces), *tables, gain_row, vm(qkv_weight))


def to_backward(place, pieces, tables, out_weight, *kept):
    return pl.pallas_call(
        backward_kernel,
        out_shape=[vshape(TOK, 3 * D), vshape(256, 4 * D), vshape(256, 4 * D)],
        in_specs=spec(13, True),
        out_specs=spec(3),
        scratch_shapes=[
            pltpu.VMEM((TOK, D), bf16),
            pltpu.VMEM((TOK, D), bf16),
            pltpu.VMEM((D, 4 * D), f32),
        ],
        compiler_params=params(),
        cost_estimate=cost(5 * 10**9, 10**7),
        name="backward",
    )(place, *vms(*pieces), *tables, vm(out_weight), *vms(*kept))


def to_back(mixed, gact, qkv_weight, out_weight, *tables):
    return pl.pallas_call(
        back_kernel,
        out_shape=[vshape(TOK, 2 * D), vshape(216, 2 * D), vshape(72, 2 * D), vshape(72, 2 * D)],
        in_specs=spec(7),
        out_specs=spec(4),
        compiler_params=params(),
        cost_estimate=cost(2 * 10**9, 5 * 10**6),
        name="back",
    )(*vms(mixed, gact, qkv_weight, out_weight, *tables))


def to_finish(*args):
    return pl.pallas_call(
        finish_kernel,
        out_shape=[shape(TOK, D), shape(TOK, D)],
        in_specs=spec(11),
        out_specs=spec(2),
        compiler_params=params(),
        cost_estimate=cost(2 * 10**9, 8 * 10**6),
        name="finish",
    )(*vms(*args))


def add(*xs):
    total = xs[0].astype(f32)
    for x in xs[1:]:
        total = total + x.astype(f32)
    return total.astype(bf16)


def tied(x):
    return lax.optimization_barrier(x)


def halo(field):
    lat = field[:, :3, 6:].reshape(-1, D)
    lon = field[:, 3:, :6].reshape(-1, D)
    diag = field[:, :3, :6].reshape(-1, D)
    return (
        lax.ppermute(lat, BOTH, shifted(-1, 0)),
        lax.ppermute(lon, BOTH, shifted(0, -1)),
        lax.ppermute(diag, BOTH, shifted(-1, -1)),
    )


def on_device(fields, cotangent, layer_norm_gain, qkv_weight, out_weight):
    a, b = lax.axis_index("lat"), lax.axis_index("lon")
    place = jnp.stack(
        [
            (a == 7).astype(jnp.int32),
            (a // 2).astype(jnp.int32),
            ((a % 2) * 2 + b // 16).astype(jnp.int32),
            (b % 2).astype(jnp.int32),
        ]
    )
    gain_row = layer_norm_gain.reshape(1, D)
    p_loc, p_lat, p_lon, p_diag = [jnp.asarray(t, bf16) for t in gather_tables()]
    s_lat, s_lon, s_diag = [jnp.asarray(t, bf16) for t in scatter_tables()]
    f_loc, c_loc = fields.reshape(TOK, D), cotangent.reshape(TOK, D)
    f_halo = halo(fields)
    c_halo = halo(cotangent)

    tables = vms(p_loc, p_lat, p_lon, p_diag)
    normed, qkv, probs, mixed = to_forward(place, (f_loc, *f_halo), tables, gain_row, qkv_weight)
    gact, own, other = to_backward(
        place, (c_loc, *c_halo), tables, out_weight, normed, qkv, probs, mixed
    )

    there = send(other, to_sibling)
    part = [add(own[64 * k : 64 * k + 64], there[64 * k : 64 * k + 64]) for k in range(4)]
    mixed, gact, part = tied((mixed, gact, part))
    both, to_lat, to_lon, to_diag = to_back(mixed, gact, qkv_weight, out_weight, *tables[1:])
    recv = [send(part[k], first_axis(k)) for k in (1, 2, 3)]
    recv, to_lat = tied((recv, to_lat))
    part = add(part[0], *recv)
    part, to_lat, to_lon, to_diag = tied((part, to_lat, to_lon, to_diag))
    part = add(part[:16], *[send(part[16 * k : 16 * k + 16], second_axis(k)) for k in (1, 2, 3)])
    r_lat = lax.ppermute(to_lat, BOTH, shifted(1, 0))
    r_lon = lax.ppermute(to_lon, BOTH, shifted(0, 1))
    r_diag = lax.ppermute(to_diag, BOTH, shifted(1, 1))
    for k in (1, 2, 6):
        part = add(part, send(part, flip_z(k)))

    block = jnp.concatenate([part] + [send(part, second_axis(4 - s)) for s in (1, 2, 3)], axis=0)
    mine = [send(block, first_axis(4 - s)) for s in (1, 2, 3)]
    out, grad = to_finish(
        f_loc, c_loc, both, r_lat, r_lon, r_diag, tables[0], s_lat, s_lon, s_diag, gain_row
    )
    mine, out = tied((mine, out))
    mine = [block] + mine
    sibling = [send(m, to_sibling) for m in mine]
    g_qkv, g_out, total = to_weights(0, place, mine, qkv_weight)
    g_qkv, g_out, g_gain = to_weights(
        1, place, sibling, qkv_weight, total, gain_row, g_qkv, g_out
    )

    grid = (LEV, ROWS, COLS, D)
    return out.reshape(grid), grad.reshape(grid), g_qkv, g_out, g_gain.reshape(D)


def solution(mesh):
    return jax.shard_map(
        on_device,
        mesh=mesh,
        in_specs=(P(None, "lat", "lon", None), P(None, "lat", "lon", None), P(), P(), P()),
        out_specs=(P(None, "lat", "lon", None), P(None, "lat", "lon", None), P(), P(), P()),
        check_vma=False,
    )
```

```python
import functools
import math

import jax
import jax.numpy as jnp
import numpy as np
from jax import lax
from jax.experimental import pallas as pl
from jax.experimental.pallas import tpu as pltpu
from jax.sharding import PartitionSpec as P

HEADS = 8
LEV, ROWS, COLS = 4, 6, 24
WL, WR, WC = 2, 6, 12
D = 512
SPAN = WL * WR * WC
TOK = LEV * ROWS * COLS
BOTH = ("lat", "lon")
f32 = jnp.float32
bf16 = jnp.bfloat16
VMEM = 24 * 1024 * 1024


def index_of(y, x, z, c):
    return (y * 2 + x // 2) * 32 + (x % 2) * 16 + z * 2 + c


def place_of(i):
    return i // 64, ((i // 32) % 2) * 2 + (i // 16) % 2, (i // 2) % 8, i % 2


def route(step):
    return [(i, index_of(*step(*place_of(i)))) for i in range(256)]


def to_sibling(y, x, z, c):
    return y, x, z, 1 - c


def first_axis(k):
    return lambda y, x, z, c: ((y + k) % 4, x, z, c) if c == 0 else (y, (x + k) % 4, z, c)


def second_axis(k):
    return lambda y, x, z, c: (y, (x + k) % 4, z, c) if c == 0 else ((y + k) % 4, x, z, c)


def flip_z(k):
    return lambda y, x, z, c: (y, x, z ^ k, c)


def send(x, step):
    return lax.ppermute(x, BOTH, route(step))


def shifted(dlat, dlon):
    def pairs():
        out = []
        for i in range(256):
            a, b = i // 32, i % 32
            out.append((i, ((a + dlat) % 8) * 32 + (b + dlon) % 32))
        return out

    return pairs()


def gather_tables():
    local = np.zeros((TOK, TOK), np.float32)
    lat = np.zeros((TOK, LEV * 3 * 18), np.float32)
    lon = np.zeros((TOK, LEV * 3 * 6), np.float32)
    diag = np.zeros((TOK, LEV * 3 * 6), np.float32)
    for lr in range(LEV):
        for rr in range(ROWS):
            for cr in range(COLS):
                w = (lr // WL) * (COLS // WC) + cr // WC
                t = w * SPAN + (lr % WL) * WR * WC + rr * WC + cr % WC
                lo, r, c = (lr + 1) % LEV, rr + 3, cr + 6
                if r < ROWS and c < COLS:
                    local[t, lo * ROWS * COLS + r * COLS + c] = 1
                elif c < COLS:
                    lat[t, lo * 54 + (r - ROWS) * 18 + c - 6] = 1
                elif r < ROWS:
                    lon[t, lo * 18 + (r - 3) * 6 + c - COLS] = 1
                else:
                    diag[t, lo * 18 + (r - ROWS) * 6 + c - COLS] = 1
    return local, lat, lon, diag


def scatter_tables():
    lat = np.zeros((TOK, LEV * 3 * 18), np.float32)
    lon = np.zeros((TOK, LEV * 3 * 6), np.float32)
    diag = np.zeros((TOK, LEV * 3 * 6), np.float32)
    for lv in range(LEV):
        for r in range(ROWS):
            for c in range(COLS):
                t = lv * ROWS * COLS + r * COLS + c
                if r < 3 and c >= 6:
                    lat[t, lv * 54 + r * 18 + c - 6] = 1
                elif r >= 3 and c < 6:
                    lon[t, lv * 18 + (r - 3) * 6 + c] = 1
                elif r < 3:
                    diag[t, lv * 18 + r * 6 + c] = 1
    return lat, lon, diag


def dot(a, b, dims=((1,), (0,))):
    return lax.dot_general(a, b, (dims, ((), ())), preferred_element_type=f32)


NT = ((1,), (1,))
TN = ((0,), (0,))


def normalise(x):
    centred = x - jnp.mean(x, axis=-1, keepdims=True)
    rstd = lax.rsqrt(jnp.mean(centred * centred, axis=-1, keepdims=True) + 1e-5)
    return centred * rstd, rstd


def pack_kernel(x, select, lat, lon, diag):
    rows = dot(select[...], x[...])
    lat[...] = rows[:216].astype(bf16)
    lon[...] = rows[216:288].astype(bf16)
    diag[...] = rows[288:].astype(bf16)


def pairs_mask():
    row = lax.broadcasted_iota(jnp.int32, (2 * SPAN, 128), 0)
    lane = lax.broadcasted_iota(jnp.int32, (2 * SPAN, 128), 1)
    return ((row < SPAN) == (lane < 64)).astype(f32).astype(bf16)


def joined(r):
    low = lax.broadcasted_iota(jnp.int32, (SPAN, 128), 1) < 64
    return jnp.where(low, r[:SPAN], r[SPAN:]).astype(bf16)


def doubled(x, pick):
    return jnp.concatenate([x, x], axis=0) * pick


def gathered(pieces, tables):
    total = dot(tables[0][...], pieces[0][...])
    for p, t in zip(pieces[1:], tables[1:]):
        total = total + dot(t[...], p[...])
    return total


def forward_kernel(place, *refs):
    pieces, tables, (gain, w_ref, normed, qkv, probs, mixed) = refs[:4], refs[4:8], refs[8:]
    xhat, _ = normalise(gathered(pieces, tables))
    normed[...] = (xhat * gain[...]).astype(bf16)
    qkv[...] = dot(normed[...], w_ref[...]).astype(bf16)

    last_lat = place[0]
    two = 2 * SPAN
    pick = pairs_mask()

    def lev_of(t):
        return (t >= SPAN // 2).astype(jnp.int32)

    def half_of(t):
        return (t - SPAN // 2 * lev_of(t) >= SPAN // 4).astype(jnp.int32)

    tq = lax.broadcasted_iota(jnp.int32, (two, SPAN), 0)
    tq = tq - SPAN * (tq >= SPAN).astype(jnp.int32)
    tk = lax.broadcasted_iota(jnp.int32, (two, SPAN), 1)
    lev_diff = jnp.abs(lev_of(tq) - lev_of(tk))
    half_diff = jnp.abs(half_of(tq) - half_of(tk)) * last_lat
    factor = 1.0 / math.sqrt(D // HEADS)

    def window(w, carry):
        at = pl.ds(pl.multiple_of(w * SPAN, SPAN), SPAN)
        top = (w >= 2).astype(jnp.int32)
        same = (lev_diff * top + half_diff) == 0
        for p in range(HEADS // 2):
            q2 = doubled(qkv[at, pl.ds(128 * p, 128)], pick)
            k = qkv[at, pl.ds(D + 128 * p, 128)]
            v = qkv[at, pl.ds(2 * D + 128 * p, 128)]
            s = jnp.where(same, dot(q2, k, NT) * factor, -1000000000.0)
            e = jnp.exp(s - jnp.max(s, axis=-1, keepdims=True))
            rounded = (e * (1.0 / jnp.sum(e, axis=-1, keepdims=True))).astype(bf16)
            probs[pl.ds(pl.multiple_of((w * 4 + p) * two, two), two), :] = rounded
            mixed[at, pl.ds(128 * p, 128)] = joined(dot(rounded, v))
        return carry

    lax.fori_loop(0, 4, window, 0)


def backward_kernel(place, *refs):
    pieces, tables, (o_ref, normed, qkv, probs, mixed, gact, own, other, ctw, gm, acc) = (
        refs[:4], refs[4:8], refs[8:],
    )
    ctw[...] = gathered(pieces, tables).astype(bf16)
    gm[...] = dot(ctw[...], o_ref[...], NT).astype(bf16)
    two = 2 * SPAN
    pick = pairs_mask()
    factor = 1.0 / math.sqrt(D // HEADS)

    def window(w, carry):
        at = pl.ds(pl.multiple_of(w * SPAN, SPAN), SPAN)
        for p in range(HEADS // 2):
            cols = pl.ds(128 * p, 128)
            q2 = doubled(qkv[at, cols], pick)
            g2 = doubled(gm[at, cols], pick)
            k = qkv[at, pl.ds(D + 128 * p, 128)]
            v = qkv[at, pl.ds(2 * D + 128 * p, 128)]
            rounded = probs[pl.ds(pl.multiple_of((w * 4 + p) * two, two), two), :]
            gact[at, pl.ds(2 * D + 128 * p, 128)] = dot(rounded, g2, TN).astype(bf16)
            dp = dot(g2, v, NT)
            pr = rounded.astype(f32)
            inner = jnp.sum(dp * pr, axis=-1, keepdims=True)
            ds = (pr * (dp - inner) * factor).astype(bf16)
            gact[at, cols] = joined(dot(ds, k))
            gact[at, pl.ds(D + 128 * p, 128)] = dot(ds, q2, TN).astype(bf16)
        return carry

    lax.fori_loop(0, 4, window, 0)

    acc[:, : 3 * D] = dot(normed[...], gact[...], TN)
    acc[:, 3 * D :] = dot(mixed[...], ctw[...], TN)
    y, x, c = place[1], place[2], place[3]

    def fill(out, core):
        d1 = jnp.where(core == 0, y, x)
        d2 = jnp.where(core == 0, x, y)
        for s1 in range(4):
            for s2 in range(4):
                r = core * 256 + lax.rem(d1 + s1, 4) * 64 + lax.rem(d2 + s2, 4) * 16
                rows = acc[pl.ds(pl.multiple_of(r, 16), 16), :]
                out[pl.ds((s1 * 4 + s2) * 16, 16), :] = rows.astype(bf16)

    fill(own, c)
    fill(other, 1 - c)


def back_kernel(mixed, gact, w_ref, o_ref, p_lat, p_lon, p_diag, both, to_lat, to_lon, to_diag):
    both[:, :D] = dot(mixed[...], o_ref[...]).astype(bf16)
    both[:, D:] = dot(gact[...], w_ref[...], NT).astype(bf16)
    to_lat[...] = dot(p_lat[...], both[...], TN).astype(bf16)
    to_lon[...] = dot(p_lon[...], both[...], TN).astype(bf16)
    to_diag[...] = dot(p_diag[...], both[...], TN).astype(bf16)


def finish_kernel(
    f_loc, c_loc, both, r_lat, r_lon, r_diag, p_loc, s_lat, s_lon, s_diag, gain, out, grad
):
    grid = (
        dot(p_loc[...], both[...], TN)
        + dot(s_lat[...], r_lat[...])
        + dot(s_lon[...], r_lon[...])
        + dot(s_diag[...], r_diag[...])
    )
    x = f_loc[...].astype(f32)
    out[...] = (x + grid[:, :D]).astype(bf16)
    xhat, rstd = normalise(x)
    g = grid[:, D:] * gain[...]
    first = jnp.mean(g, axis=-1, keepdims=True)
    second = jnp.mean(g * xhat, axis=-1, keepdims=True)
    grad[...] = (c_loc[...].astype(f32) + rstd * (g - first - xhat * second)).astype(bf16)


def weights_kernel(side, place, *refs):
    pieces, refs = refs[:4], refs[4:]
    if side == 0:
        w_ref, g_qkv, g_out, g_total, buf_q, buf_o, sem = refs
    else:
        w_ref, before, gain, _, _, g_qkv, g_out, g_total, buf_q, buf_o, sem = refs
    y, x, c = place[1], place[2], place[3]
    core = c if side == 0 else 1 - c
    d1 = jnp.where(core == 0, y, x)
    d2 = jnp.where(core == 0, x, y)
    bands = [pl.multiple_of(core * 256 + lax.rem(d1 + i, 4) * 64, 64) for i in range(4)]
    copies = []
    for i in range(4):
        for s2 in range(4):
            at = pl.ds(pl.multiple_of(lax.rem(d2 + s2, 4) * 16, 16), 16)
            block = pieces[i][pl.ds(s2 * 16, 16), :].astype(f32)
            buf_q[i, at, :] = block[:, : 3 * D]
            buf_o[i, at, :] = block[:, 3 * D :]
        for k, (src, dst) in enumerate(((buf_q, g_qkv), (buf_o, g_out))):
            copy = pltpu.make_async_copy(src.at[i], dst.at[pl.ds(bands[i], 64)], sem.at[i, k])
            copy.start()
            copies.append(copy)
    total = jnp.zeros((1, D), f32) if side == 0 else before[...]
    lane = lax.broadcasted_iota(jnp.int32, (64, D), 1)
    local = lax.broadcasted_iota(jnp.int32, (64, D), 0)
    for i in range(4):
        w = w_ref[pl.ds(bands[i], 64), :].astype(f32)
        sums = jnp.sum(buf_q[i] * w, axis=1, keepdims=True)
        spread = jnp.where(lane == local + bands[i], sums, 0.0)
        total = total + jnp.sum(spread, axis=0, keepdims=True)
    g_total[...] = total if side == 0 else total / gain[...]
    for copy in copies:
        copy.wait()


def to_weights(side, place, pieces, qkv_weight, *more):
    inside = pl.BlockSpec(memory_space=pltpu.VMEM)
    anywhere = pl.BlockSpec(memory_space=pl.ANY)
    extra = [] if side == 0 else [inside, inside, anywhere, anywhere]
    return pl.pallas_call(
        functools.partial(weights_kernel, side),
        out_shape=[shape(D, 3 * D, dtype=f32), shape(D, D, dtype=f32), shape(1, D, dtype=f32)],
        in_specs=spec(5, True) + extra,
        out_specs=[anywhere, anywhere, inside],
        scratch_shapes=[
            pltpu.VMEM((4, 64, 3 * D), f32),
            pltpu.VMEM((4, 64, D), f32),
            pltpu.SemaphoreType.DMA((4, 2)),
        ],
        input_output_aliases={} if side == 0 else {8: 0, 9: 1},
        compiler_params=params(),
        cost_estimate=cost(10**7, 4 * 10**6),
        name="weights" + str(side),
    )(place, *vms(*pieces), vm(qkv_weight), *more)


def params():
    return pltpu.CompilerParams(vmem_limit_bytes=VMEM)


def vm(x):
    return pltpu.with_memory_space_constraint(x, pltpu.VMEM)


def vms(*xs):
    return [vm(x) for x in xs]


def vshape(*dims, dtype=bf16):
    return pltpu.VMEM(dims, dtype)


def spec(count, scalar=False):
    whole = [pl.BlockSpec(memory_space=pltpu.VMEM)] * count
    return ([pl.BlockSpec(memory_space=pltpu.SMEM)] if scalar else []) + whole


def shape(*dims, dtype=bf16):
    return jax.ShapeDtypeStruct(dims, dtype)


def cost(flops, moved):
    return pl.CostEstimate(flops=flops, bytes_accessed=moved, transcendentals=0)


def to_forward(place, pieces, tables, gain_row, qkv_weight):
    return pl.pallas_call(
        forward_kernel,
        out_shape=[
            vshape(TOK, D), vshape(TOK, 3 * D), vshape(32 * SPAN, SPAN), vshape(TOK, D),
        ],
        in_specs=spec(10, True),
        out_specs=spec(4),
        compiler_params=params(),
        cost_estimate=cost(3 * 10**9, 10**7),
        name="forward",
    )(place, *vms(*pieces), *tables, gain_row, vm(qkv_weight))


def to_backward(place, pieces, tables, out_weight, *kept):
    return pl.pallas_call(
        backward_kernel,
        out_shape=[vshape(TOK, 3 * D), vshape(256, 4 * D), vshape(256, 4 * D)],
        in_specs=spec(13, True),
        out_specs=spec(3),
        scratch_shapes=[
            pltpu.VMEM((TOK, D), bf16),
            pltpu.VMEM((TOK, D), bf16),
            pltpu.VMEM((D, 4 * D), f32),
        ],
        compiler_params=params(),
        cost_estimate=cost(5 * 10**9, 10**7),
        name="backward",
    )(place, *vms(*pieces), *tables, vm(out_weight), *vms(*kept))


def to_back(mixed, gact, qkv_weight, out_weight, *tables):
    return pl.pallas_call(
        back_kernel,
        out_shape=[vshape(TOK, 2 * D), vshape(216, 2 * D), vshape(72, 2 * D), vshape(72, 2 * D)],
        in_specs=spec(7),
        out_specs=spec(4),
        compiler_params=params(),
        cost_estimate=cost(2 * 10**9, 5 * 10**6),
        name="back",
    )(*vms(mixed, gact, qkv_weight, out_weight, *tables))


def to_finish(*args):
    return pl.pallas_call(
        finish_kernel,
        out_shape=[shape(TOK, D), shape(TOK, D)],
        in_specs=spec(11),
        out_specs=spec(2),
        compiler_params=params(),
        cost_estimate=cost(2 * 10**9, 8 * 10**6),
        name="finish",
    )(*vms(*args))


def add(*xs):
    total = xs[0].astype(f32)
    for x in xs[1:]:
        total = total + x.astype(f32)
    return total.astype(bf16)


def tied(x):
    return lax.optimization_barrier(x)


def halo(field, select):
    lat, lon, diag = pl.pallas_call(
        pack_kernel,
        out_shape=[vshape(216, D), vshape(72, D), vshape(72, D)],
        in_specs=spec(2),
        out_specs=spec(3),
        compiler_params=params(),
        cost_estimate=cost(2 * 10**8, 10**6),
        name="pack",
    )(field, select)
    return (
        lax.ppermute(lat, BOTH, shifted(-1, 0)),
        lax.ppermute(lon, BOTH, shifted(0, -1)),
        lax.ppermute(diag, BOTH, shifted(-1, -1)),
    )


def on_device(fields, cotangent, layer_norm_gain, qkv_weight, out_weight):
    a, b = lax.axis_index("lat"), lax.axis_index("lon")
    place = jnp.stack(
        [
            (a == 7).astype(jnp.int32),
            (a // 2).astype(jnp.int32),
            ((a % 2) * 2 + b // 16).astype(jnp.int32),
            (b % 2).astype(jnp.int32),
        ]
    )
    gain_row = layer_norm_gain.reshape(1, D)
    p_loc, p_lat, p_lon, p_diag = [jnp.asarray(t, bf16) for t in gather_tables()]
    s_lat, s_lon, s_diag = [jnp.asarray(t, bf16) for t in scatter_tables()]
    f_loc, c_loc = fields.reshape(TOK, D), cotangent.reshape(TOK, D)
    select = jnp.asarray(np.concatenate(scatter_tables(), axis=1).T, bf16)
    f_halo = halo(f_loc, select)
    c_halo = halo(c_loc, select)

    tables = vms(p_loc, p_lat, p_lon, p_diag)
    normed, qkv, probs, mixed = to_forward(place, (f_loc, *f_halo), tables, gain_row, qkv_weight)
    gact, own, other = to_backward(
        place, (c_loc, *c_halo), tables, out_weight, normed, qkv, probs, mixed
    )

    there = send(other, to_sibling)
    part = [add(own[64 * k : 64 * k + 64], there[64 * k : 64 * k + 64]) for k in range(4)]
    mixed, gact, part = tied((mixed, gact, part))
    both, to_lat, to_lon, to_diag = to_back(mixed, gact, qkv_weight, out_weight, *tables[1:])
    recv = [send(part[k], first_axis(k)) for k in (1, 2, 3)]
    recv, to_lat = tied((recv, to_lat))
    part = add(part[0], *recv)
    part, to_lat, to_lon, to_diag = tied((part, to_lat, to_lon, to_diag))
    part = add(part[:16], *[send(part[16 * k : 16 * k + 16], second_axis(k)) for k in (1, 2, 3)])
    r_lat = lax.ppermute(to_lat, BOTH, shifted(1, 0))
    r_lon = lax.ppermute(to_lon, BOTH, shifted(0, 1))
    r_diag = lax.ppermute(to_diag, BOTH, shifted(1, 1))
    recv = send(part, flip_z(1))
    recv, r_lon = tied((recv, r_lon))
    part = add(part, recv)
    recv = send(part, flip_z(2))
    recv, r_diag = tied((recv, r_diag))
    part = add(part, recv)
    part = add(part, send(part, flip_z(6)))

    block = jnp.concatenate([part] + [send(part, second_axis(4 - s)) for s in (1, 2, 3)], axis=0)
    mine = [send(block, first_axis(4 - s)) for s in (1, 2, 3)]
    out, grad = to_finish(
        f_loc, c_loc, both, r_lat, r_lon, r_diag, tables[0], s_lat, s_lon, s_diag, gain_row
    )
    mine, out = tied((mine, out))
    mine = [block] + mine
    sibling = [send(m, to_sibling) for m in mine]
    g_qkv, g_out, total = to_weights(0, place, mine, qkv_weight)
    g_qkv, g_out, g_gain = to_weights(
        1, place, sibling, qkv_weight, total, gain_row, g_qkv, g_out
    )

    grid = (LEV, ROWS, COLS, D)
    return out.reshape(grid), grad.reshape(grid), g_qkv, g_out, g_gain.reshape(D)


def solution(mesh):
    return jax.shard_map(
        on_device,
        mesh=mesh,
        in_specs=(P(None, "lat", "lon", None), P(None, "lat", "lon", None), P(), P(), P()),
        out_specs=(P(None, "lat", "lon", None), P(None, "lat", "lon", None), P(), P(), P()),
        check_vma=False,
    )
```

```python
import functools
import math

import jax
import jax.numpy as jnp
import numpy as np
from jax import lax
from jax.experimental import pallas as pl
from jax.experimental.pallas import tpu as pltpu
from jax.sharding import PartitionSpec as P

HEADS = 8
LEV, ROWS, COLS = 4, 6, 24
WL, WR, WC = 2, 6, 12
D = 512
SPAN = WL * WR * WC
TOK = LEV * ROWS * COLS
BOTH = ("lat", "lon")
f32 = jnp.float32
bf16 = jnp.bfloat16
VMEM = 24 * 1024 * 1024


def index_of(y, x, z, c):
    return (y * 2 + x // 2) * 32 + (x % 2) * 16 + z * 2 + c


def place_of(i):
    return i // 64, ((i // 32) % 2) * 2 + (i // 16) % 2, (i // 2) % 8, i % 2


def route(step):
    return [(i, index_of(*step(*place_of(i)))) for i in range(256)]


def to_sibling(y, x, z, c):
    return y, x, z, 1 - c


def first_axis(k):
    return lambda y, x, z, c: ((y + k) % 4, x, z, c) if c == 0 else (y, (x + k) % 4, z, c)


MASKS = (0, 1, 3, 2)


def second_axis(k):
    return lambda y, x, z, c: (y, x ^ k, z, c) if c == 0 else (y ^ k, x, z, c)


def flip_z(k):
    return lambda y, x, z, c: (y, x, z ^ k, c)


def send(x, step):
    return lax.ppermute(x, BOTH, route(step))


def shifted(dlat, dlon):
    def pairs():
        out = []
        for i in range(256):
            a, b = i // 32, i % 32
            out.append((i, ((a + dlat) % 8) * 32 + (b + dlon) % 32))
        return out

    return pairs()


LAT, LON, HALO = 224, 80, 384


def gather_tables():
    local = np.zeros((TOK, TOK), np.float32)
    halo = np.zeros((TOK, HALO), np.float32)
    for lr in range(LEV):
        for rr in range(ROWS):
            for cr in range(COLS):
                w = (lr // WL) * (COLS // WC) + cr // WC
                t = w * SPAN + (lr % WL) * WR * WC + rr * WC + cr % WC
                lo, r, c = (lr + 1) % LEV, rr + 3, cr + 6
                if r < ROWS and c < COLS:
                    local[t, lo * ROWS * COLS + r * COLS + c] = 1
                elif c < COLS:
                    halo[t, lo * 54 + (r - ROWS) * 18 + c - 6] = 1
                elif r < ROWS:
                    halo[t, LAT + lo * 18 + (r - 3) * 6 + c - COLS] = 1
                else:
                    halo[t, LAT + LON + lo * 18 + (r - ROWS) * 6 + c - COLS] = 1
    return local, halo


def select_table():
    select = np.zeros((HALO, TOK), np.float32)
    for lv in range(LEV):
        for r in range(ROWS):
            for c in range(COLS):
                t = lv * ROWS * COLS + r * COLS + c
                if r < 3 and c >= 6:
                    select[lv * 54 + r * 18 + c - 6, t] = 1
                elif r >= 3 and c < 6:
                    select[LAT + lv * 18 + (r - 3) * 6 + c, t] = 1
                elif r < 3:
                    select[LAT + LON + lv * 18 + r * 6 + c, t] = 1
    return select


def dot(a, b, dims=((1,), (0,))):
    return lax.dot_general(a, b, (dims, ((), ())), preferred_element_type=f32)


NT = ((1,), (1,))
TN = ((0,), (0,))


def normalise(x):
    centred = x - jnp.mean(x, axis=-1, keepdims=True)
    rstd = lax.rsqrt(jnp.mean(centred * centred, axis=-1, keepdims=True) + 1e-5)
    return centred * rstd, rstd


def split(rows, lat, lon, diag):
    lat[...] = rows[:LAT].astype(bf16)
    lon[...] = rows[LAT : LAT + LON].astype(bf16)
    diag[...] = rows[LAT + LON :].astype(bf16)


def pack_kernel(f_hbm, c_hbm, s_hbm, f_vm, c_vm, s_vm, *refs):
    f_parts, c_parts, sem = refs[:3], refs[3:6], refs[6]
    pairs = ((s_hbm, s_vm), (f_hbm, f_vm), (c_hbm, c_vm))
    copies = [pltpu.make_async_copy(a, b, sem.at[i]) for i, (a, b) in enumerate(pairs)]
    for copy in copies:
        copy.start()
    copies[0].wait()
    copies[1].wait()
    split(dot(s_vm[...], f_vm[...]), *f_parts)
    copies[2].wait()
    split(dot(s_vm[...], c_vm[...]), *c_parts)


def load_kernel(f_vm, c_vm, *refs):
    sources, targets, (fw, cw, sem) = refs[:5], refs[5:10], refs[10:]
    copies = [
        pltpu.make_async_copy(a, b, sem.at[i]) for i, (a, b) in enumerate(zip(sources, targets))
    ]
    for copy in copies:
        copy.start()
    copies[0].wait()
    local = targets[0]
    fw[...] = dot(local[...], f_vm[...]).astype(bf16)
    cw[...] = dot(local[...], c_vm[...]).astype(bf16)
    for copy in copies[1:]:
        copy.wait()


GROUP = 4
WIDE = GROUP * (D // HEADS)


def group_mask(value=1.0):
    row = lax.broadcasted_iota(jnp.int32, (GROUP * SPAN, WIDE), 0)
    lane = lax.broadcasted_iota(jnp.int32, (GROUP * SPAN, WIDE), 1)
    first = lane // (D // HEADS) * SPAN
    return jnp.where((row >= first) & (row < first + SPAN), value, 0.0).astype(bf16)


def joined(r, factor=1.0):
    lane = lax.broadcasted_iota(jnp.int32, (SPAN, WIDE), 1)
    out = r[:SPAN]
    for h in range(1, GROUP):
        out = jnp.where(lane >= h * (D // HEADS), r[h * SPAN : (h + 1) * SPAN], out)
    return (out * factor).astype(bf16)


def repeated(x, pick):
    return jnp.concatenate([x] * GROUP, axis=0) * pick


def windows(part, table, lat, lon, diag):
    rows = jnp.concatenate([lat[...], lon[...], diag[...]], axis=0)
    return part[...].astype(f32) + dot(table[...], rows)


def forward_kernel(place, *refs):
    gain, w_ref, normed, qkv, probs, mixed = refs[5:]
    xhat, _ = normalise(windows(*refs[:5]))
    normed[...] = (xhat * gain[...]).astype(bf16)
    qkv[...] = dot(normed[...], w_ref[...]).astype(bf16)

    last_lat = place[0]
    long = 2 * SPAN
    low = lax.broadcasted_iota(jnp.int32, (SPAN, 128), 1) < 64
    row = lax.broadcasted_iota(jnp.int32, (long, 128), 0)
    lane = lax.broadcasted_iota(jnp.int32, (long, 128), 1)
    pick = jnp.where((row < SPAN) == (lane < 64), 1.0 / math.sqrt(D // HEADS), 0.0).astype(bf16)

    def lev_of(t):
        return (t >= SPAN // 2).astype(jnp.int32)

    def half_of(t):
        return (t - SPAN // 2 * lev_of(t) >= SPAN // 4).astype(jnp.int32)

    tq = lax.rem(lax.broadcasted_iota(jnp.int32, (SPAN, long), 1), SPAN)
    tk = lax.broadcasted_iota(jnp.int32, (SPAN, long), 0)
    lev_diff = jnp.abs(lev_of(tq) - lev_of(tk))
    half_diff = jnp.abs(half_of(tq) - half_of(tk)) * last_lat

    kinds = (half_diff == 0, (lev_diff + half_diff) == 0)
    for w in range(4):
        at = pl.ds(w * SPAN, SPAN)
        same = kinds[w // 2]
        for p in range(HEADS // 2):
            q_all = jnp.concatenate([qkv[at, pl.ds(128 * p, 128)]] * 2, axis=0) * pick
            k = qkv[at, pl.ds(D + 128 * p, 128)]
            v = qkv[at, pl.ds(2 * D + 128 * p, 128)]
            s = jnp.where(same, dot(k, q_all, NT), -1000000000.0)
            e = jnp.exp(s - jnp.max(s, axis=0, keepdims=True))
            rounded = (e * (1.0 / jnp.sum(e, axis=0, keepdims=True))).astype(bf16)
            probs[pl.ds((w * 2 + p // 2) * SPAN, SPAN), pl.ds(p % 2 * 2 * SPAN, 2 * SPAN)] = rounded
            r = dot(rounded, v, TN)
            mixed[at, pl.ds(128 * p, 128)] = jnp.where(low, r[:SPAN], r[SPAN:]).astype(bf16)


def backward_kernel(place, *refs):
    o_ref, normed, qkv, probs, mixed, gact, own, other, ctw, gm, acc = refs[5:]
    ctw[...] = windows(*refs[:5]).astype(bf16)
    gm[...] = dot(ctw[...], o_ref[...], NT).astype(bf16)
    long = GROUP * SPAN
    pick = group_mask()
    factor = 1.0 / math.sqrt(D // HEADS)
    scaled = group_mask(factor)

    def window(w, carry):
        at = pl.ds(pl.multiple_of(w * SPAN, SPAN), SPAN)
        for p in range(HEADS // GROUP):
            cols = pl.ds(WIDE * p, WIDE)
            q_all = repeated(qkv[at, cols], scaled)
            g_all = repeated(gm[at, cols], pick)
            k = qkv[at, pl.ds(D + WIDE * p, WIDE)]
            v = qkv[at, pl.ds(2 * D + WIDE * p, WIDE)]
            rounded = probs[pl.ds(pl.multiple_of((w * 2 + p) * SPAN, SPAN), SPAN), :]
            gact[at, pl.ds(2 * D + WIDE * p, WIDE)] = dot(rounded, g_all).astype(bf16)
            dp = dot(v, g_all, NT)
            pr = rounded.astype(f32)
            inner = jnp.sum(dp * pr, axis=0, keepdims=True)
            ds = (pr * (dp - inner)).astype(bf16)
            gact[at, cols] = joined(dot(ds, k, TN), factor)
            gact[at, pl.ds(D + WIDE * p, WIDE)] = dot(ds, q_all).astype(bf16)
        return carry

    lax.fori_loop(0, 4, window, 0, unroll=True)

    acc[:, : 3 * D] = dot(normed[...], gact[...], TN)
    acc[:, 3 * D :] = dot(mixed[...], ctw[...], TN)
    y, x, c = place[1], place[2], place[3]

    def fill(out, core):
        d1 = jnp.where(core == 0, y, x)
        d2 = jnp.where(core == 0, x, y)
        for s1 in range(4):
            for s2 in range(4):
                r = core * 256 + lax.rem(d1 + s1, 4) * 64 + (d2 ^ MASKS[s2]) * 16
                rows = acc[pl.ds(pl.multiple_of(r, 16), 16), :]
                out[pl.ds((s1 * 4 + s2) * 16, 16), :] = rows.astype(bf16)

    fill(own, c)
    fill(other, 1 - c)


def back_kernel(mixed, gact, w_ref, o_ref, p_halo, both, to_lat, to_lon, to_diag):
    both[:, :D] = dot(mixed[...], o_ref[...]).astype(bf16)
    both[:, D:] = dot(gact[...], w_ref[...], NT).astype(bf16)
    split(dot(p_halo[...], both[...], TN), to_lat, to_lon, to_diag)


def finish_kernel(f_loc, c_loc, both, r_lat, r_lon, r_diag, p_loc, select, gain, out, grad):
    rows = jnp.concatenate([r_lat[...], r_lon[...], r_diag[...]], axis=0)
    grid = dot(p_loc[...], both[...], TN) + dot(select[...], rows, TN)
    x = f_loc[...].astype(f32)
    out[...] = (x + grid[:, :D]).astype(bf16)
    xhat, rstd = normalise(x)
    g = grid[:, D:] * gain[...]
    first = jnp.mean(g, axis=-1, keepdims=True)
    second = jnp.mean(g * xhat, axis=-1, keepdims=True)
    grad[...] = (c_loc[...].astype(f32) + rstd * (g - first - xhat * second)).astype(bf16)


def weights_kernel(side, place, *refs):
    pieces, refs = refs[:4], refs[4:]
    if side == 0:
        w_ref, g_qkv, g_out, g_total, buf_q, buf_o, sem = refs
    else:
        w_ref, before, gain, _, _, g_qkv, g_out, g_total, buf_q, buf_o, sem = refs
    y, x, c = place[1], place[2], place[3]
    core = c if side == 0 else 1 - c
    d1 = jnp.where(core == 0, y, x)
    d2 = jnp.where(core == 0, x, y)
    bands = [pl.multiple_of(core * 256 + lax.rem(d1 + i, 4) * 64, 64) for i in range(4)]
    copies = []
    for i in range(4):
        for s2 in range(4):
            at = pl.ds(pl.multiple_of((d2 ^ MASKS[s2]) * 16, 16), 16)
            block = pieces[i][pl.ds(s2 * 16, 16), :].astype(f32)
            buf_q[i, at, :] = block[:, : 3 * D]
            buf_o[i, at, :] = block[:, 3 * D :]
        for k, (src, dst) in enumerate(((buf_q, g_qkv), (buf_o, g_out))):
            copy = pltpu.make_async_copy(src.at[i], dst.at[pl.ds(bands[i], 64)], sem.at[i, k])
            copy.start()
            copies.append(copy)
    total = jnp.zeros((1, D), f32) if side == 0 else before[...]
    lane = lax.broadcasted_iota(jnp.int32, (64, D), 1)
    local = lax.broadcasted_iota(jnp.int32, (64, D), 0)
    for i in range(4):
        w = w_ref[pl.ds(bands[i], 64), :].astype(f32)
        sums = jnp.sum(buf_q[i] * w, axis=1, keepdims=True)
        spread = jnp.where(lane == local + bands[i], sums, 0.0)
        total = total + jnp.sum(spread, axis=0, keepdims=True)
    g_total[...] = total if side == 0 else total / gain[...]
    for copy in copies:
        copy.wait()


def to_weights(side, place, pieces, qkv_weight, *more):
    inside = pl.BlockSpec(memory_space=pltpu.VMEM)
    anywhere = pl.BlockSpec(memory_space=pl.ANY)
    extra = [] if side == 0 else [inside, inside, anywhere, anywhere]
    return pl.pallas_call(
        functools.partial(weights_kernel, side),
        out_shape=[shape(D, 3 * D, dtype=f32), shape(D, D, dtype=f32), shape(1, D, dtype=f32)],
        in_specs=spec(5, True) + extra,
        out_specs=[anywhere, anywhere, inside],
        scratch_shapes=[
            pltpu.VMEM((4, 64, 3 * D), f32),
            pltpu.VMEM((4, 64, D), f32),
            pltpu.SemaphoreType.DMA((4, 2)),
        ],
        input_output_aliases={} if side == 0 else {8: 0, 9: 1},
        compiler_params=params(),
        cost_estimate=cost(10**7, 4 * 10**6),
        name="weights" + str(side),
    )(place, *vms(*pieces), vm(qkv_weight), *more)


def params():
    return pltpu.CompilerParams(vmem_limit_bytes=VMEM)


def vm(x):
    return pltpu.with_memory_space_constraint(x, pltpu.VMEM)


def vms(*xs):
    return [vm(x) for x in xs]


def vshape(*dims, dtype=bf16):
    return pltpu.VMEM(dims, dtype)


def spec(count, scalar=False):
    whole = [pl.BlockSpec(memory_space=pltpu.VMEM)] * count
    return ([pl.BlockSpec(memory_space=pltpu.SMEM)] if scalar else []) + whole


def shape(*dims, dtype=bf16):
    return jax.ShapeDtypeStruct(dims, dtype)


def cost(flops, moved):
    return pl.CostEstimate(flops=flops, bytes_accessed=moved, transcendentals=0)


def halo_shapes(width):
    return [vshape(LAT, width), vshape(LON, width), vshape(HALO - LAT - LON, width)]


def to_pack(fields, cotangent, select):
    return pl.pallas_call(
        pack_kernel,
        out_shape=[vshape(TOK, D), vshape(TOK, D), vshape(HALO, TOK)] + halo_shapes(D) * 2,
        in_specs=[pl.BlockSpec(memory_space=pltpu.HBM)] * 3,
        out_specs=spec(9),
        scratch_shapes=[pltpu.SemaphoreType.DMA((3,))],
        compiler_params=params(),
        cost_estimate=cost(4 * 10**8, 2 * 10**6),
        name="pack",
    )(*[pltpu.with_memory_space_constraint(x, pltpu.HBM) for x in (fields, cotangent, select)])


def to_load(f_vm, c_vm, *sources):
    return pl.pallas_call(
        load_kernel,
        out_shape=[vshape(*x.shape, dtype=x.dtype) for x in sources]
        + [vshape(TOK, D), vshape(TOK, D)],
        in_specs=spec(2) + [pl.BlockSpec(memory_space=pltpu.HBM)] * 5,
        out_specs=spec(7),
        scratch_shapes=[pltpu.SemaphoreType.DMA((5,))],
        compiler_params=params(),
        cost_estimate=cost(8 * 10**8, 4 * 10**6),
        name="load",
    )(*vms(f_vm, c_vm), *[pltpu.with_memory_space_constraint(x, pltpu.HBM) for x in sources])


def to_forward(place, *args):
    return pl.pallas_call(
        forward_kernel,
        out_shape=[
            vshape(TOK, D), vshape(TOK, 3 * D), vshape(32 // GROUP * SPAN, GROUP * SPAN), vshape(TOK, D),
        ],
        in_specs=spec(7, True),
        out_specs=spec(4),
        compiler_params=params(),
        cost_estimate=cost(3 * 10**9, 10**7),
        name="forward",
    )(place, *vms(*args))


def to_backward(place, *args):
    return pl.pallas_call(
        backward_kernel,
        out_shape=[vshape(TOK, 3 * D), vshape(256, 4 * D), vshape(256, 4 * D)],
        in_specs=spec(10, True),
        out_specs=spec(3),
        scratch_shapes=[
            pltpu.VMEM((TOK, D), bf16),
            pltpu.VMEM((TOK, D), bf16),
            pltpu.VMEM((D, 4 * D), f32),
        ],
        compiler_params=params(),
        cost_estimate=cost(5 * 10**9, 10**7),
        name="backward",
    )(place, *vms(*args))


def to_back(*args):
    return pl.pallas_call(
        back_kernel,
        out_shape=[vshape(TOK, 2 * D)] + halo_shapes(2 * D),
        in_specs=spec(5),
        out_specs=spec(4),
        compiler_params=params(),
        cost_estimate=cost(2 * 10**9, 5 * 10**6),
        name="back",
    )(*vms(*args))


def to_finish(*args):
    return pl.pallas_call(
        finish_kernel,
        out_shape=[shape(TOK, D), shape(TOK, D)],
        in_specs=spec(9),
        out_specs=spec(2),
        compiler_params=params(),
        cost_estimate=cost(2 * 10**9, 8 * 10**6),
        name="finish",
    )(*vms(*args))


def add(*xs):
    total = xs[0].astype(f32)
    for x in xs[1:]:
        total = total + x.astype(f32)
    return total.astype(bf16)


def tied(x):
    return lax.optimization_barrier(x)


def halo_in(lat, lon, diag):
    return (
        lax.ppermute(lat, BOTH, shifted(-1, 0)),
        lax.ppermute(lon, BOTH, shifted(0, -1)),
        lax.ppermute(diag, BOTH, shifted(-1, -1)),
    )


def on_device(fields, cotangent, layer_norm_gain, qkv_weight, out_weight):
    a, b = lax.axis_index("lat"), lax.axis_index("lon")
    place = jnp.stack(
        [
            (a == 7).astype(jnp.int32),
            (a // 2).astype(jnp.int32),
            ((a % 2) * 2 + b // 16).astype(jnp.int32),
            (b % 2).astype(jnp.int32),
        ]
    )
    tables = [jnp.asarray(t, bf16) for t in gather_tables()]
    select = jnp.asarray(select_table(), bf16)
    f_vm, c_vm, select, *parts = to_pack(
        fields.reshape(TOK, D), cotangent.reshape(TOK, D), select
    )
    f_halo = halo_in(*parts[:3])
    c_halo = halo_in(*parts[3:])
    p_loc, p_halo, w, o, gain, fw, cw = to_load(
        f_vm, c_vm, *tables, qkv_weight, out_weight, layer_norm_gain.reshape(1, D)
    )
    normed, qkv, probs, mixed = to_forward(place, fw, p_halo, *f_halo, gain, w)
    gact, own, other = to_backward(
        place, cw, p_halo, *c_halo, o, normed, qkv, probs, mixed
    )

    there = send(other, to_sibling)
    part = [add(own[64 * k : 64 * k + 64], there[64 * k : 64 * k + 64]) for k in range(4)]
    mixed, gact, part = tied((mixed, gact, part))
    both, to_lat, to_lon, to_diag = to_back(mixed, gact, w, o, p_halo)
    recv = [send(part[k], first_axis(k)) for k in (1, 2, 3)]
    recv, to_lat = tied((recv, to_lat))
    part = add(part[0], *recv)
    part, to_lat, to_lon, to_diag = tied((part, to_lat, to_lon, to_diag))
    part = add(part[:32], send(part[32:], second_axis(3)))
    part = add(part[:16], send(part[16:], second_axis(1)))
    r_lat = lax.ppermute(to_lat, BOTH, shifted(1, 0))
    r_lon = lax.ppermute(to_lon, BOTH, shifted(0, 1))
    r_diag = lax.ppermute(to_diag, BOTH, shifted(1, 1))
    recv = send(part, flip_z(1))
    recv, r_lon = tied((recv, r_lon))
    part = add(part, recv)
    recv = send(part, flip_z(2))
    recv, r_diag = tied((recv, r_diag))
    part = add(part, recv)
    part = add(part, send(part, flip_z(6)))

    block = jnp.concatenate([part, send(part, second_axis(1))], axis=0)
    block = jnp.concatenate([block, send(block, second_axis(3))], axis=0)
    mine = [send(block, first_axis(4 - s)) for s in (1, 2, 3)]
    out, grad = to_finish(f_vm, c_vm, both, r_lat, r_lon, r_diag, p_loc, select, gain)
    mine, out = tied((mine, out))
    mine = [block] + mine
    sibling = [send(m, to_sibling) for m in mine]
    g_qkv, g_out, total = to_weights(0, place, mine, w)
    g_qkv, g_out, g_gain = to_weights(1, place, sibling, w, total, gain, g_qkv, g_out)

    grid = (LEV, ROWS, COLS, D)
    return out.reshape(grid), grad.reshape(grid), g_qkv, g_out, g_gain.reshape(D)


def solution(mesh):
    return jax.shard_map(
        on_device,
        mesh=mesh,
        in_specs=(P(None, "lat", "lon", None), P(None, "lat", "lon", None), P(), P(), P()),
        out_specs=(P(None, "lat", "lon", None), P(None, "lat", "lon", None), P(), P(), P()),
        check_vma=False,
    )
```

```python
import functools
import math

import jax
import jax.numpy as jnp
import numpy as np
from jax import lax
from jax.experimental import pallas as pl
from jax.experimental.pallas import tpu as pltpu
from jax.sharding import PartitionSpec as P

HEADS = 8
LEV, ROWS, COLS = 4, 6, 24
WL, WR, WC = 2, 6, 12
D = 512
SPAN = WL * WR * WC
TOK = LEV * ROWS * COLS
BOTH = ("lat", "lon")
f32 = jnp.float32
bf16 = jnp.bfloat16
VMEM = 24 * 1024 * 1024


def index_of(y, x, z, c):
    return (y * 2 + x // 2) * 32 + (x % 2) * 16 + z * 2 + c


def place_of(i):
    return i // 64, ((i // 32) % 2) * 2 + (i // 16) % 2, (i // 2) % 8, i % 2


def route(step):
    return [(i, index_of(*step(*place_of(i)))) for i in range(256)]


def to_sibling(y, x, z, c):
    return y, x, z, 1 - c


def first_axis(k):
    return lambda y, x, z, c: ((y + k) % 4, x, z, c) if c == 0 else (y, (x + k) % 4, z, c)


def second_axis(k):
    return lambda y, x, z, c: (y, (x + k) % 4, z, c) if c == 0 else ((y + k) % 4, x, z, c)


def flip_z(k):
    return lambda y, x, z, c: (y, x, z ^ k, c)


def send(x, step):
    return lax.ppermute(x, BOTH, route(step))


def shifted(dlat, dlon):
    def pairs():
        out = []
        for i in range(256):
            a, b = i // 32, i % 32
            out.append((i, ((a + dlat) % 8) * 32 + (b + dlon) % 32))
        return out

    return pairs()


LAT, LON, HALO = 224, 80, 384


def gather_tables():
    local = np.zeros((TOK, TOK), np.float32)
    halo = np.zeros((TOK, HALO), np.float32)
    for lr in range(LEV):
        for rr in range(ROWS):
            for cr in range(COLS):
                w = (lr // WL) * (COLS // WC) + cr // WC
                t = w * SPAN + (lr % WL) * WR * WC + rr * WC + cr % WC
                lo, r, c = (lr + 1) % LEV, rr + 3, cr + 6
                if r < ROWS and c < COLS:
                    local[t, lo * ROWS * COLS + r * COLS + c] = 1
                elif c < COLS:
                    halo[t, lo * 54 + (r - ROWS) * 18 + c - 6] = 1
                elif r < ROWS:
                    halo[t, LAT + lo * 18 + (r - 3) * 6 + c - COLS] = 1
                else:
                    halo[t, LAT + LON + lo * 18 + (r - ROWS) * 6 + c - COLS] = 1
    return local, halo


def select_table():
    select = np.zeros((HALO, TOK), np.float32)
    for lv in range(LEV):
        for r in range(ROWS):
            for c in range(COLS):
                t = lv * ROWS * COLS + r * COLS + c
                if r < 3 and c >= 6:
                    select[lv * 54 + r * 18 + c - 6, t] = 1
                elif r >= 3 and c < 6:
                    select[LAT + lv * 18 + (r - 3) * 6 + c, t] = 1
                elif r < 3:
                    select[LAT + LON + lv * 18 + r * 6 + c, t] = 1
    return select


def dot(a, b, dims=((1,), (0,))):
    return lax.dot_general(a, b, (dims, ((), ())), preferred_element_type=f32)


NT = ((1,), (1,))
TN = ((0,), (0,))


def normalise(x):
    centred = x - jnp.mean(x, axis=-1, keepdims=True)
    rstd = lax.rsqrt(jnp.mean(centred * centred, axis=-1, keepdims=True) + 1e-5)
    return centred * rstd, rstd


def split(rows, lat, lon, diag):
    lat[...] = rows[:LAT].astype(bf16)
    lon[...] = rows[LAT : LAT + LON].astype(bf16)
    diag[...] = rows[LAT + LON :].astype(bf16)


def pack_kernel(f_hbm, c_hbm, s_hbm, f_vm, c_vm, s_vm, *refs):
    f_parts, c_parts, sem = refs[:3], refs[3:6], refs[6]
    pairs = ((s_hbm, s_vm), (f_hbm, f_vm), (c_hbm, c_vm))
    copies = [pltpu.make_async_copy(a, b, sem.at[i]) for i, (a, b) in enumerate(pairs)]
    for copy in copies:
        copy.start()
    copies[0].wait()
    copies[1].wait()
    split(dot(s_vm[...], f_vm[...]), *f_parts)
    copies[2].wait()
    split(dot(s_vm[...], c_vm[...]), *c_parts)


def load_kernel(f_vm, c_vm, *refs):
    sources, targets, (fw, cw, sem) = refs[:5], refs[5:10], refs[10:]
    copies = [
        pltpu.make_async_copy(a, b, sem.at[i]) for i, (a, b) in enumerate(zip(sources, targets))
    ]
    for copy in copies:
        copy.start()
    copies[0].wait()
    local = targets[0]
    fw[...] = dot(local[...], f_vm[...]).astype(bf16)
    cw[...] = dot(local[...], c_vm[...]).astype(bf16)
    for copy in copies[1:]:
        copy.wait()


GROUP = 4
WIDE = GROUP * (D // HEADS)


def group_mask(value=1.0):
    row = lax.broadcasted_iota(jnp.int32, (GROUP * SPAN, WIDE), 0)
    lane = lax.broadcasted_iota(jnp.int32, (GROUP * SPAN, WIDE), 1)
    first = lane // (D // HEADS) * SPAN
    return jnp.where((row >= first) & (row < first + SPAN), value, 0.0).astype(bf16)


def joined(r, factor=1.0):
    lane = lax.broadcasted_iota(jnp.int32, (SPAN, WIDE), 1)
    out = r[:SPAN]
    for h in range(1, GROUP):
        out = jnp.where(lane >= h * (D // HEADS), r[h * SPAN : (h + 1) * SPAN], out)
    return (out * factor).astype(bf16)


def repeated(x, pick):
    return jnp.concatenate([x] * GROUP, axis=0) * pick


def windows(part, table, lat, lon, diag):
    rows = jnp.concatenate([lat[...], lon[...], diag[...]], axis=0)
    return part[...].astype(f32) + dot(table[...], rows)


def forward_kernel(place, *refs):
    gain, w_ref, normed, qkv, probs, mixed = refs[5:]
    xhat, _ = normalise(windows(*refs[:5]))
    normed[...] = (xhat * gain[...]).astype(bf16)
    qkv[...] = dot(normed[...], w_ref[...]).astype(bf16)

    last_lat = place[0]
    long = 2 * SPAN
    low = lax.broadcasted_iota(jnp.int32, (SPAN, 128), 1) < 64
    row = lax.broadcasted_iota(jnp.int32, (long, 128), 0)
    lane = lax.broadcasted_iota(jnp.int32, (long, 128), 1)
    pick = jnp.where((row < SPAN) == (lane < 64), 1.0 / math.sqrt(D // HEADS), 0.0).astype(bf16)

    def lev_of(t):
        return (t >= SPAN // 2).astype(jnp.int32)

    def half_of(t):
        return (t - SPAN // 2 * lev_of(t) >= SPAN // 4).astype(jnp.int32)

    tq = lax.rem(lax.broadcasted_iota(jnp.int32, (SPAN, long), 1), SPAN)
    tk = lax.broadcasted_iota(jnp.int32, (SPAN, long), 0)
    lev_diff = jnp.abs(lev_of(tq) - lev_of(tk))
    half_diff = jnp.abs(half_of(tq) - half_of(tk)) * last_lat

    kinds = (half_diff == 0, (lev_diff + half_diff) == 0)
    for w in range(4):
        at = pl.ds(w * SPAN, SPAN)
        same = kinds[w // 2]
        for p in range(HEADS // 2):
            q_all = jnp.concatenate([qkv[at, pl.ds(128 * p, 128)]] * 2, axis=0) * pick
            k = qkv[at, pl.ds(D + 128 * p, 128)]
            v = qkv[at, pl.ds(2 * D + 128 * p, 128)]
            s = jnp.where(same, dot(k, q_all, NT), -1000000000.0)
            e = jnp.exp(s - jnp.max(s, axis=0, keepdims=True))
            rounded = (e * (1.0 / jnp.sum(e, axis=0, keepdims=True))).astype(bf16)
            probs[pl.ds((w * 2 + p // 2) * SPAN, SPAN), pl.ds(p % 2 * 2 * SPAN, 2 * SPAN)] = rounded
            r = dot(rounded, v, TN)
            mixed[at, pl.ds(128 * p, 128)] = jnp.where(low, r[:SPAN], r[SPAN:]).astype(bf16)


def backward_kernel(place, *refs):
    o_ref, normed, qkv, probs, mixed, gact, own, other, ctw, gm, acc = refs[5:]
    ctw[...] = windows(*refs[:5]).astype(bf16)
    gm[...] = dot(ctw[...], o_ref[...], NT).astype(bf16)
    long = GROUP * SPAN
    pick = group_mask()
    factor = 1.0 / math.sqrt(D // HEADS)
    scaled = group_mask(factor)

    def window(w, carry):
        at = pl.ds(pl.multiple_of(w * SPAN, SPAN), SPAN)
        for p in range(HEADS // GROUP):
            cols = pl.ds(WIDE * p, WIDE)
            q_all = repeated(qkv[at, cols], scaled)
            g_all = repeated(gm[at, cols], pick)
            k = qkv[at, pl.ds(D + WIDE * p, WIDE)]
            v = qkv[at, pl.ds(2 * D + WIDE * p, WIDE)]
            rounded = probs[pl.ds(pl.multiple_of((w * 2 + p) * SPAN, SPAN), SPAN), :]
            gact[at, pl.ds(2 * D + WIDE * p, WIDE)] = dot(rounded, g_all).astype(bf16)
            dp = dot(v, g_all, NT)
            pr = rounded.astype(f32)
            inner = jnp.sum(dp * pr, axis=0, keepdims=True)
            ds = (pr * (dp - inner)).astype(bf16)
            gact[at, cols] = joined(dot(ds, k, TN), factor)
            gact[at, pl.ds(D + WIDE * p, WIDE)] = dot(ds, q_all).astype(bf16)
        return carry

    lax.fori_loop(0, 4, window, 0, unroll=True)

    acc[:, : 3 * D] = dot(normed[...], gact[...], TN)
    acc[:, 3 * D :] = dot(mixed[...], ctw[...], TN)
    y, x, c = place[1], place[2], place[3]

    def fill(out, core):
        d1 = jnp.where(core == 0, y, x)
        d2 = jnp.where(core == 0, x, y)
        for s1 in range(4):
            for s2 in range(4):
                r = core * 256 + lax.rem(d1 + s1, 4) * 64 + lax.rem(d2 + s2, 4) * 16
                rows = acc[pl.ds(pl.multiple_of(r, 16), 16), :]
                out[pl.ds((s1 * 4 + s2) * 16, 16), :] = rows.astype(bf16)

    fill(own, c)
    fill(other, 1 - c)


def back_kernel(mixed, gact, w_ref, o_ref, p_halo, both, to_lat, to_lon, to_diag):
    both[:, :D] = dot(mixed[...], o_ref[...]).astype(bf16)
    both[:, D:] = dot(gact[...], w_ref[...], NT).astype(bf16)
    split(dot(p_halo[...], both[...], TN), to_lat, to_lon, to_diag)


def finish_kernel(f_loc, c_loc, both, r_lat, r_lon, r_diag, p_loc, select, gain, out, grad):
    rows = jnp.concatenate([r_lat[...], r_lon[...], r_diag[...]], axis=0)
    grid = dot(p_loc[...], both[...], TN) + dot(select[...], rows, TN)
    x = f_loc[...].astype(f32)
    out[...] = (x + grid[:, :D]).astype(bf16)
    xhat, rstd = normalise(x)
    g = grid[:, D:] * gain[...]
    first = jnp.mean(g, axis=-1, keepdims=True)
    second = jnp.mean(g * xhat, axis=-1, keepdims=True)
    grad[...] = (c_loc[...].astype(f32) + rstd * (g - first - xhat * second)).astype(bf16)


def weights_kernel(side, place, *refs):
    pieces, refs = refs[:4], refs[4:]
    if side == 0:
        w_ref, g_qkv, g_out, g_total, buf_q, buf_o, sem = refs
    else:
        w_ref, before, gain, _, _, g_qkv, g_out, g_total, buf_q, buf_o, sem = refs
    y, x, c = place[1], place[2], place[3]
    core = c if side == 0 else 1 - c
    d1 = jnp.where(core == 0, y, x)
    d2 = jnp.where(core == 0, x, y)
    bands = [pl.multiple_of(core * 256 + lax.rem(d1 + i, 4) * 64, 64) for i in range(4)]
    copies = []
    for i in range(4):
        for s2 in range(4):
            at = pl.ds(pl.multiple_of(lax.rem(d2 + s2, 4) * 16, 16), 16)
            block = pieces[i][pl.ds(s2 * 16, 16), :].astype(f32)
            buf_q[i, at, :] = block[:, : 3 * D]
            buf_o[i, at, :] = block[:, 3 * D :]
        for k, (src, dst) in enumerate(((buf_q, g_qkv), (buf_o, g_out))):
            copy = pltpu.make_async_copy(src.at[i], dst.at[pl.ds(bands[i], 64)], sem.at[i, k])
            copy.start()
            copies.append(copy)
    total = jnp.zeros((1, D), f32) if side == 0 else before[...]
    lane = lax.broadcasted_iota(jnp.int32, (64, D), 1)
    local = lax.broadcasted_iota(jnp.int32, (64, D), 0)
    for i in range(4):
        w = w_ref[pl.ds(bands[i], 64), :].astype(f32)
        sums = jnp.sum(buf_q[i] * w, axis=1, keepdims=True)
        spread = jnp.where(lane == local + bands[i], sums, 0.0)
        total = total + jnp.sum(spread, axis=0, keepdims=True)
    g_total[...] = total if side == 0 else total / gain[...]
    for copy in copies:
        copy.wait()


def to_weights(side, place, pieces, qkv_weight, *more):
    inside = pl.BlockSpec(memory_space=pltpu.VMEM)
    anywhere = pl.BlockSpec(memory_space=pl.ANY)
    extra = [] if side == 0 else [inside, inside, anywhere, anywhere]
    return pl.pallas_call(
        functools.partial(weights_kernel, side),
        out_shape=[
            shape(D, 3 * D, dtype=f32),
            shape(D, D, dtype=f32),
            (vshape if side == 0 else shape)(1, D, dtype=f32),
        ],
        in_specs=spec(5, True) + extra,
        out_specs=[anywhere, anywhere, inside],
        scratch_shapes=[
            pltpu.VMEM((4, 64, 3 * D), f32),
            pltpu.VMEM((4, 64, D), f32),
            pltpu.SemaphoreType.DMA((4, 2)),
        ],
        input_output_aliases={} if side == 0 else {8: 0, 9: 1},
        compiler_params=params(),
        cost_estimate=cost(10**7, 4 * 10**6),
        name="weights" + str(side),
    )(place, *vms(*pieces), vm(qkv_weight), *more)


def params():
    return pltpu.CompilerParams(vmem_limit_bytes=VMEM)


def vm(x):
    return pltpu.with_memory_space_constraint(x, pltpu.VMEM)


def vms(*xs):
    return [vm(x) for x in xs]


def vshape(*dims, dtype=bf16):
    return pltpu.VMEM(dims, dtype)


def spec(count, scalar=False):
    whole = [pl.BlockSpec(memory_space=pltpu.VMEM)] * count
    return ([pl.BlockSpec(memory_space=pltpu.SMEM)] if scalar else []) + whole


def shape(*dims, dtype=bf16):
    return jax.ShapeDtypeStruct(dims, dtype)


def cost(flops, moved):
    return pl.CostEstimate(flops=flops, bytes_accessed=moved, transcendentals=0)


def halo_shapes(width):
    return [vshape(LAT, width), vshape(LON, width), vshape(HALO - LAT - LON, width)]


def to_pack(fields, cotangent, select):
    return pl.pallas_call(
        pack_kernel,
        out_shape=[vshape(TOK, D), vshape(TOK, D), vshape(HALO, TOK)] + halo_shapes(D) * 2,
        in_specs=[pl.BlockSpec(memory_space=pltpu.HBM)] * 3,
        out_specs=spec(9),
        scratch_shapes=[pltpu.SemaphoreType.DMA((3,))],
        compiler_params=params(),
        cost_estimate=cost(4 * 10**8, 2 * 10**6),
        name="pack",
    )(*[pltpu.with_memory_space_constraint(x, pltpu.HBM) for x in (fields, cotangent, select)])


def to_load(f_vm, c_vm, *sources):
    return pl.pallas_call(
        load_kernel,
        out_shape=[vshape(*x.shape, dtype=x.dtype) for x in sources]
        + [vshape(TOK, D), vshape(TOK, D)],
        in_specs=spec(2) + [pl.BlockSpec(memory_space=pltpu.HBM)] * 5,
        out_specs=spec(7),
        scratch_shapes=[pltpu.SemaphoreType.DMA((5,))],
        compiler_params=params(),
        cost_estimate=cost(10**6, 10**4),
        name="load",
    )(*vms(f_vm, c_vm), *[pltpu.with_memory_space_constraint(x, pltpu.HBM) for x in sources])


def to_forward(place, *args):
    return pl.pallas_call(
        forward_kernel,
        out_shape=[
            vshape(TOK, D), vshape(TOK, 3 * D), vshape(32 // GROUP * SPAN, GROUP * SPAN), vshape(TOK, D),
        ],
        in_specs=spec(7, True),
        out_specs=spec(4),
        compiler_params=params(),
        cost_estimate=cost(10**6, 10**4),
        name="forward",
    )(place, *vms(*args))


def to_backward(place, *args):
    return pl.pallas_call(
        backward_kernel,
        out_shape=[vshape(TOK, 3 * D), vshape(256, 4 * D), vshape(256, 4 * D)],
        in_specs=spec(10, True),
        out_specs=spec(3),
        scratch_shapes=[
            pltpu.VMEM((TOK, D), bf16),
            pltpu.VMEM((TOK, D), bf16),
            pltpu.VMEM((D, 4 * D), f32),
        ],
        compiler_params=params(),
        cost_estimate=cost(5 * 10**9, 10**7),
        name="backward",
    )(place, *vms(*args))


def to_back(*args):
    return pl.pallas_call(
        back_kernel,
        out_shape=[vshape(TOK, 2 * D)] + halo_shapes(2 * D),
        in_specs=spec(5),
        out_specs=spec(4),
        compiler_params=params(),
        cost_estimate=cost(2 * 10**9, 5 * 10**6),
        name="back",
    )(*vms(*args))


def to_finish(*args):
    return pl.pallas_call(
        finish_kernel,
        out_shape=[shape(TOK, D), shape(TOK, D)],
        in_specs=spec(9),
        out_specs=spec(2),
        compiler_params=params(),
        cost_estimate=cost(2 * 10**9, 8 * 10**6),
        name="finish",
    )(*vms(*args))


def add(*xs):
    total = xs[0].astype(f32)
    for x in xs[1:]:
        total = total + x.astype(f32)
    return total.astype(bf16)


def tied(x):
    return lax.optimization_barrier(x)


def halo_in(lat, lon, diag):
    return (
        lax.ppermute(lat, BOTH, shifted(-1, 0)),
        lax.ppermute(lon, BOTH, shifted(0, -1)),
        lax.ppermute(diag, BOTH, shifted(-1, -1)),
    )


def on_device(fields, cotangent, layer_norm_gain, qkv_weight, out_weight):
    a, b = lax.axis_index("lat"), lax.axis_index("lon")
    place = jnp.stack(
        [
            (a == 7).astype(jnp.int32),
            (a // 2).astype(jnp.int32),
            ((a % 2) * 2 + b // 16).astype(jnp.int32),
            (b % 2).astype(jnp.int32),
        ]
    )
    tables = [jnp.asarray(t, bf16) for t in gather_tables()]
    select = jnp.asarray(select_table(), bf16)
    f_vm, c_vm, select, *parts = to_pack(
        fields.reshape(TOK, D), cotangent.reshape(TOK, D), select
    )
    f_halo = halo_in(*parts[:3])
    c_halo = halo_in(*parts[3:])
    p_loc, p_halo, w, o, gain, fw, cw = to_load(
        f_vm, c_vm, *tables, qkv_weight, out_weight, layer_norm_gain.reshape(1, D)
    )
    normed, qkv, probs, mixed = to_forward(place, fw, p_halo, *f_halo, gain, w)
    gact, own, other = to_backward(
        place, cw, p_halo, *c_halo, o, normed, qkv, probs, mixed
    )

    there = send(other, to_sibling)
    part = [add(own[64 * k : 64 * k + 64], there[64 * k : 64 * k + 64]) for k in range(4)]
    mixed, gact, part = tied((mixed, gact, part))
    both, to_lat, to_lon, to_diag = to_back(mixed, gact, w, o, p_halo)
    recv = [send(part[k], first_axis(k)) for k in (1, 2, 3)]
    recv, to_lat = tied((recv, to_lat))
    part = add(part[0], *recv)
    part, to_lat, to_lon, to_diag = tied((part, to_lat, to_lon, to_diag))
    part = add(part[:16], *[send(part[16 * k : 16 * k + 16], second_axis(k)) for k in (1, 2, 3)])
    r_lat = lax.ppermute(to_lat, BOTH, shifted(1, 0))
    r_lon = lax.ppermute(to_lon, BOTH, shifted(0, 1))
    r_diag = lax.ppermute(to_diag, BOTH, shifted(1, 1))
    recv = send(part, flip_z(1))
    recv, r_diag = tied((recv, r_diag))
    part = add(part, recv)
    recv = send(part, flip_z(2))
    recv, r_lon = tied((recv, r_lon))
    part = add(part, recv)
    recv = send(part, flip_z(6))
    recv, r_lat = tied((recv, r_lat))
    part = add(part, recv)

    block = jnp.concatenate([part] + [send(part, second_axis(4 - s)) for s in (1, 2, 3)], axis=0)
    mine = [send(block, first_axis(4 - s)) for s in (1, 2, 3)]
    out, grad = to_finish(f_vm, c_vm, both, r_lat, r_lon, r_diag, p_loc, select, gain)
    mine, out = tied((mine, out))
    mine = [block] + mine
    sibling = [send(m, to_sibling) for m in mine]
    g_qkv, g_out, total = to_weights(0, place, mine, w)
    g_qkv, g_out, g_gain = to_weights(1, place, sibling, w, vm(total), vm(gain), g_qkv, g_out)

    grid = (LEV, ROWS, COLS, D)
    return out.reshape(grid), grad.reshape(grid), g_qkv, g_out, g_gain.reshape(D)


def solution(mesh):
    return jax.shard_map(
        on_device,
        mesh=mesh,
        in_specs=(P(None, "lat", "lon", None), P(None, "lat", "lon", None), P(), P(), P()),
        out_specs=(P(None, "lat", "lon", None), P(None, "lat", "lon", None), P(), P(), P()),
        check_vma=False,
    )
```

```python
import functools
import math

import jax
import jax.numpy as jnp
import numpy as np
from jax import lax
from jax.experimental import pallas as pl
from jax.experimental.pallas import tpu as pltpu
from jax.sharding import PartitionSpec as P

HEADS = 8
LEV, ROWS, COLS = 4, 6, 24
WL, WR, WC = 2, 6, 12
D = 512
SPAN = WL * WR * WC
TOK = LEV * ROWS * COLS
BOTH = ("lat", "lon")
f32 = jnp.float32
bf16 = jnp.bfloat16
VMEM = 24 * 1024 * 1024


def index_of(y, x, z, c):
    return (y * 2 + x // 2) * 32 + (x % 2) * 16 + z * 2 + c


def place_of(i):
    return i // 64, ((i // 32) % 2) * 2 + (i // 16) % 2, (i // 2) % 8, i % 2


def route(step):
    return [(i, index_of(*step(*place_of(i)))) for i in range(256)]


def to_sibling(y, x, z, c):
    return y, x, z, 1 - c


def first_axis(k):
    return lambda y, x, z, c: ((y + k) % 4, x, z, c) if c == 0 else (y, (x + k) % 4, z, c)


def second_axis(k):
    return lambda y, x, z, c: (y, (x + k) % 4, z, c) if c == 0 else ((y + k) % 4, x, z, c)


def flip_z(k):
    return lambda y, x, z, c: (y, x, z ^ k, c)


def send(x, step):
    return lax.ppermute(x, BOTH, route(step))


def shifted(dlat, dlon):
    def pairs():
        out = []
        for i in range(256):
            a, b = i // 32, i % 32
            out.append((i, ((a + dlat) % 8) * 32 + (b + dlon) % 32))
        return out

    return pairs()


GTOK = TOK // 2
LAT, SIDE = 112, 48
HALO = LAT + 2 * SIDE
LEVELS = ((1, 2), (3, 0))


def gather_tables():
    local = np.zeros((GTOK, GTOK), np.float32)
    halo = np.zeros((GTOK, HALO), np.float32)
    for lev in range(WL):
        for rr in range(ROWS):
            for cr in range(COLS):
                t = cr // WC * SPAN + lev * WR * WC + rr * WC + cr % WC
                r, c = rr + 3, cr + 6
                if r < ROWS and c < COLS:
                    local[t, lev * ROWS * COLS + r * COLS + c] = 1
                elif c < COLS:
                    halo[t, lev * 54 + (r - ROWS) * 18 + c - 6] = 1
                elif r < ROWS:
                    halo[t, LAT + lev * 18 + (r - 3) * 6 + c - COLS] = 1
                else:
                    halo[t, LAT + SIDE + lev * 18 + (r - ROWS) * 6 + c - COLS] = 1
    return local, halo


def select_table():
    select = np.zeros((HALO, GTOK), np.float32)
    for lev in range(WL):
        for r in range(ROWS):
            for c in range(COLS):
                t = lev * ROWS * COLS + r * COLS + c
                if r < 3 and c >= 6:
                    select[lev * 54 + r * 18 + c - 6, t] = 1
                elif r >= 3 and c < 6:
                    select[LAT + lev * 18 + (r - 3) * 6 + c, t] = 1
                elif r < 3:
                    select[LAT + SIDE + lev * 18 + r * 6 + c, t] = 1
    return select


def dot(a, b, dims=((1,), (0,))):
    return lax.dot_general(a, b, (dims, ((), ())), preferred_element_type=f32)


NT = ((1,), (1,))
TN = ((0,), (0,))


def normalise(x):
    centred = x - jnp.mean(x, axis=-1, keepdims=True)
    rstd = lax.rsqrt(jnp.mean(centred * centred, axis=-1, keepdims=True) + 1e-5)
    return centred * rstd, rstd


def split(rows, lat, lon, diag):
    lat[...] = rows[:LAT].astype(bf16)
    lon[...] = rows[LAT : LAT + SIDE].astype(bf16)
    diag[...] = rows[LAT + SIDE :].astype(bf16)


def fetch(group, f_hbm, c_hbm, fc, sem):
    copies = []
    for k, level in enumerate(LEVELS[group]):
        for n, source in enumerate((f_hbm, c_hbm)):
            copies.append(
                pltpu.make_async_copy(
                    source.at[pl.ds(level * 144, 144)],
                    fc.at[pl.ds(k * 144, 144), pl.ds(n * D, D)],
                    sem.at[2 * k + n],
                )
            )
    return copies


def pack0_kernel(f_hbm, c_hbm, s_hbm, fc, select, lat, lon, diag, sem):
    copies = fetch(0, f_hbm, c_hbm, fc, sem)
    copies.append(pltpu.make_async_copy(s_hbm, select, sem.at[4]))
    for copy in copies:
        copy.start()
    for copy in copies:
        copy.wait()
    split(dot(select[...], fc[...]), lat, lon, diag)


def load_kernel(fc0, select, *refs):
    f_hbm, c_hbm, sources, targets = refs[0], refs[1], refs[2:7], refs[7:12]
    fc1, lat, lon, diag, part0, part1, fetch_sem, sem = refs[12:]
    fetches = fetch(1, f_hbm, c_hbm, fc1, fetch_sem)
    copies = [
        pltpu.make_async_copy(a, b, sem.at[i]) for i, (a, b) in enumerate(zip(sources, targets))
    ]
    for copy in fetches + copies:
        copy.start()
    for copy in fetches:
        copy.wait()
    split(dot(select[...], fc1[...]), lat, lon, diag)
    copies[0].wait()
    part0[...] = dot(targets[0][...], fc0[...]).astype(bf16)
    part1[...] = dot(targets[0][...], fc1[...]).astype(bf16)
    for copy in copies[1:]:
        copy.wait()


FACTOR = 1.0 / math.sqrt(D // HEADS)


def head_mask(heads, value):
    shape = (heads * SPAN, heads * 64)
    row = lax.broadcasted_iota(jnp.int32, shape, 0)
    first = lax.broadcasted_iota(jnp.int32, shape, 1) // 64 * SPAN
    return jnp.where((row >= first) & (row < first + SPAN), value, 0.0).astype(bf16)


def joined(r, heads, factor=1.0):
    lane = lax.broadcasted_iota(jnp.int32, (SPAN, heads * 64), 1)
    out = r[:SPAN]
    for h in range(1, heads):
        out = jnp.where(lane >= h * 64, r[h * SPAN : (h + 1) * SPAN], out)
    return (out * factor).astype(bf16)


def repeated(x, heads, pick):
    return jnp.concatenate([x] * heads, axis=0) * pick


def attend_kernel(group, place, *refs):
    part, table, lat, lon, diag, gain, w_ref, o_ref = refs[:8]
    if group == 0:
        normed, ctw, mixed, gact, qkv, gm, probs = refs[8:]
    else:
        (normed0, ctw0, mixed0, gact0, mixed, gact, own, other, normed, ctw, qkv, gm, probs, acc) = refs[8:]
    rows = jnp.concatenate([lat[...], lon[...], diag[...]], axis=0)
    tokens = part[...].astype(f32) + dot(table[...], rows)
    xhat, _ = normalise(tokens[:, :D])
    normed[...] = (xhat * gain[...]).astype(bf16)
    qkv[...] = dot(normed[...], w_ref[...]).astype(bf16)
    ctw[...] = tokens[:, D:].astype(bf16)
    gm[...] = dot(ctw[...], o_ref[...], NT).astype(bf16)

    tq = lax.rem(lax.broadcasted_iota(jnp.int32, (SPAN, 2 * SPAN), 1), SPAN)
    tk = lax.broadcasted_iota(jnp.int32, (SPAN, 2 * SPAN), 0)

    def lev_of(t):
        return (t >= SPAN // 2).astype(jnp.int32)

    def half_of(t):
        return (t - SPAN // 2 * lev_of(t) >= SPAN // 4).astype(jnp.int32)

    differ = jnp.abs(half_of(tq) - half_of(tk)) * place[0]
    if group == 1:
        differ = differ + jnp.abs(lev_of(tq) - lev_of(tk))
    same = differ == 0

    pair = head_mask(2, FACTOR)
    for w in range(2):
        at = pl.ds(w * SPAN, SPAN)
        for p in range(HEADS // 2):
            cols = pl.ds(128 * p, 128)
            q = repeated(qkv[at, cols], 2, pair)
            k = qkv[at, pl.ds(D + 128 * p, 128)]
            v = qkv[at, pl.ds(2 * D + 128 * p, 128)]
            s = jnp.where(same, dot(k, q, NT), -1000000000.0)
            e = jnp.exp(s - jnp.max(s, axis=0, keepdims=True))
            rounded = (e * (1.0 / jnp.sum(e, axis=0, keepdims=True))).astype(bf16)
            probs[pl.ds((w * 2 + p // 2) * SPAN, SPAN), pl.ds(p % 2 * 2 * SPAN, 2 * SPAN)] = rounded
            mixed[at, cols] = joined(dot(rounded, v, TN), 2)

    four = head_mask(4, 1.0)
    scaled = head_mask(4, FACTOR)
    for w in range(2):
        at = pl.ds(w * SPAN, SPAN)
        for p in range(HEADS // 4):
            cols = pl.ds(256 * p, 256)
            q = repeated(qkv[at, cols], 4, scaled)
            g = repeated(gm[at, cols], 4, four)
            k = qkv[at, pl.ds(D + 256 * p, 256)]
            v = qkv[at, pl.ds(2 * D + 256 * p, 256)]
            rounded = probs[pl.ds((w * 2 + p) * SPAN, SPAN), :]
            gact[at, pl.ds(2 * D + 256 * p, 256)] = dot(rounded, g).astype(bf16)
            dp = dot(v, g, NT)
            pr = rounded.astype(f32)
            inner = jnp.sum(dp * pr, axis=0, keepdims=True)
            ds = (pr * (dp - inner)).astype(bf16)
            gact[at, cols] = joined(dot(ds, k, TN), 4, FACTOR)
            gact[at, pl.ds(D + 256 * p, 256)] = dot(ds, q).astype(bf16)

    if group == 0:
        return

    def both(a, b):
        return jnp.concatenate([a[...], b[...]], axis=0)

    acc[:, : 3 * D] = dot(both(normed0, normed), both(gact0, gact), TN)
    acc[:, 3 * D :] = dot(both(mixed0, mixed), both(ctw0, ctw), TN)
    y, x, c = place[1], place[2], place[3]

    def fill(out, core):
        d1 = jnp.where(core == 0, y, x)
        d2 = jnp.where(core == 0, x, y)
        for s1 in range(4):
            for s2 in range(4):
                r = core * 256 + lax.rem(d1 + s1, 4) * 64 + lax.rem(d2 + s2, 4) * 16
                rows = acc[pl.ds(pl.multiple_of(r, 16), 16), :]
                out[pl.ds((s1 * 4 + s2) * 16, 16), :] = rows.astype(bf16)

    fill(own, c)
    fill(other, 1 - c)


def back_kernel(
    mixed0, mixed1, gact0, gact1, w_ref, o_ref, table,
    both0, both1, to_lat0, to_lat1, to_lon, to_diag,
):
    for g, (mixed, gact, both, to_lat) in enumerate(
        ((mixed0, gact0, both0, to_lat0), (mixed1, gact1, both1, to_lat1))
    ):
        both[:, :D] = dot(mixed[...], o_ref[...]).astype(bf16)
        both[:, D:] = dot(gact[...], w_ref[...], NT).astype(bf16)
        side = pl.ds(g * SIDE, SIDE)
        split(dot(table[...], both[...], TN), to_lat, to_lon.at[side], to_diag.at[side])


def finish_kernel(
    fc0, fc1, both0, both1, r_lat0, r_lat1, r_lon, r_diag, table, select, gain, out, grad
):
    for g, (fc, both, r_lat) in enumerate(((fc0, both0, r_lat0), (fc1, both1, r_lat1))):
        side = pl.ds(g * SIDE, SIDE)
        rows = jnp.concatenate([r_lat[...], r_lon[side, :], r_diag[side, :]], axis=0)
        grid = dot(table[...], both[...], TN) + dot(select[...], rows, TN)
        x = fc[:, :D].astype(f32)
        xhat, rstd = normalise(x)
        gs = grid[:, D:] * gain[...]
        first = jnp.mean(gs, axis=-1, keepdims=True)
        second = jnp.mean(gs * xhat, axis=-1, keepdims=True)
        result = (x + grid[:, :D]).astype(bf16)
        slope = (fc[:, D:].astype(f32) + rstd * (gs - first - xhat * second)).astype(bf16)
        for k, level in enumerate(LEVELS[g]):
            at = pl.ds(level * 144, 144)
            out[at, :] = result[k * 144 : (k + 1) * 144]
            grad[at, :] = slope[k * 144 : (k + 1) * 144]


def weights_kernel(side, place, *refs):
    pieces, refs = refs[:4], refs[4:]
    if side == 0:
        w_ref, g_qkv, g_out, g_total, buf_q, buf_o, sem = refs
    else:
        w_ref, before, gain, _, _, g_qkv, g_out, g_total, buf_q, buf_o, sem = refs
    y, x, c = place[1], place[2], place[3]
    core = c if side == 0 else 1 - c
    d1 = jnp.where(core == 0, y, x)
    d2 = jnp.where(core == 0, x, y)
    bands = [pl.multiple_of(core * 256 + lax.rem(d1 + i, 4) * 64, 64) for i in range(4)]
    copies = []
    for i in range(4):
        for s2 in range(4):
            at = pl.ds(pl.multiple_of(lax.rem(d2 + s2, 4) * 16, 16), 16)
            block = pieces[i][pl.ds(s2 * 16, 16), :].astype(f32)
            buf_q[i, at, :] = block[:, : 3 * D]
            buf_o[i, at, :] = block[:, 3 * D :]
        for k, (src, dst) in enumerate(((buf_q, g_qkv), (buf_o, g_out))):
            copy = pltpu.make_async_copy(src.at[i], dst.at[pl.ds(bands[i], 64)], sem.at[i, k])
            copy.start()
            copies.append(copy)
    total = jnp.zeros((1, D), f32) if side == 0 else before[...]
    lane = lax.broadcasted_iota(jnp.int32, (64, D), 1)
    local = lax.broadcasted_iota(jnp.int32, (64, D), 0)
    for i in range(4):
        w = w_ref[pl.ds(bands[i], 64), :].astype(f32)
        sums = jnp.sum(buf_q[i] * w, axis=1, keepdims=True)
        spread = jnp.where(lane == local + bands[i], sums, 0.0)
        total = total + jnp.sum(spread, axis=0, keepdims=True)
    g_total[...] = total if side == 0 else total / gain[...]
    for copy in copies:
        copy.wait()


def to_weights(side, place, pieces, qkv_weight, *more):
    inside = pl.BlockSpec(memory_space=pltpu.VMEM)
    anywhere = pl.BlockSpec(memory_space=pl.ANY)
    extra = [] if side == 0 else [inside, inside, anywhere, anywhere]
    return pl.pallas_call(
        functools.partial(weights_kernel, side),
        out_shape=[
            shape(D, 3 * D, dtype=f32),
            shape(D, D, dtype=f32),
            (vshape if side == 0 else shape)(1, D, dtype=f32),
        ],
        in_specs=spec(5, True) + extra,
        out_specs=[anywhere, anywhere, inside],
        scratch_shapes=[
            pltpu.VMEM((4, 64, 3 * D), f32),
            pltpu.VMEM((4, 64, D), f32),
            pltpu.SemaphoreType.DMA((4, 2)),
        ],
        input_output_aliases={} if side == 0 else {8: 0, 9: 1},
        compiler_params=params(),
        cost_estimate=cost(10**7, 4 * 10**6),
        name="weights" + str(side),
    )(place, *vms(*pieces), vm(qkv_weight), *more)


def params():
    return pltpu.CompilerParams(vmem_limit_bytes=VMEM)


def vm(x):
    return pltpu.with_memory_space_constraint(x, pltpu.VMEM)


def vms(*xs):
    return [vm(x) for x in xs]


def vshape(*dims, dtype=bf16):
    return pltpu.VMEM(dims, dtype)


def spec(count, scalar=False):
    whole = [pl.BlockSpec(memory_space=pltpu.VMEM)] * count
    return ([pl.BlockSpec(memory_space=pltpu.SMEM)] if scalar else []) + whole


def shape(*dims, dtype=bf16):
    return jax.ShapeDtypeStruct(dims, dtype)


def cost(flops, moved):
    return pl.CostEstimate(flops=flops, bytes_accessed=moved, transcendentals=0)


def hbm(*xs):
    return [pltpu.with_memory_space_constraint(x, pltpu.HBM) for x in xs]


def kernel_call(body, name, args, outs, in_hbm=0, place=None, scratch=(), price=(10**6, 10**4)):
    if in_hbm > 0:
        specs = [pl.BlockSpec(memory_space=pltpu.HBM)] * in_hbm + spec(len(args) - in_hbm)
        args = hbm(*args[:in_hbm]) + vms(*args[in_hbm:])
    else:
        specs = spec(len(args) + in_hbm) + [pl.BlockSpec(memory_space=pltpu.HBM)] * -in_hbm
        args = vms(*args[: len(args) + in_hbm]) + hbm(*args[len(args) + in_hbm :])
    if place is not None:
        specs = spec(0, True) + specs
        args = [place] + args
    return pl.pallas_call(
        body,
        out_shape=outs,
        in_specs=specs,
        out_specs=spec(len(outs)),
        scratch_shapes=list(scratch),
        compiler_params=params(),
        cost_estimate=cost(*price),
        name=name,
    )(*args)


def message_shapes():
    return [vshape(LAT, 2 * D), vshape(SIDE, 2 * D), vshape(SIDE, 2 * D)]


def to_pack0(f, c, select):
    return kernel_call(
        pack0_kernel, "pack0", (f, c, select),
        [vshape(GTOK, 2 * D), vshape(HALO, GTOK)] + message_shapes(),
        in_hbm=3, scratch=[pltpu.SemaphoreType.DMA((5,))],
    )


def to_load(fc0, select, f, c, *sources):
    return kernel_call(
        load_kernel, "load", (fc0, select, f, c, *sources),
        [vshape(*x.shape, dtype=x.dtype) for x in sources]
        + [vshape(GTOK, 2 * D)] + message_shapes() + [vshape(GTOK, 2 * D)] * 2,
        in_hbm=-2 - len(sources),
        scratch=[pltpu.SemaphoreType.DMA((4,)), pltpu.SemaphoreType.DMA((len(sources),))],
    )


def to_attend(group, place, *args):
    kept = [vshape(GTOK, D), vshape(GTOK, D)]
    results = [vshape(GTOK, D), vshape(GTOK, 3 * D)]
    inner = [
        pltpu.VMEM((GTOK, 3 * D), bf16),
        pltpu.VMEM((GTOK, D), bf16),
        pltpu.VMEM((4 * SPAN, 4 * SPAN), bf16),
    ]
    if group == 0:
        outs, scratch = kept + results, inner
    else:
        outs = results + [vshape(256, 4 * D), vshape(256, 4 * D)]
        scratch = [pltpu.VMEM((GTOK, D), bf16)] * 2 + inner + [pltpu.VMEM((D, 4 * D), f32)]
    return kernel_call(
        functools.partial(attend_kernel, group), "attend" + str(group), args, outs,
        place=place, scratch=scratch,
    )


def to_back(*args):
    return kernel_call(
        back_kernel, "back", args,
        [vshape(GTOK, 2 * D)] * 2 + [vshape(LAT, 2 * D)] * 2 + [vshape(2 * SIDE, 2 * D)] * 2,
        price=(2 * 10**9, 5 * 10**6),
    )


def to_finish(*args):
    return kernel_call(
        finish_kernel, "finish", args, [shape(TOK, D)] * 2, price=(2 * 10**9, 8 * 10**6)
    )


def add(*xs):
    total = xs[0].astype(f32)
    for x in xs[1:]:
        total = total + x.astype(f32)
    return total.astype(bf16)


def tied(x):
    return lax.optimization_barrier(x)


def halo_in(lat, lon, diag):
    return (
        lax.ppermute(lat, BOTH, shifted(-1, 0)),
        lax.ppermute(lon, BOTH, shifted(0, -1)),
        lax.ppermute(diag, BOTH, shifted(-1, -1)),
    )


def on_device(fields, cotangent, layer_norm_gain, qkv_weight, out_weight):
    a, b = lax.axis_index("lat"), lax.axis_index("lon")
    place = jnp.stack(
        [
            (a == 7).astype(jnp.int32),
            (a // 2).astype(jnp.int32),
            ((a % 2) * 2 + b // 16).astype(jnp.int32),
            (b % 2).astype(jnp.int32),
        ]
    )
    tables = [jnp.asarray(t, bf16) for t in gather_tables()]
    select = jnp.asarray(select_table(), bf16)
    f, c = fields.reshape(TOK, D), cotangent.reshape(TOK, D)
    fc0, select, *parts = to_pack0(f, c, select)
    halo0 = halo_in(*parts)
    local, table, w, o, gain, fc1, lat1, lon1, diag1, part0, part1 = to_load(
        fc0, select, f, c, *tables, qkv_weight, out_weight, layer_norm_gain.reshape(1, D)
    )
    lat1, lon1, diag1, near, far = tied((lat1, lon1, diag1, *halo0[1:]))
    halo0, halo1 = (halo0[0], near, far), halo_in(lat1, lon1, diag1)
    normed0, ctw0, mixed0, gact0 = to_attend(0, place, part0, table, *halo0, gain, w, o)
    mixed1, gact1, own, other = to_attend(
        1, place, part1, table, *halo1, gain, w, o, normed0, ctw0, mixed0, gact0
    )

    there = send(other, to_sibling)
    part = [add(own[64 * k : 64 * k + 64], there[64 * k : 64 * k + 64]) for k in range(4)]
    mixed1, part = tied((mixed1, part))
    both0, both1, to_lat0, to_lat1, to_lon, to_diag = to_back(
        mixed0, mixed1, gact0, gact1, w, o, table
    )
    recv = [send(part[k], first_axis(k)) for k in (1, 2, 3)]
    recv, to_lat0 = tied((recv, to_lat0))
    part = add(part[0], *recv)
    part, to_lat0, to_lat1, to_lon, to_diag = tied((part, to_lat0, to_lat1, to_lon, to_diag))
    part = add(part[:16], *[send(part[16 * k : 16 * k + 16], second_axis(k)) for k in (1, 2, 3)])
    r_lat0 = lax.ppermute(to_lat0, BOTH, shifted(1, 0))
    r_lat1 = lax.ppermute(to_lat1, BOTH, shifted(1, 0))
    r_lon = lax.ppermute(to_lon, BOTH, shifted(0, 1))
    r_diag = lax.ppermute(to_diag, BOTH, shifted(1, 1))
    recv = send(part, flip_z(1))
    recv, r_lat0 = tied((recv, r_lat0))
    part = add(part, recv)
    recv = send(part, flip_z(2))
    recv, r_lat1 = tied((recv, r_lat1))
    part = add(part, recv)
    recv = send(part, flip_z(6))
    recv, r_lon, r_diag = tied((recv, r_lon, r_diag))
    part = add(part, recv)

    block = jnp.concatenate([part] + [send(part, second_axis(4 - s)) for s in (1, 2, 3)], axis=0)
    mine = [send(block, first_axis(4 - s)) for s in (1, 2, 3)]
    out, grad = to_finish(
        fc0, fc1, both0, both1, r_lat0, r_lat1, r_lon, r_diag, local, select, gain
    )
    mine, out = tied((mine, out))
    mine = [block] + mine
    sibling = [send(m, to_sibling) for m in mine]
    g_qkv, g_out, total = to_weights(0, place, mine, w)
    g_qkv, g_out, g_gain = to_weights(1, place, sibling, w, vm(total), vm(gain), g_qkv, g_out)

    grid = (LEV, ROWS, COLS, D)
    return out.reshape(grid), grad.reshape(grid), g_qkv, g_out, g_gain.reshape(D)


def solution(mesh):
    return jax.shard_map(
        on_device,
        mesh=mesh,
        in_specs=(P(None, "lat", "lon", None), P(None, "lat", "lon", None), P(), P(), P()),
        out_specs=(P(None, "lat", "lon", None), P(None, "lat", "lon", None), P(), P(), P()),
        check_vma=False,
    )
```

```python
import functools
import math

import jax
import jax.numpy as jnp
import numpy as np
from jax import lax
from jax.experimental import pallas as pl
from jax.experimental.pallas import tpu as pltpu
from jax.sharding import PartitionSpec as P

HEADS = 8
LEV, ROWS, COLS = 4, 6, 24
WL, WR, WC = 2, 6, 12
D = 512
SPAN = WL * WR * WC
TOK = LEV * ROWS * COLS
BOTH = ("lat", "lon")
f32 = jnp.float32
bf16 = jnp.bfloat16
VMEM = 24 * 1024 * 1024


def index_of(y, x, z, c):
    return (y * 2 + x // 2) * 32 + (x % 2) * 16 + z * 2 + c


def place_of(i):
    return i // 64, ((i // 32) % 2) * 2 + (i // 16) % 2, (i // 2) % 8, i % 2


def route(step):
    return [(i, index_of(*step(*place_of(i)))) for i in range(256)]


def to_sibling(y, x, z, c):
    return y, x, z, 1 - c


def first_axis(k):
    return lambda y, x, z, c: ((y + k) % 4, x, z, c) if c == 0 else (y, (x + k) % 4, z, c)


def second_axis(k):
    return lambda y, x, z, c: (y, (x + k) % 4, z, c) if c == 0 else ((y + k) % 4, x, z, c)


def flip_z(k):
    return lambda y, x, z, c: (y, x, z ^ k, c)


def send(x, step):
    return lax.ppermute(x, BOTH, route(step))


def shifted(dlat, dlon):
    def pairs():
        out = []
        for i in range(256):
            a, b = i // 32, i % 32
            out.append((i, ((a + dlat) % 8) * 32 + (b + dlon) % 32))
        return out

    return pairs()


GTOK = TOK // 2
LAT, SIDE = 112, 48
HALO = LAT + 2 * SIDE
LEVELS = ((1, 2), (3, 0))


def gather_tables():
    local = np.zeros((GTOK, GTOK), np.float32)
    halo = np.zeros((GTOK, HALO), np.float32)
    for lev in range(WL):
        for rr in range(ROWS):
            for cr in range(COLS):
                t = cr // WC * SPAN + lev * WR * WC + rr * WC + cr % WC
                r, c = rr + 3, cr + 6
                if r < ROWS and c < COLS:
                    local[t, lev * ROWS * COLS + r * COLS + c] = 1
                elif c < COLS:
                    halo[t, lev * 54 + (r - ROWS) * 18 + c - 6] = 1
                elif r < ROWS:
                    halo[t, LAT + lev * 18 + (r - 3) * 6 + c - COLS] = 1
                else:
                    halo[t, LAT + SIDE + lev * 18 + (r - ROWS) * 6 + c - COLS] = 1
    return local, halo


def select_table():
    select = np.zeros((HALO, GTOK), np.float32)
    for lev in range(WL):
        for r in range(ROWS):
            for c in range(COLS):
                t = lev * ROWS * COLS + r * COLS + c
                if r < 3 and c >= 6:
                    select[lev * 54 + r * 18 + c - 6, t] = 1
                elif r >= 3 and c < 6:
                    select[LAT + lev * 18 + (r - 3) * 6 + c, t] = 1
                elif r < 3:
                    select[LAT + SIDE + lev * 18 + r * 6 + c, t] = 1
    return select


def dot(a, b, dims=((1,), (0,))):
    return lax.dot_general(a, b, (dims, ((), ())), preferred_element_type=f32)


NT = ((1,), (1,))
TN = ((0,), (0,))


def normalise(x):
    centred = x - jnp.mean(x, axis=-1, keepdims=True)
    rstd = lax.rsqrt(jnp.mean(centred * centred, axis=-1, keepdims=True) + 1e-5)
    return centred * rstd, rstd


def split(rows, lat, lon, diag):
    lat[...] = rows[:LAT].astype(bf16)
    lon[...] = rows[LAT : LAT + SIDE].astype(bf16)
    diag[...] = rows[LAT + SIDE :].astype(bf16)


def fetch(group, f_hbm, c_hbm, fc, sem):
    copies = []
    for k, level in enumerate(LEVELS[group]):
        for n, source in enumerate((f_hbm, c_hbm)):
            copies.append(
                pltpu.make_async_copy(
                    source.at[pl.ds(level * 144, 144)],
                    fc.at[pl.ds(k * 144, 144), pl.ds(n * D, D)],
                    sem.at[2 * k + n],
                )
            )
    return copies


def pack0_kernel(f_hbm, c_hbm, s_hbm, fc, select, lat, lon, diag, sem):
    copies = fetch(0, f_hbm, c_hbm, fc, sem)
    copies.append(pltpu.make_async_copy(s_hbm, select, sem.at[4]))
    for copy in copies:
        copy.start()
    for copy in copies:
        copy.wait()
    split(dot(select[...], fc[...]), lat, lon, diag)


def pack1_kernel(f_hbm, c_hbm, select, fc, lat, lon, diag, sem):
    copies = fetch(1, f_hbm, c_hbm, fc, sem)
    for copy in copies:
        copy.start()
    for copy in copies:
        copy.wait()
    split(dot(select[...], fc[...]), lat, lon, diag)


def load_kernel(fc0, fc1, *refs):
    sources, targets, (part0, part1, sem) = refs[:5], refs[5:10], refs[10:]
    copies = [
        pltpu.make_async_copy(a, b, sem.at[i]) for i, (a, b) in enumerate(zip(sources, targets))
    ]
    for copy in copies:
        copy.start()
    copies[0].wait()
    part0[...] = dot(targets[0][...], fc0[...]).astype(bf16)
    part1[...] = dot(targets[0][...], fc1[...]).astype(bf16)
    for copy in copies[1:]:
        copy.wait()


FACTOR = 1.0 / math.sqrt(D // HEADS)


def head_mask(heads, value):
    shape = (heads * SPAN, heads * 64)
    row = lax.broadcasted_iota(jnp.int32, shape, 0)
    first = lax.broadcasted_iota(jnp.int32, shape, 1) // 64 * SPAN
    return jnp.where((row >= first) & (row < first + SPAN), value, 0.0).astype(bf16)


def joined(r, heads, factor=1.0):
    lane = lax.broadcasted_iota(jnp.int32, (SPAN, heads * 64), 1)
    out = r[:SPAN]
    for h in range(1, heads):
        out = jnp.where(lane >= h * 64, r[h * SPAN : (h + 1) * SPAN], out)
    return (out * factor).astype(bf16)


def repeated(x, heads, pick):
    return jnp.concatenate([x] * heads, axis=0) * pick


def attend_kernel(group, place, *refs):
    part, table, lat, lon, diag, gain, w_ref, o_ref = refs[:8]
    if group == 0:
        normed, ctw, mixed, gact, qkv, gm, probs = refs[8:]
    else:
        (normed0, ctw0, mixed0, gact0, mixed, gact, own, other, normed, ctw, qkv, gm, probs, acc) = refs[8:]
    rows = jnp.concatenate([lat[...], lon[...], diag[...]], axis=0)
    tokens = part[...].astype(f32) + dot(table[...], rows)
    xhat, _ = normalise(tokens[:, :D])
    normed[...] = (xhat * gain[...]).astype(bf16)
    qkv[...] = dot(normed[...], w_ref[...]).astype(bf16)
    ctw[...] = tokens[:, D:].astype(bf16)
    gm[...] = dot(ctw[...], o_ref[...], NT).astype(bf16)

    tq = lax.rem(lax.broadcasted_iota(jnp.int32, (SPAN, 2 * SPAN), 1), SPAN)
    tk = lax.broadcasted_iota(jnp.int32, (SPAN, 2 * SPAN), 0)

    def lev_of(t):
        return (t >= SPAN // 2).astype(jnp.int32)

    def half_of(t):
        return (t - SPAN // 2 * lev_of(t) >= SPAN // 4).astype(jnp.int32)

    differ = jnp.abs(half_of(tq) - half_of(tk)) * place[0]
    if group == 1:
        differ = differ + jnp.abs(lev_of(tq) - lev_of(tk))
    same = differ == 0

    pair = head_mask(2, FACTOR)
    for w in range(2):
        at = pl.ds(w * SPAN, SPAN)
        for p in range(HEADS // 2):
            cols = pl.ds(128 * p, 128)
            q = repeated(qkv[at, cols], 2, pair)
            k = qkv[at, pl.ds(D + 128 * p, 128)]
            v = qkv[at, pl.ds(2 * D + 128 * p, 128)]
            s = jnp.where(same, dot(k, q, NT), -1000000000.0)
            e = jnp.exp(s - jnp.max(s, axis=0, keepdims=True))
            rounded = (e * (1.0 / jnp.sum(e, axis=0, keepdims=True))).astype(bf16)
            probs[pl.ds((w * 2 + p // 2) * SPAN, SPAN), pl.ds(p % 2 * 2 * SPAN, 2 * SPAN)] = rounded
            mixed[at, cols] = joined(dot(rounded, v, TN), 2)

    four = head_mask(4, 1.0)
    scaled = head_mask(4, FACTOR)
    for w in range(2):
        at = pl.ds(w * SPAN, SPAN)
        for p in range(HEADS // 4):
            cols = pl.ds(256 * p, 256)
            q = repeated(qkv[at, cols], 4, scaled)
            g = repeated(gm[at, cols], 4, four)
            k = qkv[at, pl.ds(D + 256 * p, 256)]
            v = qkv[at, pl.ds(2 * D + 256 * p, 256)]
            rounded = probs[pl.ds((w * 2 + p) * SPAN, SPAN), :]
            gact[at, pl.ds(2 * D + 256 * p, 256)] = dot(rounded, g).astype(bf16)
            dp = dot(v, g, NT)
            pr = rounded.astype(f32)
            inner = jnp.sum(dp * pr, axis=0, keepdims=True)
            ds = (pr * (dp - inner)).astype(bf16)
            gact[at, cols] = joined(dot(ds, k, TN), 4, FACTOR)
            gact[at, pl.ds(D + 256 * p, 256)] = dot(ds, q).astype(bf16)

    if group == 0:
        return

    def both(a, b):
        return jnp.concatenate([a[...], b[...]], axis=0)

    acc[:, : 3 * D] = dot(both(normed0, normed), both(gact0, gact), TN)
    acc[:, 3 * D :] = dot(both(mixed0, mixed), both(ctw0, ctw), TN)
    y, x, c = place[1], place[2], place[3]

    def fill(out, core):
        d1 = jnp.where(core == 0, y, x)
        d2 = jnp.where(core == 0, x, y)
        for s1 in range(4):
            for s2 in range(4):
                r = core * 256 + lax.rem(d1 + s1, 4) * 64 + lax.rem(d2 + s2, 4) * 16
                rows = acc[pl.ds(pl.multiple_of(r, 16), 16), :]
                out[pl.ds((s1 * 4 + s2) * 16, 16), :] = rows.astype(bf16)

    fill(own, c)
    fill(other, 1 - c)


def back_kernel(
    mixed0, mixed1, gact0, gact1, w_ref, o_ref, table,
    both0, both1, to_lat0, to_lat1, to_lon, to_diag,
):
    for g, (mixed, gact, both, to_lat) in enumerate(
        ((mixed0, gact0, both0, to_lat0), (mixed1, gact1, both1, to_lat1))
    ):
        both[:, :D] = dot(mixed[...], o_ref[...]).astype(bf16)
        both[:, D:] = dot(gact[...], w_ref[...], NT).astype(bf16)
        side = pl.ds(g * SIDE, SIDE)
        split(dot(table[...], both[...], TN), to_lat, to_lon.at[side], to_diag.at[side])


def finish_kernel(
    both0, both1, r_lat0, r_lat1, r_lon, r_diag, gain, f_hbm, c_hbm, t_hbm, s_hbm,
    out, grad, fc0, fc1, table, select, sem,
):
    copies = fetch(0, f_hbm, c_hbm, fc0, sem.at[0]) + fetch(1, f_hbm, c_hbm, fc1, sem.at[1])
    copies.append(pltpu.make_async_copy(t_hbm, table, sem.at[2, 0]))
    copies.append(pltpu.make_async_copy(s_hbm, select, sem.at[2, 1]))
    for copy in copies:
        copy.start()
    for copy in copies:
        copy.wait()
    for g, (fc, both, r_lat) in enumerate(((fc0, both0, r_lat0), (fc1, both1, r_lat1))):
        side = pl.ds(g * SIDE, SIDE)
        rows = jnp.concatenate([r_lat[...], r_lon[side, :], r_diag[side, :]], axis=0)
        grid = dot(table[...], both[...], TN) + dot(select[...], rows, TN)
        x = fc[:, :D].astype(f32)
        xhat, rstd = normalise(x)
        gs = grid[:, D:] * gain[...]
        first = jnp.mean(gs, axis=-1, keepdims=True)
        second = jnp.mean(gs * xhat, axis=-1, keepdims=True)
        result = (x + grid[:, :D]).astype(bf16)
        slope = (fc[:, D:].astype(f32) + rstd * (gs - first - xhat * second)).astype(bf16)
        for k, level in enumerate(LEVELS[g]):
            at = pl.ds(level * 144, 144)
            out[at, :] = result[k * 144 : (k + 1) * 144]
            grad[at, :] = slope[k * 144 : (k + 1) * 144]


def weights_kernel(side, place, *refs):
    pieces, refs = refs[:4], refs[4:]
    if side == 0:
        w_ref, g_qkv, g_out, g_total, buf_q, buf_o, sem = refs
    else:
        w_ref, before, gain, _, _, g_qkv, g_out, g_total, buf_q, buf_o, sem = refs
    y, x, c = place[1], place[2], place[3]
    core = c if side == 0 else 1 - c
    d1 = jnp.where(core == 0, y, x)
    d2 = jnp.where(core == 0, x, y)
    bands = [pl.multiple_of(core * 256 + lax.rem(d1 + i, 4) * 64, 64) for i in range(4)]
    copies = []
    for i in range(4):
        for s2 in range(4):
            at = pl.ds(pl.multiple_of(lax.rem(d2 + s2, 4) * 16, 16), 16)
            block = pieces[i][pl.ds(s2 * 16, 16), :].astype(f32)
            buf_q[i, at, :] = block[:, : 3 * D]
            buf_o[i, at, :] = block[:, 3 * D :]
        for k, (src, dst) in enumerate(((buf_q, g_qkv), (buf_o, g_out))):
            copy = pltpu.make_async_copy(src.at[i], dst.at[pl.ds(bands[i], 64)], sem.at[i, k])
            copy.start()
            copies.append(copy)
    total = jnp.zeros((1, D), f32) if side == 0 else before[...]
    lane = lax.broadcasted_iota(jnp.int32, (64, D), 1)
    local = lax.broadcasted_iota(jnp.int32, (64, D), 0)
    for i in range(4):
        w = w_ref[pl.ds(bands[i], 64), :].astype(f32)
        sums = jnp.sum(buf_q[i] * w, axis=1, keepdims=True)
        spread = jnp.where(lane == local + bands[i], sums, 0.0)
        total = total + jnp.sum(spread, axis=0, keepdims=True)
    g_total[...] = total if side == 0 else total / gain[...]
    for copy in copies:
        copy.wait()


def to_weights(side, place, pieces, qkv_weight, *more):
    inside = pl.BlockSpec(memory_space=pltpu.VMEM)
    anywhere = pl.BlockSpec(memory_space=pl.ANY)
    extra = [] if side == 0 else [inside, inside, anywhere, anywhere]
    return pl.pallas_call(
        functools.partial(weights_kernel, side),
        out_shape=[
            shape(D, 3 * D, dtype=f32),
            shape(D, D, dtype=f32),
            (vshape if side == 0 else shape)(1, D, dtype=f32),
        ],
        in_specs=spec(5, True) + extra,
        out_specs=[anywhere, anywhere, inside],
        scratch_shapes=[
            pltpu.VMEM((4, 64, 3 * D), f32),
            pltpu.VMEM((4, 64, D), f32),
            pltpu.SemaphoreType.DMA((4, 2)),
        ],
        input_output_aliases={} if side == 0 else {8: 0, 9: 1},
        compiler_params=params(),
        cost_estimate=cost(10**7, 4 * 10**6),
        name="weights" + str(side),
    )(place, *vms(*pieces), vm(qkv_weight), *more)


def params():
    return pltpu.CompilerParams(vmem_limit_bytes=VMEM)


def vm(x):
    return pltpu.with_memory_space_constraint(x, pltpu.VMEM)


def vms(*xs):
    return [vm(x) for x in xs]


def vshape(*dims, dtype=bf16):
    return pltpu.VMEM(dims, dtype)


def spec(count, scalar=False):
    whole = [pl.BlockSpec(memory_space=pltpu.VMEM)] * count
    return ([pl.BlockSpec(memory_space=pltpu.SMEM)] if scalar else []) + whole


def shape(*dims, dtype=bf16):
    return jax.ShapeDtypeStruct(dims, dtype)


def cost(flops, moved):
    return pl.CostEstimate(flops=flops, bytes_accessed=moved, transcendentals=0)


def hbm(*xs):
    return [pltpu.with_memory_space_constraint(x, pltpu.HBM) for x in xs]


def kernel_call(
    body, name, args, outs, in_hbm=0, place=None, scratch=(), price=(10**6, 10**4), loose=()
):
    if in_hbm > 0:
        specs = [pl.BlockSpec(memory_space=pltpu.HBM)] * in_hbm + spec(len(args) - in_hbm)
        args = hbm(*args[:in_hbm]) + vms(*args[in_hbm:])
    else:
        specs = spec(len(args) + in_hbm) + [pl.BlockSpec(memory_space=pltpu.HBM)] * -in_hbm
        inside = args[: len(args) + in_hbm]
        inside = [x if i in loose else vm(x) for i, x in enumerate(inside)]
        args = inside + hbm(*args[len(args) + in_hbm :])
    if place is not None:
        specs = spec(0, True) + specs
        args = [place] + args
    return pl.pallas_call(
        body,
        out_shape=outs,
        in_specs=specs,
        out_specs=spec(len(outs)),
        scratch_shapes=list(scratch),
        compiler_params=params(),
        cost_estimate=cost(*price),
        name=name,
    )(*args)


def message_shapes():
    return [shape(LAT, 2 * D), shape(SIDE, 2 * D), shape(SIDE, 2 * D)]


def to_pack0(f, c, select):
    return kernel_call(
        pack0_kernel, "pack0", (f, c, select),
        [vshape(GTOK, 2 * D), vshape(HALO, GTOK)] + message_shapes(),
        in_hbm=3, scratch=[pltpu.SemaphoreType.DMA((5,))],
    )


def to_pack1(f, c, select):
    return kernel_call(
        pack1_kernel, "pack1", (f, c, select),
        [vshape(GTOK, 2 * D)] + [pltpu.HBM(x.shape, x.dtype) for x in message_shapes()],
        in_hbm=2, scratch=[pltpu.SemaphoreType.DMA((4,))],
    )


def to_load(fc0, fc1, *sources):
    return kernel_call(
        load_kernel, "load", (fc0, fc1, *sources),
        [vshape(*x.shape, dtype=x.dtype) for x in sources] + [vshape(GTOK, 2 * D)] * 2,
        in_hbm=-len(sources), scratch=[pltpu.SemaphoreType.DMA((len(sources),))],
    )


def to_attend(group, place, *args):
    kept = [vshape(GTOK, D), vshape(GTOK, D)]
    results = [vshape(GTOK, D), vshape(GTOK, 3 * D)]
    inner = [
        pltpu.VMEM((GTOK, 3 * D), bf16),
        pltpu.VMEM((GTOK, D), bf16),
        pltpu.VMEM((4 * SPAN, 4 * SPAN), bf16),
    ]
    if group == 0:
        outs, scratch = kept + results, inner
    else:
        outs = results + [vshape(256, 4 * D), vshape(256, 4 * D)]
        scratch = [pltpu.VMEM((GTOK, D), bf16)] * 2 + inner + [pltpu.VMEM((D, 4 * D), f32)]
    return kernel_call(
        functools.partial(attend_kernel, group), "attend" + str(group), args, outs,
        place=place, scratch=scratch, loose=(2, 3, 4),
    )


def to_back(*args):
    return kernel_call(
        back_kernel, "back", args,
        [vshape(GTOK, 2 * D)] * 2 + [vshape(LAT, 2 * D)] * 2 + [vshape(2 * SIDE, 2 * D)] * 2,
        price=(2 * 10**9, 5 * 10**6),
    )


def to_finish(*args):
    return kernel_call(
        finish_kernel, "finish", args, [shape(TOK, D)] * 2, in_hbm=-4,
        scratch=[
            pltpu.VMEM((GTOK, 2 * D), bf16),
            pltpu.VMEM((GTOK, 2 * D), bf16),
            pltpu.VMEM((GTOK, GTOK), bf16),
            pltpu.VMEM((HALO, GTOK), bf16),
            pltpu.SemaphoreType.DMA((3, 4)),
        ],
        price=(2 * 10**9, 8 * 10**6),
    )


def add(*xs):
    total = xs[0].astype(f32)
    for x in xs[1:]:
        total = total + x.astype(f32)
    return total.astype(bf16)


def tied(x):
    return lax.optimization_barrier(x)


def halo_in(lat, lon, diag):
    return (
        lax.ppermute(lat, BOTH, shifted(-1, 0)),
        lax.ppermute(lon, BOTH, shifted(0, -1)),
        lax.ppermute(diag, BOTH, shifted(-1, -1)),
    )


def on_device(fields, cotangent, layer_norm_gain, qkv_weight, out_weight):
    a, b = lax.axis_index("lat"), lax.axis_index("lon")
    place = jnp.stack(
        [
            (a == 7).astype(jnp.int32),
            (a // 2).astype(jnp.int32),
            ((a % 2) * 2 + b // 16).astype(jnp.int32),
            (b % 2).astype(jnp.int32),
        ]
    )
    tables = [jnp.asarray(t, bf16) for t in gather_tables()]
    select_all = jnp.asarray(select_table(), bf16)
    f, c = fields.reshape(TOK, D), cotangent.reshape(TOK, D)
    fc0, select, *parts = to_pack0(f, c, select_all)
    halo0 = halo_in(*parts)
    fc1, *parts = to_pack1(f, c, select)
    local, table, w, o, gain, part0, part1 = to_load(
        fc0, fc1, *tables, qkv_weight, out_weight, layer_norm_gain.reshape(1, D)
    )
    gain, near, far, *parts = tied((gain, *halo0[1:], *parts))
    halo0, halo1 = (halo0[0], near, far), halo_in(*parts)
    normed0, ctw0, mixed0, gact0 = to_attend(0, place, part0, table, *halo0, gain, w, o)
    mixed1, gact1, own, other = to_attend(
        1, place, part1, table, *halo1, gain, w, o, normed0, ctw0, mixed0, gact0
    )

    there = send(other, to_sibling)
    part = [add(own[64 * k : 64 * k + 64], there[64 * k : 64 * k + 64]) for k in range(4)]
    mixed1, part = tied((mixed1, part))
    both0, both1, to_lat0, to_lat1, to_lon, to_diag = to_back(
        mixed0, mixed1, gact0, gact1, w, o, table
    )
    recv = [send(part[k], first_axis(k)) for k in (1, 2, 3)]
    recv, to_lat0 = tied((recv, to_lat0))
    part = add(part[0], *recv)
    part, to_lat0, to_lat1, to_lon, to_diag = tied((part, to_lat0, to_lat1, to_lon, to_diag))
    part = add(part[:16], *[send(part[16 * k : 16 * k + 16], second_axis(k)) for k in (1, 2, 3)])
    r_lat0 = lax.ppermute(to_lat0, BOTH, shifted(1, 0))
    r_lat1 = lax.ppermute(to_lat1, BOTH, shifted(1, 0))
    r_lon = lax.ppermute(to_lon, BOTH, shifted(0, 1))
    r_diag = lax.ppermute(to_diag, BOTH, shifted(1, 1))
    recv = send(part, flip_z(1))
    recv, r_lat0 = tied((recv, r_lat0))
    part = add(part, recv)
    recv = send(part, flip_z(2))
    recv, r_lat1 = tied((recv, r_lat1))
    part = add(part, recv)
    recv = send(part, flip_z(6))
    recv, r_lon, r_diag = tied((recv, r_lon, r_diag))
    part = add(part, recv)

    block = jnp.concatenate([part] + [send(part, second_axis(4 - s)) for s in (1, 2, 3)], axis=0)
    mine = [send(block, first_axis(4 - s)) for s in (1, 2, 3)]
    out, grad = to_finish(
        both0, both1, r_lat0, r_lat1, r_lon, r_diag, gain, f, c, tables[0], select_all
    )
    mine, out = tied((mine, out))
    mine = [block] + mine
    sibling = [send(m, to_sibling) for m in mine]
    g_qkv, g_out, total = to_weights(0, place, mine, w)
    g_qkv, g_out, g_gain = to_weights(1, place, sibling, w, vm(total), vm(gain), g_qkv, g_out)

    grid = (LEV, ROWS, COLS, D)
    return out.reshape(grid), grad.reshape(grid), g_qkv, g_out, g_gain.reshape(D)


def solution(mesh):
    return jax.shard_map(
        on_device,
        mesh=mesh,
        in_specs=(P(None, "lat", "lon", None), P(None, "lat", "lon", None), P(), P(), P()),
        out_specs=(P(None, "lat", "lon", None), P(None, "lat", "lon", None), P(), P(), P()),
        check_vma=False,
    )
```

```python
import functools
import math

import jax
import jax.numpy as jnp
import numpy as np
from jax import lax
from jax.experimental import pallas as pl
from jax.experimental.pallas import tpu as pltpu
from jax.sharding import PartitionSpec as P

HEADS = 8
LEV, ROWS, COLS = 4, 6, 24
WL, WR, WC = 2, 6, 12
D = 512
SPAN = WL * WR * WC
TOK = LEV * ROWS * COLS
BOTH = ("lat", "lon")
f32 = jnp.float32
bf16 = jnp.bfloat16
VMEM = 24 * 1024 * 1024


def index_of(y, x, z, c):
    return (y * 2 + x // 2) * 32 + (x % 2) * 16 + z * 2 + c


def place_of(i):
    return i // 64, ((i // 32) % 2) * 2 + (i // 16) % 2, (i // 2) % 8, i % 2


def route(step):
    return [(i, index_of(*step(*place_of(i)))) for i in range(256)]


def to_sibling(y, x, z, c):
    return y, x, z, 1 - c


def first_axis(k):
    return lambda y, x, z, c: ((y + k) % 4, x, z, c) if c == 0 else (y, (x + k) % 4, z, c)


def second_axis(k):
    return lambda y, x, z, c: (y, (x + k) % 4, z, c) if c == 0 else ((y + k) % 4, x, z, c)


def flip_z(k):
    return lambda y, x, z, c: (y, x, z ^ k, c)


def send(x, step):
    return lax.ppermute(x, BOTH, route(step))


def shifted(dlat, dlon):
    def pairs():
        out = []
        for i in range(256):
            a, b = i // 32, i % 32
            out.append((i, ((a + dlat) % 8) * 32 + (b + dlon) % 32))
        return out

    return pairs()


LAT, LON, HALO = 224, 80, 384


def gather_tables():
    local = np.zeros((TOK, TOK), np.float32)
    halo = np.zeros((TOK, HALO), np.float32)
    for lr in range(LEV):
        for rr in range(ROWS):
            for cr in range(COLS):
                w = (lr // WL) * (COLS // WC) + cr // WC
                t = w * SPAN + (lr % WL) * WR * WC + rr * WC + cr % WC
                lo, r, c = (lr + 1) % LEV, rr + 3, cr + 6
                if r < ROWS and c < COLS:
                    local[t, lo * ROWS * COLS + r * COLS + c] = 1
                elif c < COLS:
                    halo[t, lo * 54 + (r - ROWS) * 18 + c - 6] = 1
                elif r < ROWS:
                    halo[t, LAT + lo * 18 + (r - 3) * 6 + c - COLS] = 1
                else:
                    halo[t, LAT + LON + lo * 18 + (r - ROWS) * 6 + c - COLS] = 1
    return local, halo


def select_table():
    select = np.zeros((HALO, TOK), np.float32)
    for lv in range(LEV):
        for r in range(ROWS):
            for c in range(COLS):
                t = lv * ROWS * COLS + r * COLS + c
                if r < 3 and c >= 6:
                    select[lv * 54 + r * 18 + c - 6, t] = 1
                elif r >= 3 and c < 6:
                    select[LAT + lv * 18 + (r - 3) * 6 + c, t] = 1
                elif r < 3:
                    select[LAT + LON + lv * 18 + r * 6 + c, t] = 1
    return select


def dot(a, b, dims=((1,), (0,))):
    return lax.dot_general(a, b, (dims, ((), ())), preferred_element_type=f32)


NT = ((1,), (1,))
TN = ((0,), (0,))


def normalise(x):
    centred = x - jnp.mean(x, axis=-1, keepdims=True)
    rstd = lax.rsqrt(jnp.mean(centred * centred, axis=-1, keepdims=True) + 1e-5)
    return centred * rstd, rstd


def split(rows, lat, lon, diag):
    lat[...] = rows[:LAT].astype(bf16)
    lon[...] = rows[LAT : LAT + LON].astype(bf16)
    diag[...] = rows[LAT + LON :].astype(bf16)


def pack_kernel(f_hbm, c_hbm, s_hbm, f_vm, c_vm, s_vm, *refs):
    f_parts, c_parts, sem = refs[:3], refs[3:6], refs[6]
    pairs = ((s_hbm, s_vm), (f_hbm, f_vm), (c_hbm, c_vm))
    copies = [pltpu.make_async_copy(a, b, sem.at[i]) for i, (a, b) in enumerate(pairs)]
    for copy in copies:
        copy.start()
    copies[0].wait()
    copies[1].wait()
    split(dot(s_vm[...], f_vm[...]), *f_parts)
    copies[2].wait()
    split(dot(s_vm[...], c_vm[...]), *c_parts)


def load_kernel(f_vm, c_vm, *refs):
    sources, targets, (fw, cw, sem) = refs[:5], refs[5:10], refs[10:]
    copies = [
        pltpu.make_async_copy(a, b, sem.at[i]) for i, (a, b) in enumerate(zip(sources, targets))
    ]
    for copy in copies:
        copy.start()
    copies[0].wait()
    local = targets[0]
    fw[...] = dot(local[...], f_vm[...]).astype(bf16)
    cw[...] = dot(local[...], c_vm[...]).astype(bf16)
    for copy in copies[1:]:
        copy.wait()


GROUP = 4
WIDE = GROUP * (D // HEADS)


def group_mask(value=1.0):
    row = lax.broadcasted_iota(jnp.int32, (GROUP * SPAN, WIDE), 0)
    lane = lax.broadcasted_iota(jnp.int32, (GROUP * SPAN, WIDE), 1)
    first = lane // (D // HEADS) * SPAN
    return jnp.where((row >= first) & (row < first + SPAN), value, 0.0).astype(bf16)


def joined(r, factor=1.0):
    lane = lax.broadcasted_iota(jnp.int32, (SPAN, WIDE), 1)
    out = r[:SPAN]
    for h in range(1, GROUP):
        out = jnp.where(lane >= h * (D // HEADS), r[h * SPAN : (h + 1) * SPAN], out)
    return (out * factor).astype(bf16)


def repeated(x, pick):
    return jnp.concatenate([x] * GROUP, axis=0) * pick


def windows(part, table, lat, lon, diag):
    rows = jnp.concatenate([lat[...], lon[...], diag[...]], axis=0)
    return part[...].astype(f32) + dot(table[...], rows)


def forward_kernel(place, *refs):
    gain, w_ref, normed, qkv, probs, mixed = refs[5:]
    xhat, _ = normalise(windows(*refs[:5]))
    normed[...] = (xhat * gain[...]).astype(bf16)
    qkv[...] = dot(normed[...], w_ref[...]).astype(bf16)

    last_lat = place[0]
    long = 2 * SPAN
    low = lax.broadcasted_iota(jnp.int32, (SPAN, 128), 1) < 64
    row = lax.broadcasted_iota(jnp.int32, (long, 128), 0)
    lane = lax.broadcasted_iota(jnp.int32, (long, 128), 1)
    pick = jnp.where((row < SPAN) == (lane < 64), 1.0 / math.sqrt(D // HEADS), 0.0).astype(bf16)

    def lev_of(t):
        return (t >= SPAN // 2).astype(jnp.int32)

    def half_of(t):
        return (t - SPAN // 2 * lev_of(t) >= SPAN // 4).astype(jnp.int32)

    tq = lax.rem(lax.broadcasted_iota(jnp.int32, (SPAN, long), 1), SPAN)
    tk = lax.broadcasted_iota(jnp.int32, (SPAN, long), 0)
    lev_diff = jnp.abs(lev_of(tq) - lev_of(tk))
    half_diff = jnp.abs(half_of(tq) - half_of(tk)) * last_lat

    kinds = (half_diff == 0, (lev_diff + half_diff) == 0)
    for w in range(4):
        at = pl.ds(w * SPAN, SPAN)
        same = kinds[w // 2]
        for p in range(HEADS // 2):
            q_all = jnp.concatenate([qkv[at, pl.ds(128 * p, 128)]] * 2, axis=0) * pick
            k = qkv[at, pl.ds(D + 128 * p, 128)]
            v = qkv[at, pl.ds(2 * D + 128 * p, 128)]
            s = jnp.where(same, dot(k, q_all, NT), -1000000000.0)
            e = jnp.exp(s - jnp.max(s, axis=0, keepdims=True))
            rounded = (e * (1.0 / jnp.sum(e, axis=0, keepdims=True))).astype(bf16)
            probs[pl.ds((w * 2 + p // 2) * SPAN, SPAN), pl.ds(p % 2 * 2 * SPAN, 2 * SPAN)] = rounded
            r = dot(rounded, v, TN)
            mixed[at, pl.ds(128 * p, 128)] = jnp.where(low, r[:SPAN], r[SPAN:]).astype(bf16)


def backward_kernel(place, *refs):
    o_ref, normed, qkv, probs, mixed, gact, own, other, ctw, gm, acc = refs[5:]
    ctw[...] = windows(*refs[:5]).astype(bf16)
    gm[...] = dot(ctw[...], o_ref[...], NT).astype(bf16)
    long = GROUP * SPAN
    pick = group_mask()
    factor = 1.0 / math.sqrt(D // HEADS)
    scaled = group_mask(factor)

    def window(w, carry):
        at = pl.ds(pl.multiple_of(w * SPAN, SPAN), SPAN)
        for p in range(HEADS // GROUP):
            cols = pl.ds(WIDE * p, WIDE)
            q_all = repeated(qkv[at, cols], scaled)
            g_all = repeated(gm[at, cols], pick)
            k = qkv[at, pl.ds(D + WIDE * p, WIDE)]
            v = qkv[at, pl.ds(2 * D + WIDE * p, WIDE)]
            rounded = probs[pl.ds(pl.multiple_of((w * 2 + p) * SPAN, SPAN), SPAN), :]
            gact[at, pl.ds(2 * D + WIDE * p, WIDE)] = dot(rounded, g_all).astype(bf16)
            dp = dot(v, g_all, NT)
            pr = rounded.astype(f32)
            inner = jnp.sum(dp * pr, axis=0, keepdims=True)
            ds = (pr * (dp - inner)).astype(bf16)
            gact[at, cols] = joined(dot(ds, k, TN), factor)
            gact[at, pl.ds(D + WIDE * p, WIDE)] = dot(ds, q_all).astype(bf16)
        return carry

    lax.fori_loop(0, 4, window, 0, unroll=True)

    acc[:, : 3 * D] = dot(normed[...], gact[...], TN)
    acc[:, 3 * D :] = dot(mixed[...], ctw[...], TN)
    y, x, c = place[1], place[2], place[3]

    def fill(out, core):
        d1 = jnp.where(core == 0, y, x)
        d2 = jnp.where(core == 0, x, y)
        for s1 in range(4):
            for s2 in range(4):
                r = core * 256 + lax.rem(d1 + s1, 4) * 64 + lax.rem(d2 + s2, 4) * 16
                rows = acc[pl.ds(pl.multiple_of(r, 16), 16), :]
                out[pl.ds((s1 * 4 + s2) * 16, 16), :] = rows.astype(bf16)

    fill(own, c)
    fill(other, 1 - c)


def back_kernel(
    mixed, gact, w_ref, o_ref, p_halo, both, to_lat_p, to_lat_g, to_lon, to_diag
):
    both[:, :D] = dot(mixed[...], o_ref[...]).astype(bf16)
    both[:, D:] = dot(gact[...], w_ref[...], NT).astype(bf16)
    rows = dot(p_halo[...], both[...], TN)
    to_lat_p[...] = rows[:LAT, :D].astype(bf16)
    to_lat_g[...] = rows[:LAT, D:].astype(bf16)
    to_lon[...] = rows[LAT : LAT + LON].astype(bf16)
    to_diag[...] = rows[LAT + LON :].astype(bf16)


def finish_kernel(
    f_loc, c_loc, both, r_lat_p, r_lat_g, r_lon, r_diag, p_loc, select, gain, out, grad
):
    r_lat = jnp.concatenate([r_lat_p[...], r_lat_g[...]], axis=1)
    rows = jnp.concatenate([r_lat, r_lon[...], r_diag[...]], axis=0)
    grid = dot(p_loc[...], both[...], TN) + dot(select[...], rows, TN)
    x = f_loc[...].astype(f32)
    out[...] = (x + grid[:, :D]).astype(bf16)
    xhat, rstd = normalise(x)
    g = grid[:, D:] * gain[...]
    first = jnp.mean(g, axis=-1, keepdims=True)
    second = jnp.mean(g * xhat, axis=-1, keepdims=True)
    grad[...] = (c_loc[...].astype(f32) + rstd * (g - first - xhat * second)).astype(bf16)


def weights_kernel(side, place, *refs):
    pieces, refs = refs[:4], refs[4:]
    if side == 0:
        w_ref, g_qkv, g_out, g_total, buf_q, buf_o, sem = refs
    else:
        w_ref, before, gain, _, _, g_qkv, g_out, g_total, buf_q, buf_o, sem = refs
    y, x, c = place[1], place[2], place[3]
    core = c if side == 0 else 1 - c
    d1 = jnp.where(core == 0, y, x)
    d2 = jnp.where(core == 0, x, y)
    bands = [pl.multiple_of(core * 256 + lax.rem(d1 + i, 4) * 64, 64) for i in range(4)]
    copies = []
    for i in range(4):
        for s2 in range(4):
            at = pl.ds(pl.multiple_of(lax.rem(d2 + s2, 4) * 16, 16), 16)
            block = pieces[i][pl.ds(s2 * 16, 16), :].astype(f32)
            buf_q[i, at, :] = block[:, : 3 * D]
            buf_o[i, at, :] = block[:, 3 * D :]
        for k, (src, dst) in enumerate(((buf_q, g_qkv), (buf_o, g_out))):
            copy = pltpu.make_async_copy(src.at[i], dst.at[pl.ds(bands[i], 64)], sem.at[i, k])
            copy.start()
            copies.append(copy)
    total = jnp.zeros((1, D), f32) if side == 0 else before[...]
    lane = lax.broadcasted_iota(jnp.int32, (64, D), 1)
    local = lax.broadcasted_iota(jnp.int32, (64, D), 0)
    for i in range(4):
        w = w_ref[pl.ds(bands[i], 64), :].astype(f32)
        sums = jnp.sum(buf_q[i] * w, axis=1, keepdims=True)
        spread = jnp.where(lane == local + bands[i], sums, 0.0)
        total = total + jnp.sum(spread, axis=0, keepdims=True)
    g_total[...] = total if side == 0 else total / gain[...]
    for copy in copies:
        copy.wait()


def to_weights(side, place, pieces, qkv_weight, *more):
    inside = pl.BlockSpec(memory_space=pltpu.VMEM)
    anywhere = pl.BlockSpec(memory_space=pl.ANY)
    extra = [] if side == 0 else [inside, inside, anywhere, anywhere]
    return pl.pallas_call(
        functools.partial(weights_kernel, side),
        out_shape=[
            shape(D, 3 * D, dtype=f32),
            shape(D, D, dtype=f32),
            (vshape if side == 0 else shape)(1, D, dtype=f32),
        ],
        in_specs=spec(5, True) + extra,
        out_specs=[anywhere, anywhere, inside],
        scratch_shapes=[
            pltpu.VMEM((4, 64, 3 * D), f32),
            pltpu.VMEM((4, 64, D), f32),
            pltpu.SemaphoreType.DMA((4, 2)),
        ],
        input_output_aliases={} if side == 0 else {8: 0, 9: 1},
        compiler_params=params(),
        cost_estimate=cost(10**7, 4 * 10**6),
        name="weights" + str(side),
    )(place, *vms(*pieces), vm(qkv_weight), *more)


def params():
    return pltpu.CompilerParams(vmem_limit_bytes=VMEM)


def vm(x):
    return pltpu.with_memory_space_constraint(x, pltpu.VMEM)


def vms(*xs):
    return [vm(x) for x in xs]


def vshape(*dims, dtype=bf16):
    return pltpu.VMEM(dims, dtype)


def spec(count, scalar=False):
    whole = [pl.BlockSpec(memory_space=pltpu.VMEM)] * count
    return ([pl.BlockSpec(memory_space=pltpu.SMEM)] if scalar else []) + whole


def shape(*dims, dtype=bf16):
    return jax.ShapeDtypeStruct(dims, dtype)


def cost(flops, moved):
    return pl.CostEstimate(flops=flops, bytes_accessed=moved, transcendentals=0)


def halo_shapes(width):
    return [vshape(LAT, width), vshape(LON, width), vshape(HALO - LAT - LON, width)]


def to_pack(fields, cotangent, select):
    return pl.pallas_call(
        pack_kernel,
        out_shape=[vshape(TOK, D), vshape(TOK, D), vshape(HALO, TOK)] + halo_shapes(D) * 2,
        in_specs=[pl.BlockSpec(memory_space=pltpu.HBM)] * 3,
        out_specs=spec(9),
        scratch_shapes=[pltpu.SemaphoreType.DMA((3,))],
        compiler_params=params(),
        cost_estimate=cost(4 * 10**8, 2 * 10**6),
        name="pack",
    )(*[pltpu.with_memory_space_constraint(x, pltpu.HBM) for x in (fields, cotangent, select)])


def to_load(f_vm, c_vm, *sources):
    return pl.pallas_call(
        load_kernel,
        out_shape=[vshape(*x.shape, dtype=x.dtype) for x in sources]
        + [vshape(TOK, D), vshape(TOK, D)],
        in_specs=spec(2) + [pl.BlockSpec(memory_space=pltpu.HBM)] * 5,
        out_specs=spec(7),
        scratch_shapes=[pltpu.SemaphoreType.DMA((5,))],
        compiler_params=params(),
        cost_estimate=cost(10**6, 10**4),
        name="load",
    )(*vms(f_vm, c_vm), *[pltpu.with_memory_space_constraint(x, pltpu.HBM) for x in sources])


def to_forward(place, *args):
    return pl.pallas_call(
        forward_kernel,
        out_shape=[
            vshape(TOK, D), vshape(TOK, 3 * D), vshape(32 // GROUP * SPAN, GROUP * SPAN), vshape(TOK, D),
        ],
        in_specs=spec(7, True),
        out_specs=spec(4),
        compiler_params=params(),
        cost_estimate=cost(10**6, 10**4),
        name="forward",
    )(place, *vms(*args))


def to_backward(place, *args):
    return pl.pallas_call(
        backward_kernel,
        out_shape=[vshape(TOK, 3 * D), vshape(256, 4 * D), vshape(256, 4 * D)],
        in_specs=spec(10, True),
        out_specs=spec(3),
        scratch_shapes=[
            pltpu.VMEM((TOK, D), bf16),
            pltpu.VMEM((TOK, D), bf16),
            pltpu.VMEM((D, 4 * D), f32),
        ],
        compiler_params=params(),
        cost_estimate=cost(5 * 10**9, 10**7),
        name="backward",
    )(place, *vms(*args))


def to_back(*args):
    return pl.pallas_call(
        back_kernel,
        out_shape=[vshape(TOK, 2 * D), vshape(LAT, D), vshape(LAT, D)] + halo_shapes(2 * D)[1:],
        in_specs=spec(5),
        out_specs=spec(5),
        compiler_params=params(),
        cost_estimate=cost(2 * 10**9, 5 * 10**6),
        name="back",
    )(*vms(*args))


def to_finish(*args):
    return pl.pallas_call(
        finish_kernel,
        out_shape=[shape(TOK, D), shape(TOK, D)],
        in_specs=spec(10),
        out_specs=spec(2),
        compiler_params=params(),
        cost_estimate=cost(2 * 10**9, 8 * 10**6),
        name="finish",
    )(*vms(*args))


def add(*xs):
    total = xs[0].astype(f32)
    for x in xs[1:]:
        total = total + x.astype(f32)
    return total.astype(bf16)


def tied(x):
    return lax.optimization_barrier(x)


def halo_in(lat, lon, diag):
    return (
        lax.ppermute(lat, BOTH, shifted(-1, 0)),
        lax.ppermute(lon, BOTH, shifted(0, -1)),
        lax.ppermute(diag, BOTH, shifted(-1, -1)),
    )


def on_device(fields, cotangent, layer_norm_gain, qkv_weight, out_weight):
    a, b = lax.axis_index("lat"), lax.axis_index("lon")
    place = jnp.stack(
        [
            (a == 7).astype(jnp.int32),
            (a // 2).astype(jnp.int32),
            ((a % 2) * 2 + b // 16).astype(jnp.int32),
            (b % 2).astype(jnp.int32),
        ]
    )
    tables = [jnp.asarray(t, bf16) for t in gather_tables()]
    select = jnp.asarray(select_table(), bf16)
    f_vm, c_vm, select, *parts = to_pack(
        fields.reshape(TOK, D), cotangent.reshape(TOK, D), select
    )
    f_halo = halo_in(*parts[:3])
    p_loc, p_halo, w, o, gain, fw, cw = to_load(
        f_vm, c_vm, *tables, qkv_weight, out_weight, layer_norm_gain.reshape(1, D)
    )
    near, far, *parts = tied((*f_halo[1:], *parts[3:]))
    f_halo, c_halo = (f_halo[0], near, far), halo_in(*parts)
    normed, qkv, probs, mixed = to_forward(place, fw, p_halo, *f_halo, gain, w)
    gact, own, other = to_backward(
        place, cw, p_halo, *c_halo, o, normed, qkv, probs, mixed
    )

    there = send(other, to_sibling)
    part = [add(own[64 * k : 64 * k + 64], there[64 * k : 64 * k + 64]) for k in range(4)]
    mixed, gact, part = tied((mixed, gact, part))
    both, to_lat_p, to_lat_g, to_lon, to_diag = to_back(mixed, gact, w, o, p_halo)
    recv = [send(part[k], first_axis(k)) for k in (1, 2, 3)]
    recv, to_lon = tied((recv, to_lon))
    part = add(part[0], *recv)
    part, to_lat_p, to_lat_g, to_lon, to_diag = tied((part, to_lat_p, to_lat_g, to_lon, to_diag))
    part = add(part[:16], *[send(part[16 * k : 16 * k + 16], second_axis(k)) for k in (1, 2, 3)])
    r_lat_p = lax.ppermute(to_lat_p, BOTH, shifted(1, 0))
    r_lat_g = lax.ppermute(to_lat_g, BOTH, shifted(1, 0))
    r_lon = lax.ppermute(to_lon, BOTH, shifted(0, 1))
    r_diag = lax.ppermute(to_diag, BOTH, shifted(1, 1))
    recv = [send(part, flip_z(k)) for k in (1, 2, 3)]
    recv, r_lat_p, r_diag = tied((recv, r_lat_p, r_diag))
    part = add(part, *recv)
    recv = send(part, flip_z(6))
    recv, r_lat_g, r_lon = tied((recv, r_lat_g, r_lon))
    part = add(part, recv)

    block = jnp.concatenate([part] + [send(part, second_axis(4 - s)) for s in (1, 2, 3)], axis=0)
    mine = [send(block, first_axis(4 - s)) for s in (1, 2, 3)]
    out, grad = to_finish(
        f_vm, c_vm, both, r_lat_p, r_lat_g, r_lon, r_diag, p_loc, select, gain
    )
    mine, out = tied((mine, out))
    mine = [block] + mine
    sibling = [send(m, to_sibling) for m in mine]
    g_qkv, g_out, total = to_weights(0, place, mine, w)
    g_qkv, g_out, g_gain = to_weights(1, place, sibling, w, vm(total), vm(gain), g_qkv, g_out)

    grid = (LEV, ROWS, COLS, D)
    return out.reshape(grid), grad.reshape(grid), g_qkv, g_out, g_gain.reshape(D)


def solution(mesh):
    return jax.shard_map(
        on_device,
        mesh=mesh,
        in_specs=(P(None, "lat", "lon", None), P(None, "lat", "lon", None), P(), P(), P()),
        out_specs=(P(None, "lat", "lon", None), P(None, "lat", "lon", None), P(), P(), P()),
        check_vma=False,
    )
```

```python
import functools
import math

import jax
import jax.numpy as jnp
import numpy as np
from jax import lax
from jax.experimental import pallas as pl
from jax.experimental.pallas import tpu as pltpu
from jax.sharding import PartitionSpec as P

HEADS = 8
LEV, ROWS, COLS = 4, 6, 24
WL, WR, WC = 2, 6, 12
D = 512
SPAN = WL * WR * WC
TOK = LEV * ROWS * COLS
BOTH = ("lat", "lon")
f32 = jnp.float32
bf16 = jnp.bfloat16
VMEM = 24 * 1024 * 1024


def index_of(y, x, z, c):
    return (y * 2 + x // 2) * 32 + (x % 2) * 16 + z * 2 + c


def place_of(i):
    return i // 64, ((i // 32) % 2) * 2 + (i // 16) % 2, (i // 2) % 8, i % 2


def route(step):
    return [(i, index_of(*step(*place_of(i)))) for i in range(256)]


def to_sibling(y, x, z, c):
    return y, x, z, 1 - c


def first_axis(k):
    return lambda y, x, z, c: ((y + k) % 4, x, z, c) if c == 0 else (y, (x + k) % 4, z, c)


def second_axis(k):
    return lambda y, x, z, c: (y, (x + k) % 4, z, c) if c == 0 else ((y + k) % 4, x, z, c)


def flip_z(k):
    return lambda y, x, z, c: (y, x, z ^ k, c)


def send(x, step):
    return lax.ppermute(x, BOTH, route(step))


def shifted(dlat, dlon):
    def pairs():
        out = []
        for i in range(256):
            a, b = i // 32, i % 32
            out.append((i, ((a + dlat) % 8) * 32 + (b + dlon) % 32))
        return out

    return pairs()


LAT, LON, HALO = 224, 80, 384


def gather_tables():
    local = np.zeros((TOK, TOK), np.float32)
    halo = np.zeros((TOK, HALO), np.float32)
    for lr in range(LEV):
        for rr in range(ROWS):
            for cr in range(COLS):
                w = (lr // WL) * (COLS // WC) + cr // WC
                t = w * SPAN + (lr % WL) * WR * WC + rr * WC + cr % WC
                lo, r, c = (lr + 1) % LEV, rr + 3, cr + 6
                if r < ROWS and c < COLS:
                    local[t, lo * ROWS * COLS + r * COLS + c] = 1
                elif c < COLS:
                    halo[t, lo * 54 + (r - ROWS) * 18 + c - 6] = 1
                elif r < ROWS:
                    halo[t, LAT + lo * 18 + (r - 3) * 6 + c - COLS] = 1
                else:
                    halo[t, LAT + LON + lo * 18 + (r - ROWS) * 6 + c - COLS] = 1
    return local, halo


def select_table():
    select = np.zeros((HALO, TOK), np.float32)
    for lv in range(LEV):
        for r in range(ROWS):
            for c in range(COLS):
                t = lv * ROWS * COLS + r * COLS + c
                if r < 3 and c >= 6:
                    select[lv * 54 + r * 18 + c - 6, t] = 1
                elif r >= 3 and c < 6:
                    select[LAT + lv * 18 + (r - 3) * 6 + c, t] = 1
                elif r < 3:
                    select[LAT + LON + lv * 18 + r * 6 + c, t] = 1
    return select


def dot(a, b, dims=((1,), (0,))):
    return lax.dot_general(a, b, (dims, ((), ())), preferred_element_type=f32)


NT = ((1,), (1,))
TN = ((0,), (0,))


def normalise(x):
    centred = x - jnp.mean(x, axis=-1, keepdims=True)
    rstd = lax.rsqrt(jnp.mean(centred * centred, axis=-1, keepdims=True) + 1e-5)
    return centred * rstd, rstd


def split(rows, lat, lon, diag):
    lat[...] = rows[:LAT].astype(bf16)
    lon[...] = rows[LAT : LAT + LON].astype(bf16)
    diag[...] = rows[LAT + LON :].astype(bf16)


def pack_kernel(f_hbm, c_hbm, s_hbm, f_vm, c_vm, s_vm, *refs):
    f_parts, c_parts, sem = refs[:3], refs[3:6], refs[6]
    pairs = ((s_hbm, s_vm), (f_hbm, f_vm), (c_hbm, c_vm))
    copies = [pltpu.make_async_copy(a, b, sem.at[i]) for i, (a, b) in enumerate(pairs)]
    for copy in copies:
        copy.start()
    copies[0].wait()
    copies[1].wait()
    split(dot(s_vm[...], f_vm[...]), *f_parts)
    copies[2].wait()
    split(dot(s_vm[...], c_vm[...]), *c_parts)


def load_kernel(f_vm, c_vm, *refs):
    sources, targets, (fw, cw, sem) = refs[:5], refs[5:10], refs[10:]
    copies = [
        pltpu.make_async_copy(a, b, sem.at[i]) for i, (a, b) in enumerate(zip(sources, targets))
    ]
    for copy in copies:
        copy.start()
    copies[0].wait()
    local = targets[0]
    fw[...] = dot(local[...], f_vm[...]).astype(bf16)
    cw[...] = dot(local[...], c_vm[...]).astype(bf16)
    for copy in copies[1:]:
        copy.wait()


GROUP = 4
WIDE = GROUP * (D // HEADS)


def group_mask(value=1.0):
    row = lax.broadcasted_iota(jnp.int32, (GROUP * SPAN, WIDE), 0)
    lane = lax.broadcasted_iota(jnp.int32, (GROUP * SPAN, WIDE), 1)
    first = lane // (D // HEADS) * SPAN
    return jnp.where((row >= first) & (row < first + SPAN), value, 0.0).astype(bf16)


def joined(r, factor=1.0):
    lane = lax.broadcasted_iota(jnp.int32, (SPAN, WIDE), 1)
    out = r[:SPAN]
    for h in range(1, GROUP):
        out = jnp.where(lane >= h * (D // HEADS), r[h * SPAN : (h + 1) * SPAN], out)
    return (out * factor).astype(bf16)


def repeated(x, pick):
    return jnp.concatenate([x] * GROUP, axis=0) * pick


def windows(part, table, lat, lon, diag):
    rows = jnp.concatenate([lat[...], lon[...], diag[...]], axis=0)
    return part[...].astype(f32) + dot(table[...], rows)


def forward_kernel(place, *refs):
    gain, w_ref, normed, qkv, probs, mixed = refs[5:]
    xhat, _ = normalise(windows(*refs[:5]))
    normed[...] = (xhat * gain[...]).astype(bf16)
    qkv[...] = dot(normed[...], w_ref[...]).astype(bf16)

    last_lat = place[0]
    long = 2 * SPAN
    low = lax.broadcasted_iota(jnp.int32, (SPAN, 128), 1) < 64
    row = lax.broadcasted_iota(jnp.int32, (long, 128), 0)
    lane = lax.broadcasted_iota(jnp.int32, (long, 128), 1)
    pick = jnp.where((row < SPAN) == (lane < 64), 1.0 / math.sqrt(D // HEADS), 0.0).astype(bf16)

    def lev_of(t):
        return (t >= SPAN // 2).astype(jnp.int32)

    def half_of(t):
        return (t - SPAN // 2 * lev_of(t) >= SPAN // 4).astype(jnp.int32)

    tq = lax.rem(lax.broadcasted_iota(jnp.int32, (SPAN, long), 1), SPAN)
    tk = lax.broadcasted_iota(jnp.int32, (SPAN, long), 0)
    lev_diff = jnp.abs(lev_of(tq) - lev_of(tk))
    half_diff = jnp.abs(half_of(tq) - half_of(tk)) * last_lat

    kinds = (half_diff == 0, (lev_diff + half_diff) == 0)
    for w in range(4):
        at = pl.ds(w * SPAN, SPAN)
        same = kinds[w // 2]
        for p in range(HEADS // 2):
            q_all = jnp.concatenate([qkv[at, pl.ds(128 * p, 128)]] * 2, axis=0) * pick
            k = qkv[at, pl.ds(D + 128 * p, 128)]
            v = qkv[at, pl.ds(2 * D + 128 * p, 128)]
            s = jnp.where(same, dot(k, q_all, NT), -1000000000.0)
            e = jnp.exp(s - jnp.max(s, axis=0, keepdims=True))
            rounded = (e * (1.0 / jnp.sum(e, axis=0, keepdims=True))).astype(bf16)
            probs[pl.ds((w * 2 + p // 2) * SPAN, SPAN), pl.ds(p % 2 * 2 * SPAN, 2 * SPAN)] = rounded
            r = dot(rounded, v, TN)
            mixed[at, pl.ds(128 * p, 128)] = jnp.where(low, r[:SPAN], r[SPAN:]).astype(bf16)


def backward_kernel(place, *refs):
    o_ref, normed, qkv, probs, mixed, gact, own, other, ctw, gm, acc = refs[5:]
    ctw[...] = windows(*refs[:5]).astype(bf16)
    gm[...] = dot(ctw[...], o_ref[...], NT).astype(bf16)
    long = GROUP * SPAN
    pick = group_mask()
    factor = 1.0 / math.sqrt(D // HEADS)
    scaled = group_mask(factor)

    def window(w, carry):
        at = pl.ds(pl.multiple_of(w * SPAN, SPAN), SPAN)
        for p in range(HEADS // GROUP):
            cols = pl.ds(WIDE * p, WIDE)
            q_all = repeated(qkv[at, cols], scaled)
            g_all = repeated(gm[at, cols], pick)
            k = qkv[at, pl.ds(D + WIDE * p, WIDE)]
            v = qkv[at, pl.ds(2 * D + WIDE * p, WIDE)]
            rounded = probs[pl.ds(pl.multiple_of((w * 2 + p) * SPAN, SPAN), SPAN), :]
            gact[at, pl.ds(2 * D + WIDE * p, WIDE)] = dot(rounded, g_all).astype(bf16)
            dp = dot(v, g_all, NT)
            pr = rounded.astype(f32)
            inner = jnp.sum(dp * pr, axis=0, keepdims=True)
            ds = (pr * (dp - inner)).astype(bf16)
            gact[at, cols] = joined(dot(ds, k, TN), factor)
            gact[at, pl.ds(D + WIDE * p, WIDE)] = dot(ds, q_all).astype(bf16)
        return carry

    lax.fori_loop(0, 4, window, 0, unroll=True)

    acc[:, : 3 * D] = dot(normed[...], gact[...], TN)
    acc[:, 3 * D :] = dot(mixed[...], ctw[...], TN)
    y, x, c = place[1], place[2], place[3]

    def fill(out, core):
        d1 = jnp.where(core == 0, y, x)
        d2 = jnp.where(core == 0, x, y)
        for s1 in range(4):
            for s2 in range(4):
                r = core * 256 + lax.rem(d1 + s1, 4) * 64 + lax.rem(d2 + s2, 4) * 16
                rows = acc[pl.ds(pl.multiple_of(r, 16), 16), :]
                out[pl.ds((s1 * 4 + s2) * 16, 16), :] = rows.astype(bf16)

    fill(own, c)
    fill(other, 1 - c)


def back_kernel(mixed, gact, w_ref, o_ref, p_halo, both, to_lat, to_lon, to_diag):
    both[:, :D] = dot(mixed[...], o_ref[...]).astype(bf16)
    both[:, D:] = dot(gact[...], w_ref[...], NT).astype(bf16)
    split(dot(p_halo[...], both[...], TN), to_lat, to_lon, to_diag)


def finish_kernel(f_loc, c_loc, both, r_lat, r_lon, r_diag, p_loc, select, gain, out, grad):
    rows = jnp.concatenate([r_lat[...], r_lon[...], r_diag[...]], axis=0)
    grid = dot(p_loc[...], both[...], TN) + dot(select[...], rows, TN)
    x = f_loc[...].astype(f32)
    out[...] = (x + grid[:, :D]).astype(bf16)
    xhat, rstd = normalise(x)
    g = grid[:, D:] * gain[...]
    first = jnp.mean(g, axis=-1, keepdims=True)
    second = jnp.mean(g * xhat, axis=-1, keepdims=True)
    grad[...] = (c_loc[...].astype(f32) + rstd * (g - first - xhat * second)).astype(bf16)


def weights_kernel(side, place, *refs):
    pieces, refs = refs[:4], refs[4:]
    if side == 0:
        w_ref, g_qkv, g_out, g_total, buf_q, buf_o, sem = refs
    else:
        w_ref, before, gain, _, _, g_qkv, g_out, g_gain, buf_q, buf_o, sem, g_total = refs
    y, x, c = place[1], place[2], place[3]
    core = c if side == 0 else 1 - c
    d1 = jnp.where(core == 0, y, x)
    d2 = jnp.where(core == 0, x, y)
    bands = [pl.multiple_of(core * 256 + lax.rem(d1 + i, 4) * 64, 64) for i in range(4)]
    copies = []
    for i in range(4):
        for s2 in range(4):
            at = pl.ds(pl.multiple_of(lax.rem(d2 + s2, 4) * 16, 16), 16)
            block = pieces[i][pl.ds(s2 * 16, 16), :].astype(f32)
            buf_q[i, at, :] = block[:, : 3 * D]
            buf_o[i, at, :] = block[:, 3 * D :]
        for k, (src, dst) in enumerate(((buf_q, g_qkv), (buf_o, g_out))):
            copy = pltpu.make_async_copy(src.at[i], dst.at[pl.ds(bands[i], 64)], sem.at[i, k])
            copy.start()
            copies.append(copy)
    total = jnp.zeros((1, D), f32) if side == 0 else before[...]
    lane = lax.broadcasted_iota(jnp.int32, (64, D), 1)
    local = lax.broadcasted_iota(jnp.int32, (64, D), 0)
    for i in range(4):
        w = w_ref[pl.ds(bands[i], 64), :].astype(f32)
        sums = jnp.sum(buf_q[i] * w, axis=1, keepdims=True)
        spread = jnp.where(lane == local + bands[i], sums, 0.0)
        total = total + jnp.sum(spread, axis=0, keepdims=True)
    g_total[...] = total if side == 0 else total / gain[...]
    if side == 1:
        copies.append(pltpu.make_async_copy(g_total, g_gain, sem.at[4, 0]))
        copies[-1].start()
    for copy in copies:
        copy.wait()


def to_weights(side, place, pieces, qkv_weight, *more):
    inside = pl.BlockSpec(memory_space=pltpu.VMEM)
    anywhere = pl.BlockSpec(memory_space=pl.ANY)
    extra = [] if side == 0 else [inside, inside, anywhere, anywhere]
    return pl.pallas_call(
        functools.partial(weights_kernel, side),
        out_shape=[
            shape(D, 3 * D, dtype=f32),
            shape(D, D, dtype=f32),
            (vshape if side == 0 else shape)(1, D, dtype=f32),
        ],
        in_specs=spec(5, True) + extra,
        out_specs=[anywhere, anywhere, inside if side == 0 else anywhere],
        scratch_shapes=[
            pltpu.VMEM((4, 64, 3 * D), f32),
            pltpu.VMEM((4, 64, D), f32),
            pltpu.SemaphoreType.DMA((5, 2)),
        ]
        + ([] if side == 0 else [pltpu.VMEM((1, D), f32)]),
        input_output_aliases={} if side == 0 else {8: 0, 9: 1},
        compiler_params=params(),
        cost_estimate=cost(10**7, 4 * 10**6),
        name="weights" + str(side),
    )(place, *vms(*pieces), vm(qkv_weight), *more)


def params():
    return pltpu.CompilerParams(vmem_limit_bytes=VMEM)


def vm(x):
    return pltpu.with_memory_space_constraint(x, pltpu.VMEM)


def vms(*xs):
    return [vm(x) for x in xs]


def vshape(*dims, dtype=bf16):
    return pltpu.VMEM(dims, dtype)


def spec(count, scalar=False):
    whole = [pl.BlockSpec(memory_space=pltpu.VMEM)] * count
    return ([pl.BlockSpec(memory_space=pltpu.SMEM)] if scalar else []) + whole


def shape(*dims, dtype=bf16):
    return jax.ShapeDtypeStruct(dims, dtype)


def cost(flops, moved):
    return pl.CostEstimate(flops=flops, bytes_accessed=moved, transcendentals=0)


def halo_shapes(width):
    return [vshape(LAT, width), vshape(LON, width), vshape(HALO - LAT - LON, width)]


def to_pack(fields, cotangent, select):
    return pl.pallas_call(
        pack_kernel,
        out_shape=[vshape(TOK, D), vshape(TOK, D), vshape(HALO, TOK)] + halo_shapes(D) * 2,
        in_specs=[pl.BlockSpec(memory_space=pltpu.HBM)] * 3,
        out_specs=spec(9),
        scratch_shapes=[pltpu.SemaphoreType.DMA((3,))],
        compiler_params=params(),
        cost_estimate=cost(4 * 10**8, 2 * 10**6),
        name="pack",
    )(*[pltpu.with_memory_space_constraint(x, pltpu.HBM) for x in (fields, cotangent, select)])


def to_load(f_vm, c_vm, *sources):
    return pl.pallas_call(
        load_kernel,
        out_shape=[vshape(*x.shape, dtype=x.dtype) for x in sources]
        + [vshape(TOK, D), vshape(TOK, D)],
        in_specs=spec(2) + [pl.BlockSpec(memory_space=pltpu.HBM)] * 5,
        out_specs=spec(7),
        scratch_shapes=[pltpu.SemaphoreType.DMA((5,))],
        compiler_params=params(),
        cost_estimate=cost(10**6, 10**4),
        name="load",
    )(*vms(f_vm, c_vm), *[pltpu.with_memory_space_constraint(x, pltpu.HBM) for x in sources])


def to_forward(place, *args):
    return pl.pallas_call(
        forward_kernel,
        out_shape=[
            vshape(TOK, D), vshape(TOK, 3 * D), vshape(32 // GROUP * SPAN, GROUP * SPAN), vshape(TOK, D),
        ],
        in_specs=spec(7, True),
        out_specs=spec(4),
        compiler_params=params(),
        cost_estimate=cost(10**6, 10**4),
        name="forward",
    )(place, *vms(*args))


def to_backward(place, *args):
    return pl.pallas_call(
        backward_kernel,
        out_shape=[vshape(TOK, 3 * D), vshape(256, 4 * D), vshape(256, 4 * D)],
        in_specs=spec(10, True),
        out_specs=spec(3),
        scratch_shapes=[
            pltpu.VMEM((TOK, D), bf16),
            pltpu.VMEM((TOK, D), bf16),
            pltpu.VMEM((D, 4 * D), f32),
        ],
        compiler_params=params(),
        cost_estimate=cost(5 * 10**9, 10**7),
        name="backward",
    )(place, *vms(*args))


def to_back(*args):
    return pl.pallas_call(
        back_kernel,
        out_shape=[vshape(TOK, 2 * D)] + halo_shapes(2 * D),
        in_specs=spec(5),
        out_specs=spec(4),
        compiler_params=params(),
        cost_estimate=cost(2 * 10**9, 5 * 10**6),
        name="back",
    )(*vms(*args))


def to_finish(*args):
    return pl.pallas_call(
        finish_kernel,
        out_shape=[shape(TOK, D), shape(TOK, D)],
        in_specs=spec(9),
        out_specs=spec(2),
        compiler_params=params(),
        cost_estimate=cost(2 * 10**9, 8 * 10**6),
        name="finish",
    )(*vms(*args))


def add(*xs):
    total = xs[0].astype(f32)
    for x in xs[1:]:
        total = total + x.astype(f32)
    return total.astype(bf16)


def tied(x):
    return lax.optimization_barrier(x)


def halo_in(lat, lon, diag):
    return (
        lax.ppermute(lat, BOTH, shifted(-1, 0)),
        lax.ppermute(lon, BOTH, shifted(0, -1)),
        lax.ppermute(diag, BOTH, shifted(-1, -1)),
    )


def on_device(fields, cotangent, layer_norm_gain, qkv_weight, out_weight):
    a, b = lax.axis_index("lat"), lax.axis_index("lon")
    place = jnp.stack(
        [
            (a == 7).astype(jnp.int32),
            (a // 2).astype(jnp.int32),
            ((a % 2) * 2 + b // 16).astype(jnp.int32),
            (b % 2).astype(jnp.int32),
        ]
    )
    tables = [jnp.asarray(t, bf16) for t in gather_tables()]
    select = jnp.asarray(select_table(), bf16)
    f_vm, c_vm, select, *parts = to_pack(
        fields.reshape(TOK, D), cotangent.reshape(TOK, D), select
    )
    f_halo = halo_in(*parts[:3])
    c_halo = halo_in(*parts[3:])
    p_loc, p_halo, w, o, gain, fw, cw = to_load(
        f_vm, c_vm, *tables, qkv_weight, out_weight, layer_norm_gain.reshape(1, D)
    )
    normed, qkv, probs, mixed = to_forward(place, fw, p_halo, *f_halo, gain, w)
    gact, own, other = to_backward(
        place, cw, p_halo, *c_halo, o, normed, qkv, probs, mixed
    )

    there = send(other, to_sibling)
    part = [add(own[64 * k : 64 * k + 64], there[64 * k : 64 * k + 64]) for k in range(4)]
    mixed, gact, part = tied((mixed, gact, part))
    both, to_lat, to_lon, to_diag = to_back(mixed, gact, w, o, p_halo)
    recv = [send(part[k], first_axis(k)) for k in (1, 2, 3)]
    recv, to_lat = tied((recv, to_lat))
    part = add(part[0], *recv)
    part, to_lat, to_lon, to_diag = tied((part, to_lat, to_lon, to_diag))
    part = add(part[:16], *[send(part[16 * k : 16 * k + 16], second_axis(k)) for k in (1, 2, 3)])
    r_lat = lax.ppermute(to_lat, BOTH, shifted(1, 0))
    r_lon = lax.ppermute(to_lon, BOTH, shifted(0, 1))
    r_diag = lax.ppermute(to_diag, BOTH, shifted(1, 1))
    recv = send(part, flip_z(1))
    recv, r_diag = tied((recv, r_diag))
    part = add(part, recv)
    recv = send(part, flip_z(2))
    recv, r_lon = tied((recv, r_lon))
    part = add(part, recv)
    recv = send(part, flip_z(6))
    recv, r_lat = tied((recv, r_lat))
    part = add(part, recv)

    block = jnp.concatenate([part] + [send(part, second_axis(4 - s)) for s in (1, 2, 3)], axis=0)
    mine = [send(block, first_axis(4 - s)) for s in (1, 2, 3)]
    out, grad = to_finish(f_vm, c_vm, both, r_lat, r_lon, r_diag, p_loc, select, gain)
    mine, out = tied((mine, out))
    mine = [block] + mine
    sibling = [send(m, to_sibling) for m in mine]
    g_qkv, g_out, total = to_weights(0, place, mine, w)
    g_qkv, g_out, g_gain = to_weights(1, place, sibling, w, vm(total), vm(gain), g_qkv, g_out)

    grid = (LEV, ROWS, COLS, D)
    return out.reshape(grid), grad.reshape(grid), g_qkv, g_out, g_gain.reshape(D)


def solution(mesh):
    return jax.shard_map(
        on_device,
        mesh=mesh,
        in_specs=(P(None, "lat", "lon", None), P(None, "lat", "lon", None), P(), P(), P()),
        out_specs=(P(None, "lat", "lon", None), P(None, "lat", "lon", None), P(), P(), P()),
        check_vma=False,
    )
```

```python
import functools
import math

import jax
import jax.numpy as jnp
import numpy as np
from jax import lax
from jax.experimental import pallas as pl
from jax.experimental.pallas import tpu as pltpu
from jax.sharding import PartitionSpec as P

HEADS = 8
LEV, ROWS, COLS = 4, 6, 24
WL, WR, WC = 2, 6, 12
D = 512
SPAN = WL * WR * WC
TOK = LEV * ROWS * COLS
BOTH = ("lat", "lon")
f32 = jnp.float32
bf16 = jnp.bfloat16
VMEM = 24 * 1024 * 1024


def index_of(y, x, z, c):
    return (y * 2 + x // 2) * 32 + (x % 2) * 16 + z * 2 + c


def place_of(i):
    return i // 64, ((i // 32) % 2) * 2 + (i // 16) % 2, (i // 2) % 8, i % 2


def route(step):
    return [(i, index_of(*step(*place_of(i)))) for i in range(256)]


def to_sibling(y, x, z, c):
    return y, x, z, 1 - c


def first_axis(k):
    return lambda y, x, z, c: ((y + k) % 4, x, z, c) if c == 0 else (y, (x + k) % 4, z, c)


def second_axis(k):
    return lambda y, x, z, c: (y, (x + k) % 4, z, c) if c == 0 else ((y + k) % 4, x, z, c)


def flip_z(k):
    return lambda y, x, z, c: (y, x, z ^ k, c)


def send(x, step):
    return lax.ppermute(x, BOTH, route(step))


def shifted(dlat, dlon):
    def pairs():
        out = []
        for i in range(256):
            a, b = i // 32, i % 32
            out.append((i, ((a + dlat) % 8) * 32 + (b + dlon) % 32))
        return out

    return pairs()


LAT, LON, HALO = 224, 80, 384


def gather_tables():
    local = np.zeros((TOK, TOK), np.float32)
    halo = np.zeros((TOK, HALO), np.float32)
    for lr in range(LEV):
        for rr in range(ROWS):
            for cr in range(COLS):
                w = (lr // WL) * (COLS // WC) + cr // WC
                t = w * SPAN + (lr % WL) * WR * WC + rr * WC + cr % WC
                lo, r, c = (lr + 1) % LEV, rr + 3, cr + 6
                if r < ROWS and c < COLS:
                    local[t, lo * ROWS * COLS + r * COLS + c] = 1
                elif c < COLS:
                    halo[t, lo * 54 + (r - ROWS) * 18 + c - 6] = 1
                elif r < ROWS:
                    halo[t, LAT + lo * 18 + (r - 3) * 6 + c - COLS] = 1
                else:
                    halo[t, LAT + LON + lo * 18 + (r - ROWS) * 6 + c - COLS] = 1
    return local, halo


def select_table():
    select = np.zeros((HALO, TOK), np.float32)
    for lv in range(LEV):
        for r in range(ROWS):
            for c in range(COLS):
                t = lv * ROWS * COLS + r * COLS + c
                if r < 3 and c >= 6:
                    select[lv * 54 + r * 18 + c - 6, t] = 1
                elif r >= 3 and c < 6:
                    select[LAT + lv * 18 + (r - 3) * 6 + c, t] = 1
                elif r < 3:
                    select[LAT + LON + lv * 18 + r * 6 + c, t] = 1
    return select


def dot(a, b, dims=((1,), (0,))):
    return lax.dot_general(a, b, (dims, ((), ())), preferred_element_type=f32)


NT = ((1,), (1,))
TN = ((0,), (0,))


def normalise(x):
    centred = x - jnp.mean(x, axis=-1, keepdims=True)
    rstd = lax.rsqrt(jnp.mean(centred * centred, axis=-1, keepdims=True) + 1e-5)
    return centred * rstd, rstd


def split(rows, lat, lon, diag):
    lat[...] = rows[:LAT].astype(bf16)
    lon[...] = rows[LAT : LAT + LON].astype(bf16)
    diag[...] = rows[LAT + LON :].astype(bf16)


def pack_kernel(f_hbm, c_hbm, s_hbm, f_vm, c_vm, s_vm, *refs):
    f_parts, c_parts, sem = refs[:3], refs[3:6], refs[6]
    pairs = ((s_hbm, s_vm), (f_hbm, f_vm), (c_hbm, c_vm))
    copies = [pltpu.make_async_copy(a, b, sem.at[i]) for i, (a, b) in enumerate(pairs)]
    for copy in copies:
        copy.start()
    copies[0].wait()
    copies[1].wait()
    split(dot(s_vm[...], f_vm[...]), *f_parts)
    copies[2].wait()
    split(dot(s_vm[...], c_vm[...]), *c_parts)


def load_kernel(f_vm, c_vm, *refs):
    sources, targets, (fw, cw, sem) = refs[:5], refs[5:10], refs[10:]
    copies = [
        pltpu.make_async_copy(a, b, sem.at[i]) for i, (a, b) in enumerate(zip(sources, targets))
    ]
    for copy in copies:
        copy.start()
    copies[0].wait()
    local = targets[0]
    fw[...] = dot(local[...], f_vm[...]).astype(bf16)
    cw[...] = dot(local[...], c_vm[...]).astype(bf16)
    for copy in copies[1:]:
        copy.wait()


GROUP = 4
WIDE = GROUP * (D // HEADS)


def group_mask(value=1.0):
    row = lax.broadcasted_iota(jnp.int32, (GROUP * SPAN, WIDE), 0)
    lane = lax.broadcasted_iota(jnp.int32, (GROUP * SPAN, WIDE), 1)
    first = lane // (D // HEADS) * SPAN
    return jnp.where((row >= first) & (row < first + SPAN), value, 0.0).astype(bf16)


def joined(r, factor=1.0):
    lane = lax.broadcasted_iota(jnp.int32, (SPAN, WIDE), 1)
    out = r[:SPAN]
    for h in range(1, GROUP):
        out = jnp.where(lane >= h * (D // HEADS), r[h * SPAN : (h + 1) * SPAN], out)
    return (out * factor).astype(bf16)


def repeated(x, pick):
    return jnp.concatenate([x] * GROUP, axis=0) * pick


def windows(part, table, lat, lon, diag):
    rows = jnp.concatenate([lat[...], lon[...], diag[...]], axis=0)
    return part[...].astype(f32) + dot(table[...], rows)


def forward_kernel(place, *refs):
    gain, w_ref, normed, qkv, probs, mixed = refs[5:]
    xhat, _ = normalise(windows(*refs[:5]))
    normed[...] = (xhat * gain[...]).astype(bf16)
    qkv[...] = dot(normed[...], w_ref[...]).astype(bf16)

    last_lat = place[0]
    long = 2 * SPAN
    low = lax.broadcasted_iota(jnp.int32, (SPAN, 128), 1) < 64
    row = lax.broadcasted_iota(jnp.int32, (long, 128), 0)
    lane = lax.broadcasted_iota(jnp.int32, (long, 128), 1)
    pick = jnp.where((row < SPAN) == (lane < 64), 1.0 / math.sqrt(D // HEADS), 0.0).astype(bf16)

    def lev_of(t):
        return (t >= SPAN // 2).astype(jnp.int32)

    def half_of(t):
        return (t - SPAN // 2 * lev_of(t) >= SPAN // 4).astype(jnp.int32)

    tq = lax.rem(lax.broadcasted_iota(jnp.int32, (SPAN, long), 1), SPAN)
    tk = lax.broadcasted_iota(jnp.int32, (SPAN, long), 0)
    lev_diff = jnp.abs(lev_of(tq) - lev_of(tk))
    half_diff = jnp.abs(half_of(tq) - half_of(tk)) * last_lat

    kinds = (half_diff == 0, (lev_diff + half_diff) == 0)
    for w in range(4):
        at = pl.ds(w * SPAN, SPAN)
        same = kinds[w // 2]
        for p in range(HEADS // 2):
            q_all = jnp.concatenate([qkv[at, pl.ds(128 * p, 128)]] * 2, axis=0) * pick
            k = qkv[at, pl.ds(D + 128 * p, 128)]
            v = qkv[at, pl.ds(2 * D + 128 * p, 128)]
            s = jnp.where(same, dot(k, q_all, NT), -1000000000.0)
            e = jnp.exp(s - jnp.max(s, axis=0, keepdims=True))
            rounded = (e * (1.0 / jnp.sum(e, axis=0, keepdims=True))).astype(bf16)
            probs[pl.ds((w * 2 + p // 2) * SPAN, SPAN), pl.ds(p % 2 * 2 * SPAN, 2 * SPAN)] = rounded
            r = dot(rounded, v, TN)
            mixed[at, pl.ds(128 * p, 128)] = jnp.where(low, r[:SPAN], r[SPAN:]).astype(bf16)


def backward_kernel(place, *refs):
    o_ref, normed, qkv, probs, mixed, gact, own, other, ctw, gm, acc = refs[5:]
    ctw[...] = windows(*refs[:5]).astype(bf16)
    gm[...] = dot(ctw[...], o_ref[...], NT).astype(bf16)
    long = GROUP * SPAN
    pick = group_mask()
    factor = 1.0 / math.sqrt(D // HEADS)
    scaled = group_mask(factor)

    def window(w, carry):
        at = pl.ds(pl.multiple_of(w * SPAN, SPAN), SPAN)
        for p in range(HEADS // GROUP):
            cols = pl.ds(WIDE * p, WIDE)
            q_all = repeated(qkv[at, cols], scaled)
            g_all = repeated(gm[at, cols], pick)
            k = qkv[at, pl.ds(D + WIDE * p, WIDE)]
            v = qkv[at, pl.ds(2 * D + WIDE * p, WIDE)]
            rounded = probs[pl.ds(pl.multiple_of((w * 2 + p) * SPAN, SPAN), SPAN), :]
            gact[at, pl.ds(2 * D + WIDE * p, WIDE)] = dot(rounded, g_all).astype(bf16)
            dp = dot(v, g_all, NT)
            pr = rounded.astype(f32)
            inner = jnp.sum(dp * pr, axis=0, keepdims=True)
            ds = (pr * (dp - inner)).astype(bf16)
            gact[at, cols] = joined(dot(ds, k, TN), factor)
            gact[at, pl.ds(D + WIDE * p, WIDE)] = dot(ds, q_all).astype(bf16)
        return carry

    lax.fori_loop(0, 4, window, 0, unroll=True)

    acc[:, : 3 * D] = dot(normed[...], gact[...], TN)
    acc[:, 3 * D :] = dot(mixed[...], ctw[...], TN)
    y, x, c = place[1], place[2], place[3]

    def fill(out, core):
        d1 = jnp.where(core == 0, y, x)
        d2 = jnp.where(core == 0, x, y)
        for s1 in range(4):
            for s2 in range(4):
                r = core * 256 + lax.rem(d1 + s1, 4) * 64 + lax.rem(d2 + s2, 4) * 16
                rows = acc[pl.ds(pl.multiple_of(r, 16), 16), :]
                out[pl.ds((s1 * 4 + s2) * 16, 16), :] = rows.astype(bf16)

    fill(own, c)
    fill(other, 1 - c)


def back_kernel(mixed, gact, w_ref, o_ref, p_halo, both, to_lat, to_lon, to_diag):
    both[:, :D] = dot(mixed[...], o_ref[...]).astype(bf16)
    both[:, D:] = dot(gact[...], w_ref[...], NT).astype(bf16)
    split(dot(p_halo[...], both[...], TN), to_lat, to_lon, to_diag)


def finish_kernel(f_loc, c_loc, both, r_lat, r_lon, r_diag, p_loc, select, gain, out, grad):
    rows = jnp.concatenate([r_lat[...], r_lon[...], r_diag[...]], axis=0)
    grid = dot(p_loc[...], both[...], TN) + dot(select[...], rows, TN)
    x = f_loc[...].astype(f32)
    out[...] = (x + grid[:, :D]).astype(bf16)
    xhat, rstd = normalise(x)
    g = grid[:, D:] * gain[...]
    first = jnp.mean(g, axis=-1, keepdims=True)
    second = jnp.mean(g * xhat, axis=-1, keepdims=True)
    grad[...] = (c_loc[...].astype(f32) + rstd * (g - first - xhat * second)).astype(bf16)


def weights_kernel(side, place, *refs):
    pieces, refs = refs[:4], refs[4:]
    if side == 0:
        w_ref, g_qkv, g_out, g_total, buf_q, buf_o, sem = refs
    else:
        w_ref, before, gain, _, _, g_qkv, g_out, g_gain, buf_q, buf_o, sem, g_total = refs
    y, x, c = place[1], place[2], place[3]
    core = c if side == 0 else 1 - c
    d1 = jnp.where(core == 0, y, x)
    d2 = jnp.where(core == 0, x, y)
    bands = [pl.multiple_of(core * 256 + lax.rem(d1 + i, 4) * 64, 64) for i in range(4)]
    copies = []
    for i in range(4):
        for s2 in range(4):
            at = pl.ds(pl.multiple_of(lax.rem(d2 + s2, 4) * 16, 16), 16)
            block = pieces[i][pl.ds(s2 * 16, 16), :].astype(f32)
            buf_q[i, at, :] = block[:, : 3 * D]
            buf_o[i, at, :] = block[:, 3 * D :]
        for k, (src, dst) in enumerate(((buf_q, g_qkv), (buf_o, g_out))):
            copy = pltpu.make_async_copy(src.at[i], dst.at[pl.ds(bands[i], 64)], sem.at[i, k])
            copy.start()
            copies.append(copy)
    total = jnp.zeros((1, D), f32) if side == 0 else before[...]
    lane = lax.broadcasted_iota(jnp.int32, (64, D), 1)
    local = lax.broadcasted_iota(jnp.int32, (64, D), 0)
    for i in range(4):
        w = w_ref[pl.ds(bands[i], 64), :].astype(f32)
        sums = jnp.sum(buf_q[i] * w, axis=1, keepdims=True)
        spread = jnp.where(lane == local + bands[i], sums, 0.0)
        total = total + jnp.sum(spread, axis=0, keepdims=True)
    g_total[...] = total if side == 0 else total / gain[...]
    if side == 1:
        copies.append(pltpu.make_async_copy(g_total, g_gain, sem.at[4, 0]))
        copies[-1].start()
    for copy in copies:
        copy.wait()


def to_weights(side, place, pieces, qkv_weight, *more):
    inside = pl.BlockSpec(memory_space=pltpu.VMEM)
    anywhere = pl.BlockSpec(memory_space=pl.ANY)
    extra = [] if side == 0 else [inside, inside, anywhere, anywhere]
    return pl.pallas_call(
        functools.partial(weights_kernel, side),
        out_shape=[
            shape(D, 3 * D, dtype=f32),
            shape(D, D, dtype=f32),
            (vshape if side == 0 else shape)(1, D, dtype=f32),
        ],
        in_specs=spec(5, True) + extra,
        out_specs=[anywhere, anywhere, inside if side == 0 else anywhere],
        scratch_shapes=[
            pltpu.VMEM((4, 64, 3 * D), f32),
            pltpu.VMEM((4, 64, D), f32),
            pltpu.SemaphoreType.DMA((5, 2)),
        ]
        + ([] if side == 0 else [pltpu.VMEM((1, D), f32)]),
        input_output_aliases={} if side == 0 else {8: 0, 9: 1},
        compiler_params=params(),
        cost_estimate=cost(10**7, 4 * 10**6),
        name="weights" + str(side),
    )(place, *vms(*pieces), vm(qkv_weight), *more)


def params():
    return pltpu.CompilerParams(vmem_limit_bytes=VMEM)


def vm(x):
    return pltpu.with_memory_space_constraint(x, pltpu.VMEM)


def vms(*xs):
    return [vm(x) for x in xs]


def vshape(*dims, dtype=bf16):
    return pltpu.VMEM(dims, dtype)


def spec(count, scalar=False):
    whole = [pl.BlockSpec(memory_space=pltpu.VMEM)] * count
    return ([pl.BlockSpec(memory_space=pltpu.SMEM)] if scalar else []) + whole


def shape(*dims, dtype=bf16):
    return jax.ShapeDtypeStruct(dims, dtype)


def cost(flops, moved):
    return pl.CostEstimate(flops=flops, bytes_accessed=moved, transcendentals=0)


def halo_shapes(width):
    return [vshape(LAT, width), vshape(LON, width), vshape(HALO - LAT - LON, width)]


def to_pack(fields, cotangent, select):
    return pl.pallas_call(
        pack_kernel,
        out_shape=[vshape(TOK, D), vshape(TOK, D), vshape(HALO, TOK)] + halo_shapes(D) * 2,
        in_specs=[pl.BlockSpec(memory_space=pltpu.HBM)] * 3,
        out_specs=spec(9),
        scratch_shapes=[pltpu.SemaphoreType.DMA((3,))],
        compiler_params=params(),
        cost_estimate=cost(4 * 10**8, 2 * 10**6),
        name="pack",
    )(*[pltpu.with_memory_space_constraint(x, pltpu.HBM) for x in (fields, cotangent, select)])


def to_load(f_vm, c_vm, *sources):
    return pl.pallas_call(
        load_kernel,
        out_shape=[vshape(*x.shape, dtype=x.dtype) for x in sources]
        + [vshape(TOK, D), vshape(TOK, D)],
        in_specs=spec(2) + [pl.BlockSpec(memory_space=pltpu.HBM)] * 5,
        out_specs=spec(7),
        scratch_shapes=[pltpu.SemaphoreType.DMA((5,))],
        compiler_params=params(),
        cost_estimate=cost(10**6, 10**4),
        name="load",
    )(*vms(f_vm, c_vm), *[pltpu.with_memory_space_constraint(x, pltpu.HBM) for x in sources])


def to_forward(place, *args):
    return pl.pallas_call(
        forward_kernel,
        out_shape=[
            vshape(TOK, D), vshape(TOK, 3 * D), vshape(32 // GROUP * SPAN, GROUP * SPAN), vshape(TOK, D),
        ],
        in_specs=spec(7, True),
        out_specs=spec(4),
        compiler_params=params(),
        cost_estimate=cost(10**6, 10**4),
        name="forward",
    )(place, *vms(*args))


def to_backward(place, *args):
    return pl.pallas_call(
        backward_kernel,
        out_shape=[vshape(TOK, 3 * D), vshape(256, 4 * D), vshape(256, 4 * D)],
        in_specs=spec(10, True),
        out_specs=spec(3),
        scratch_shapes=[
            pltpu.VMEM((TOK, D), bf16),
            pltpu.VMEM((TOK, D), bf16),
            pltpu.VMEM((D, 4 * D), f32),
        ],
        compiler_params=params(),
        cost_estimate=cost(5 * 10**9, 10**7),
        name="backward",
    )(place, *vms(*args))


def to_back(*args):
    return pl.pallas_call(
        back_kernel,
        out_shape=[vshape(TOK, 2 * D)] + halo_shapes(2 * D),
        in_specs=spec(5),
        out_specs=spec(4),
        compiler_params=params(),
        cost_estimate=cost(2 * 10**9, 5 * 10**6),
        name="back",
    )(*vms(*args))


def to_finish(*args):
    return pl.pallas_call(
        finish_kernel,
        out_shape=[shape(TOK, D), shape(TOK, D)],
        in_specs=spec(9),
        out_specs=spec(2),
        compiler_params=params(),
        cost_estimate=cost(2 * 10**9, 8 * 10**6),
        name="finish",
    )(*vms(*args))


def add(*xs):
    total = xs[0].astype(f32)
    for x in xs[1:]:
        total = total + x.astype(f32)
    return total.astype(bf16)


def tied(x):
    return lax.optimization_barrier(x)


def halo_in(lat, lon, diag):
    return (
        lax.ppermute(lat, BOTH, shifted(-1, 0)),
        lax.ppermute(lon, BOTH, shifted(0, -1)),
        lax.ppermute(diag, BOTH, shifted(-1, -1)),
    )


def on_device(fields, cotangent, layer_norm_gain, qkv_weight, out_weight):
    a, b = lax.axis_index("lat"), lax.axis_index("lon")
    place = jnp.stack(
        [
            (a == 7).astype(jnp.int32),
            (a // 2).astype(jnp.int32),
            ((a % 2) * 2 + b // 16).astype(jnp.int32),
            (b % 2).astype(jnp.int32),
        ]
    )
    tables = [jnp.asarray(t, bf16) for t in gather_tables()]
    select = jnp.asarray(select_table(), bf16)
    f_vm, c_vm, select, *parts = to_pack(
        fields.reshape(TOK, D), cotangent.reshape(TOK, D), select
    )
    f_halo = halo_in(*parts[:3])
    c_halo = halo_in(*parts[3:])
    p_loc, p_halo, w, o, gain, fw, cw = to_load(
        f_vm, c_vm, *tables, qkv_weight, out_weight, layer_norm_gain.reshape(1, D)
    )
    normed, qkv, probs, mixed = to_forward(place, fw, p_halo, *f_halo, gain, w)
    gact, own, other = to_backward(
        place, cw, p_halo, *c_halo, o, normed, qkv, probs, mixed
    )

    there = send(other, to_sibling)
    part = [add(own[64 * k : 64 * k + 64], there[64 * k : 64 * k + 64]) for k in range(4)]
    mixed, gact, part = tied((mixed, gact, part))
    both, to_lat, to_lon, to_diag = to_back(mixed, gact, w, o, p_halo)
    recv = [send(part[k], first_axis(k)) for k in (1, 2, 3)]
    recv, to_lat = tied((recv, to_lat))
    part = add(part[0], *recv)
    part, to_lat, to_lon, to_diag = tied((part, to_lat, to_lon, to_diag))
    part = add(part[:16], *[send(part[16 * k : 16 * k + 16], second_axis(k)) for k in (1, 2, 3)])
    r_lat = lax.ppermute(to_lat, BOTH, shifted(1, 0))
    r_lon = lax.ppermute(to_lon, BOTH, shifted(0, 1))
    r_diag = lax.ppermute(to_diag, BOTH, shifted(1, 1))
    recv = send(part, flip_z(1))
    recv, r_lon = tied((recv, r_lon))
    part = add(part, recv)
    recv = send(part, flip_z(2))
    recv, r_diag = tied((recv, r_diag))
    part = add(part, recv)
    recv = send(part, flip_z(6))
    recv, r_lat = tied((recv, r_lat))
    part = add(part, recv)

    block = jnp.concatenate([part] + [send(part, second_axis(4 - s)) for s in (1, 2, 3)], axis=0)
    mine = [send(block, first_axis(4 - s)) for s in (1, 2, 3)]
    out, grad = to_finish(f_vm, c_vm, both, r_lat, r_lon, r_diag, p_loc, select, gain)
    mine, out = tied((mine, out))
    mine = [block] + mine
    sibling = [send(m, to_sibling) for m in mine]
    g_qkv, g_out, total = to_weights(0, place, mine, w)
    g_qkv, g_out, g_gain = to_weights(1, place, sibling, w, vm(total), vm(gain), g_qkv, g_out)

    grid = (LEV, ROWS, COLS, D)
    return out.reshape(grid), grad.reshape(grid), g_qkv, g_out, g_gain.reshape(D)


def solution(mesh):
    return jax.shard_map(
        on_device,
        mesh=mesh,
        in_specs=(P(None, "lat", "lon", None), P(None, "lat", "lon", None), P(), P(), P()),
        out_specs=(P(None, "lat", "lon", None), P(None, "lat", "lon", None), P(), P(), P()),
        check_vma=False,
    )
```

```python
import functools
import math

import jax
import jax.numpy as jnp
import numpy as np
from jax import lax
from jax.experimental import pallas as pl
from jax.experimental.pallas import tpu as pltpu
from jax.sharding import PartitionSpec as P

HEADS = 8
LEV, ROWS, COLS = 4, 6, 24
WL, WR, WC = 2, 6, 12
D = 512
SPAN = WL * WR * WC
TOK = LEV * ROWS * COLS
BOTH = ("lat", "lon")
f32 = jnp.float32
bf16 = jnp.bfloat16
VMEM = 24 * 1024 * 1024


def index_of(y, x, z, c):
    return (y * 2 + x // 2) * 32 + (x % 2) * 16 + z * 2 + c


def place_of(i):
    return i // 64, ((i // 32) % 2) * 2 + (i // 16) % 2, (i // 2) % 8, i % 2


def route(step):
    return [(i, index_of(*step(*place_of(i)))) for i in range(256)]


def to_sibling(y, x, z, c):
    return y, x, z, 1 - c


def first_axis(k):
    return lambda y, x, z, c: ((y + k) % 4, x, z, c) if c == 0 else (y, (x + k) % 4, z, c)


def second_axis(k):
    return lambda y, x, z, c: (y, (x + k) % 4, z, c) if c == 0 else ((y + k) % 4, x, z, c)


def flip_z(k):
    return lambda y, x, z, c: (y, x, z ^ k, c)


def send(x, step):
    return lax.ppermute(x, BOTH, route(step))


def shifted(dlat, dlon):
    def pairs():
        out = []
        for i in range(256):
            a, b = i // 32, i % 32
            out.append((i, ((a + dlat) % 8) * 32 + (b + dlon) % 32))
        return out

    return pairs()


LAT, LON, HALO = 224, 80, 384


def gather_tables():
    local = np.zeros((TOK, TOK), np.float32)
    halo = np.zeros((TOK, HALO), np.float32)
    for lr in range(LEV):
        for rr in range(ROWS):
            for cr in range(COLS):
                w = (lr // WL) * (COLS // WC) + cr // WC
                t = w * SPAN + (lr % WL) * WR * WC + rr * WC + cr % WC
                lo, r, c = (lr + 1) % LEV, rr + 3, cr + 6
                if r < ROWS and c < COLS:
                    local[t, lo * ROWS * COLS + r * COLS + c] = 1
                elif c < COLS:
                    halo[t, lo * 54 + (r - ROWS) * 18 + c - 6] = 1
                elif r < ROWS:
                    halo[t, LAT + lo * 18 + (r - 3) * 6 + c - COLS] = 1
                else:
                    halo[t, LAT + LON + lo * 18 + (r - ROWS) * 6 + c - COLS] = 1
    return local, halo


def select_table():
    select = np.zeros((HALO, TOK), np.float32)
    for lv in range(LEV):
        for r in range(ROWS):
            for c in range(COLS):
                t = lv * ROWS * COLS + r * COLS + c
                if r < 3 and c >= 6:
                    select[lv * 54 + r * 18 + c - 6, t] = 1
                elif r >= 3 and c < 6:
                    select[LAT + lv * 18 + (r - 3) * 6 + c, t] = 1
                elif r < 3:
                    select[LAT + LON + lv * 18 + r * 6 + c, t] = 1
    return select


def dot(a, b, dims=((1,), (0,))):
    return lax.dot_general(a, b, (dims, ((), ())), preferred_element_type=f32)


NT = ((1,), (1,))
TN = ((0,), (0,))


def normalise(x):
    centred = x - jnp.mean(x, axis=-1, keepdims=True)
    rstd = lax.rsqrt(jnp.mean(centred * centred, axis=-1, keepdims=True) + 1e-5)
    return centred * rstd, rstd


def split(rows, lat, lon, diag):
    lat[...] = rows[:LAT].astype(bf16)
    lon[...] = rows[LAT : LAT + LON].astype(bf16)
    diag[...] = rows[LAT + LON :].astype(bf16)


def pack_kernel(f_hbm, c_hbm, s_hbm, f_vm, c_vm, s_vm, *refs):
    f_parts, c_parts, sem = refs[:3], refs[3:6], refs[6]
    pairs = ((s_hbm, s_vm), (f_hbm, f_vm), (c_hbm, c_vm))
    copies = [pltpu.make_async_copy(a, b, sem.at[i]) for i, (a, b) in enumerate(pairs)]
    for copy in copies:
        copy.start()
    copies[0].wait()
    copies[1].wait()
    split(dot(s_vm[...], f_vm[...]), *f_parts)
    copies[2].wait()
    split(dot(s_vm[...], c_vm[...]), *c_parts)


def load_kernel(f_vm, c_vm, *refs):
    sources, targets, (fw, cw, sem) = refs[:5], refs[5:10], refs[10:]
    copies = [
        pltpu.make_async_copy(a, b, sem.at[i]) for i, (a, b) in enumerate(zip(sources, targets))
    ]
    for copy in copies:
        copy.start()
    copies[0].wait()
    local = targets[0]
    fw[...] = dot(local[...], f_vm[...]).astype(bf16)
    cw[...] = dot(local[...], c_vm[...]).astype(bf16)
    for copy in copies[1:]:
        copy.wait()


GROUP = 4
WIDE = GROUP * (D // HEADS)


def group_mask(value=1.0):
    row = lax.broadcasted_iota(jnp.int32, (GROUP * SPAN, WIDE), 0)
    lane = lax.broadcasted_iota(jnp.int32, (GROUP * SPAN, WIDE), 1)
    first = lane // (D // HEADS) * SPAN
    return jnp.where((row >= first) & (row < first + SPAN), value, 0.0).astype(bf16)


def joined(r, factor=1.0):
    lane = lax.broadcasted_iota(jnp.int32, (SPAN, WIDE), 1)
    out = r[:SPAN]
    for h in range(1, GROUP):
        out = jnp.where(lane >= h * (D // HEADS), r[h * SPAN : (h + 1) * SPAN], out)
    return (out * factor).astype(bf16)


def repeated(x, pick):
    return jnp.concatenate([x] * GROUP, axis=0) * pick


def windows(part, table, lat, lon, diag):
    rows = jnp.concatenate([lat[...], lon[...], diag[...]], axis=0)
    return part[...].astype(f32) + dot(table[...], rows)


def forward_kernel(place, *refs):
    gain, w_ref, normed, qkv, probs, mixed = refs[5:]
    xhat, _ = normalise(windows(*refs[:5]))
    normed[...] = (xhat * gain[...]).astype(bf16)
    qkv[...] = dot(normed[...], w_ref[...]).astype(bf16)

    last_lat = place[0]
    long = 2 * SPAN
    low = lax.broadcasted_iota(jnp.int32, (SPAN, 128), 1) < 64
    row = lax.broadcasted_iota(jnp.int32, (long, 128), 0)
    lane = lax.broadcasted_iota(jnp.int32, (long, 128), 1)
    pick = jnp.where((row < SPAN) == (lane < 64), 1.0 / math.sqrt(D // HEADS), 0.0).astype(bf16)

    def lev_of(t):
        return (t >= SPAN // 2).astype(jnp.int32)

    def half_of(t):
        return (t - SPAN // 2 * lev_of(t) >= SPAN // 4).astype(jnp.int32)

    tq = lax.rem(lax.broadcasted_iota(jnp.int32, (SPAN, long), 1), SPAN)
    tk = lax.broadcasted_iota(jnp.int32, (SPAN, long), 0)
    lev_diff = jnp.abs(lev_of(tq) - lev_of(tk))
    half_diff = jnp.abs(half_of(tq) - half_of(tk)) * last_lat

    kinds = (half_diff == 0, (lev_diff + half_diff) == 0)
    for w in range(4):
        at = pl.ds(w * SPAN, SPAN)
        same = kinds[w // 2]
        for p in range(HEADS // 2):
            q_all = jnp.concatenate([qkv[at, pl.ds(128 * p, 128)]] * 2, axis=0) * pick
            k = qkv[at, pl.ds(D + 128 * p, 128)]
            v = qkv[at, pl.ds(2 * D + 128 * p, 128)]
            s = jnp.where(same, dot(k, q_all, NT), -1000000000.0)
            e = jnp.exp(s - jnp.max(s, axis=0, keepdims=True))
            rounded = (e * (1.0 / jnp.sum(e, axis=0, keepdims=True))).astype(bf16)
            probs[pl.ds((w * 2 + p // 2) * SPAN, SPAN), pl.ds(p % 2 * 2 * SPAN, 2 * SPAN)] = rounded
            r = dot(rounded, v, TN)
            mixed[at, pl.ds(128 * p, 128)] = jnp.where(low, r[:SPAN], r[SPAN:]).astype(bf16)


def backward_kernel(place, *refs):
    o_ref, normed, qkv, probs, mixed, gact, own, other, ctw, gm, acc = refs[5:]
    ctw[...] = windows(*refs[:5]).astype(bf16)
    gm[...] = dot(ctw[...], o_ref[...], NT).astype(bf16)
    long = GROUP * SPAN
    pick = group_mask()
    factor = 1.0 / math.sqrt(D // HEADS)
    scaled = group_mask(factor)

    def window(w, carry):
        at = pl.ds(pl.multiple_of(w * SPAN, SPAN), SPAN)
        for p in range(HEADS // GROUP):
            cols = pl.ds(WIDE * p, WIDE)
            q_all = repeated(qkv[at, cols], scaled)
            g_all = repeated(gm[at, cols], pick)
            k = qkv[at, pl.ds(D + WIDE * p, WIDE)]
            v = qkv[at, pl.ds(2 * D + WIDE * p, WIDE)]
            rounded = probs[pl.ds(pl.multiple_of((w * 2 + p) * SPAN, SPAN), SPAN), :]
            gact[at, pl.ds(2 * D + WIDE * p, WIDE)] = dot(rounded, g_all).astype(bf16)
            dp = dot(v, g_all, NT)
            pr = rounded.astype(f32)
            inner = jnp.sum(dp * pr, axis=0, keepdims=True)
            ds = (pr * (dp - inner)).astype(bf16)
            gact[at, cols] = joined(dot(ds, k, TN), factor)
            gact[at, pl.ds(D + WIDE * p, WIDE)] = dot(ds, q_all).astype(bf16)
        return carry

    lax.fori_loop(0, 4, window, 0, unroll=True)

    acc[:, : 3 * D] = dot(normed[...], gact[...], TN)
    acc[:, 3 * D :] = dot(mixed[...], ctw[...], TN)
    y, x, c = place[1], place[2], place[3]

    def fill(out, core):
        d1 = jnp.where(core == 0, y, x)
        d2 = jnp.where(core == 0, x, y)
        for s1 in range(4):
            for s2 in range(4):
                r = core * 256 + lax.rem(d1 + s1, 4) * 64 + lax.rem(d2 + s2, 4) * 16
                rows = acc[pl.ds(pl.multiple_of(r, 16), 16), :]
                out[pl.ds((s1 * 4 + s2) * 16, 16), :] = rows.astype(bf16)

    fill(own, c)
    fill(other, 1 - c)


def back_kernel(mixed, gact, w_ref, o_ref, p_halo, both, to_lat, to_lon, to_diag):
    both[:, :D] = dot(mixed[...], o_ref[...]).astype(bf16)
    both[:, D:] = dot(gact[...], w_ref[...], NT).astype(bf16)
    split(dot(p_halo[...], both[...], TN), to_lat, to_lon, to_diag)


def finish_kernel(f_loc, c_loc, both, r_lat, r_lon, r_diag, p_loc, select, gain, out, grad):
    rows = jnp.concatenate([r_lat[...], r_lon[...], r_diag[...]], axis=0)
    grid = dot(p_loc[...], both[...], TN) + dot(select[...], rows, TN)
    x = f_loc[...].astype(f32)
    out[...] = (x + grid[:, :D]).astype(bf16)
    xhat, rstd = normalise(x)
    g = grid[:, D:] * gain[...]
    first = jnp.mean(g, axis=-1, keepdims=True)
    second = jnp.mean(g * xhat, axis=-1, keepdims=True)
    grad[...] = (c_loc[...].astype(f32) + rstd * (g - first - xhat * second)).astype(bf16)


def weights_kernel(side, place, *refs):
    pieces, refs = refs[:4], refs[4:]
    if side == 0:
        w_ref, g_qkv, g_out, g_total, buf_q, buf_o, sem = refs
    else:
        w_ref, before, gain, _, _, g_qkv, g_out, g_gain, buf_q, buf_o, sem, g_total = refs
    y, x, c = place[1], place[2], place[3]
    core = c if side == 0 else 1 - c
    d1 = jnp.where(core == 0, y, x)
    d2 = jnp.where(core == 0, x, y)
    bands = [pl.multiple_of(core * 256 + lax.rem(d1 + i, 4) * 64, 64) for i in range(4)]
    copies = []
    for i in range(4):
        for s2 in range(4):
            at = pl.ds(pl.multiple_of(lax.rem(d2 + s2, 4) * 16, 16), 16)
            block = pieces[i][pl.ds(s2 * 16, 16), :].astype(f32)
            buf_q[i, at, :] = block[:, : 3 * D]
            buf_o[i, at, :] = block[:, 3 * D :]
        for k, (src, dst) in enumerate(((buf_q, g_qkv), (buf_o, g_out))):
            copy = pltpu.make_async_copy(src.at[i], dst.at[pl.ds(bands[i], 64)], sem.at[i, k])
            copy.start()
            copies.append(copy)
    total = jnp.zeros((1, D), f32) if side == 0 else before[...]
    lane = lax.broadcasted_iota(jnp.int32, (64, D), 1)
    local = lax.broadcasted_iota(jnp.int32, (64, D), 0)
    for i in range(4):
        w = w_ref[pl.ds(bands[i], 64), :].astype(f32)
        sums = jnp.sum(buf_q[i] * w, axis=1, keepdims=True)
        spread = jnp.where(lane == local + bands[i], sums, 0.0)
        total = total + jnp.sum(spread, axis=0, keepdims=True)
    g_total[...] = total if side == 0 else total / gain[...]
    if side == 1:
        copies.append(pltpu.make_async_copy(g_total, g_gain, sem.at[4, 0]))
        copies[-1].start()
    for copy in copies:
        copy.wait()


def to_weights(side, place, pieces, qkv_weight, *more):
    inside = pl.BlockSpec(memory_space=pltpu.VMEM)
    anywhere = pl.BlockSpec(memory_space=pl.ANY)
    extra = [] if side == 0 else [inside, inside, anywhere, anywhere]
    return pl.pallas_call(
        functools.partial(weights_kernel, side),
        out_shape=[
            shape(D, 3 * D, dtype=f32),
            shape(D, D, dtype=f32),
            (vshape if side == 0 else shape)(1, D, dtype=f32),
        ],
        in_specs=spec(5, True) + extra,
        out_specs=[anywhere, anywhere, inside if side == 0 else anywhere],
        scratch_shapes=[
            pltpu.VMEM((4, 64, 3 * D), f32),
            pltpu.VMEM((4, 64, D), f32),
            pltpu.SemaphoreType.DMA((5, 2)),
        ]
        + ([] if side == 0 else [pltpu.VMEM((1, D), f32)]),
        input_output_aliases={} if side == 0 else {8: 0, 9: 1},
        compiler_params=params(),
        cost_estimate=cost(10**7, 4 * 10**6),
        name="weights" + str(side),
    )(place, *vms(*pieces), vm(qkv_weight), *more)


def params():
    return pltpu.CompilerParams(vmem_limit_bytes=VMEM)


def vm(x):
    return pltpu.with_memory_space_constraint(x, pltpu.VMEM)


def vms(*xs):
    return [vm(x) for x in xs]


def vshape(*dims, dtype=bf16):
    return pltpu.VMEM(dims, dtype)


def spec(count, scalar=False):
    whole = [pl.BlockSpec(memory_space=pltpu.VMEM)] * count
    return ([pl.BlockSpec(memory_space=pltpu.SMEM)] if scalar else []) + whole


def shape(*dims, dtype=bf16):
    return jax.ShapeDtypeStruct(dims, dtype)


def cost(flops, moved):
    return pl.CostEstimate(flops=flops, bytes_accessed=moved, transcendentals=0)


def halo_shapes(width):
    return [vshape(LAT, width), vshape(LON, width), vshape(HALO - LAT - LON, width)]


def to_pack(fields, cotangent, select):
    return pl.pallas_call(
        pack_kernel,
        out_shape=[vshape(TOK, D), vshape(TOK, D), vshape(HALO, TOK)] + halo_shapes(D) * 2,
        in_specs=[pl.BlockSpec(memory_space=pltpu.HBM)] * 3,
        out_specs=spec(9),
        scratch_shapes=[pltpu.SemaphoreType.DMA((3,))],
        compiler_params=params(),
        cost_estimate=cost(4 * 10**8, 2 * 10**6),
        name="pack",
    )(*[pltpu.with_memory_space_constraint(x, pltpu.HBM) for x in (fields, cotangent, select)])


def to_load(f_vm, c_vm, *sources):
    return pl.pallas_call(
        load_kernel,
        out_shape=[vshape(*x.shape, dtype=x.dtype) for x in sources]
        + [vshape(TOK, D), vshape(TOK, D)],
        in_specs=spec(2) + [pl.BlockSpec(memory_space=pltpu.HBM)] * 5,
        out_specs=spec(7),
        scratch_shapes=[pltpu.SemaphoreType.DMA((5,))],
        compiler_params=params(),
        cost_estimate=cost(10**6, 10**4),
        name="load",
    )(*vms(f_vm, c_vm), *[pltpu.with_memory_space_constraint(x, pltpu.HBM) for x in sources])


def to_forward(place, *args):
    return pl.pallas_call(
        forward_kernel,
        out_shape=[
            vshape(TOK, D), vshape(TOK, 3 * D), vshape(32 // GROUP * SPAN, GROUP * SPAN), vshape(TOK, D),
        ],
        in_specs=spec(7, True),
        out_specs=spec(4),
        compiler_params=params(),
        cost_estimate=cost(10**6, 10**4),
        name="forward",
    )(place, *vms(*args))


def to_backward(place, *args):
    return pl.pallas_call(
        backward_kernel,
        out_shape=[vshape(TOK, 3 * D), vshape(256, 4 * D), vshape(256, 4 * D)],
        in_specs=spec(10, True),
        out_specs=spec(3),
        scratch_shapes=[
            pltpu.VMEM((TOK, D), bf16),
            pltpu.VMEM((TOK, D), bf16),
            pltpu.VMEM((D, 4 * D), f32),
        ],
        compiler_params=params(),
        cost_estimate=cost(5 * 10**9, 10**7),
        name="backward",
    )(place, *vms(*args))


def to_back(*args):
    return pl.pallas_call(
        back_kernel,
        out_shape=[vshape(TOK, 2 * D)] + halo_shapes(2 * D),
        in_specs=spec(5),
        out_specs=spec(4),
        compiler_params=params(),
        cost_estimate=cost(2 * 10**9, 5 * 10**6),
        name="back",
    )(*vms(*args))


def to_finish(*args):
    return pl.pallas_call(
        finish_kernel,
        out_shape=[shape(TOK, D), shape(TOK, D)],
        in_specs=spec(9),
        out_specs=spec(2),
        compiler_params=params(),
        cost_estimate=cost(2 * 10**9, 8 * 10**6),
        name="finish",
    )(*vms(*args))


def add(*xs):
    total = xs[0].astype(f32)
    for x in xs[1:]:
        total = total + x.astype(f32)
    return total.astype(bf16)


def tied(x):
    return lax.optimization_barrier(x)


def halo_in(lat, lon, diag):
    return (
        lax.ppermute(lat, BOTH, shifted(-1, 0)),
        lax.ppermute(lon, BOTH, shifted(0, -1)),
        lax.ppermute(diag, BOTH, shifted(-1, -1)),
    )


def on_device(fields, cotangent, layer_norm_gain, qkv_weight, out_weight):
    a, b = lax.axis_index("lat"), lax.axis_index("lon")
    place = jnp.stack(
        [
            (a == 7).astype(jnp.int32),
            (a // 2).astype(jnp.int32),
            ((a % 2) * 2 + b // 16).astype(jnp.int32),
            (b % 2).astype(jnp.int32),
        ]
    )
    tables = [jnp.asarray(t, bf16) for t in gather_tables()]
    select = jnp.asarray(select_table(), bf16)
    f_vm, c_vm, select, *parts = to_pack(
        fields.reshape(TOK, D), cotangent.reshape(TOK, D), select
    )
    f_halo = halo_in(*parts[:3])
    c_halo = halo_in(*parts[3:])
    p_loc, p_halo, w, o, gain, fw, cw = to_load(
        f_vm, c_vm, *tables, qkv_weight, out_weight, layer_norm_gain.reshape(1, D)
    )
    normed, qkv, probs, mixed = to_forward(place, fw, p_halo, *f_halo, gain, w)
    gact, own, other = to_backward(
        place, cw, p_halo, *c_halo, o, normed, qkv, probs, mixed
    )

    there = send(other, to_sibling)
    part = [add(own[64 * k : 64 * k + 64], there[64 * k : 64 * k + 64]) for k in range(4)]
    mixed, gact, part = tied((mixed, gact, part))
    both, to_lat, to_lon, to_diag = to_back(mixed, gact, w, o, p_halo)
    recv = [send(part[k], first_axis(k)) for k in (1, 2, 3)]
    recv, to_lat = tied((recv, to_lat))
    part = add(part[0], *recv)
    part, to_lat, to_lon, to_diag = tied((part, to_lat, to_lon, to_diag))
    part = add(part[:16], *[send(part[16 * k : 16 * k + 16], second_axis(k)) for k in (1, 2, 3)])
    r_lat = lax.ppermute(to_lat, BOTH, shifted(1, 0))
    r_lon = lax.ppermute(to_lon, BOTH, shifted(0, 1))
    r_diag = lax.ppermute(to_diag, BOTH, shifted(1, 1))
    recv = send(part, flip_z(1))
    recv, r_lon = tied((recv, r_lon))
    part = add(part, recv)
    recv = send(part, flip_z(2))
    part = add(part, recv)
    recv = send(part, flip_z(6))
    recv, r_lat, r_diag = tied((recv, r_lat, r_diag))
    part = add(part, recv)

    block = jnp.concatenate([part] + [send(part, second_axis(4 - s)) for s in (1, 2, 3)], axis=0)
    mine = [send(block, first_axis(4 - s)) for s in (1, 2, 3)]
    out, grad = to_finish(f_vm, c_vm, both, r_lat, r_lon, r_diag, p_loc, select, gain)
    mine, out = tied((mine, out))
    mine = [block] + mine
    sibling = [send(m, to_sibling) for m in mine]
    g_qkv, g_out, total = to_weights(0, place, mine, w)
    g_qkv, g_out, g_gain = to_weights(1, place, sibling, w, vm(total), vm(gain), g_qkv, g_out)

    grid = (LEV, ROWS, COLS, D)
    return out.reshape(grid), grad.reshape(grid), g_qkv, g_out, g_gain.reshape(D)


def solution(mesh):
    return jax.shard_map(
        on_device,
        mesh=mesh,
        in_specs=(P(None, "lat", "lon", None), P(None, "lat", "lon", None), P(), P(), P()),
        out_specs=(P(None, "lat", "lon", None), P(None, "lat", "lon", None), P(), P(), P()),
        check_vma=False,
    )
```
